256 devices in a mesh: bucket: 64 (over x, z, core), row: 4 (over y).
Axes of the slice: x: 4, y: 4, z: 8, core: 2. Of those that a mesh axis runs over, the one named last changes fastest.
Arguments:
- entities: float32 [131072, 400], P(('bucket', 'row')), may hold values from -21.6 to 21.6
- relations: float32 [1300, 400], replicated, may hold values from -1.35 to 1.35
- touch_owner: int32 [256, 64], P(('bucket', 'row')), may hold values from 0 to 63, as said below
- touch_block: int32 [256, 64], P(('bucket', 'row')), may hold values from 0 to 3
- head_ids: int32 [262144], P(('bucket', 'row')), may hold values from 0 to 8191
- rel_ids: int32 [262144], P(('bucket', 'row')), may hold values from 0 to 1299
- tail_ids: int32 [262144], P(('bucket', 'row')), may hold values from 0 to 8191
- neg_tail: int32 [256, 100], P(('bucket', 'row')), may hold values from 0 to 8191
- neg_head: int32 [256, 100], P(('bucket', 'row')), may hold values from 0 to 8191
Outputs:
- entity_grad: float32 [131072, 400], P(('bucket', 'row'))
- relation_grad: float32 [1300, 400], replicated
The draws below stay inside these ranges and needn't reach their ends.
Inputs may be any that keep to these rules, and one draw needn't show every extreme that they name: `touch_owner`: each row names every bucket index once.
All inputs are finite; a program needn't handle non-finite values.
Results may differ from the reference program's by a relative error of at most 0.0073.
Values may be sent and summed in bfloat16 or wider, within the bound.
A program may use at most 192 MiB of HBM per device.

```python
import math
import jax
import jax.numpy as jnp
import numpy as np
from jax import lax

D = 400
REL = 1300
NEG = 100
BLOCK = 128
OWN = 4
TB = 64
EDGE_BLOCKS = 1
GROUPS = 256
EDGES = 262144
ENT_ROWS = 131072
N_BUCKET = 64
N_ROW = 4


def draw_entities(key, part):
    key = jax.random.fold_in(key, 5)
    first = jax.random.fold_in(key, 0)
    base = jnp.clip(jax.random.normal(first, (ENT_ROWS, D), jnp.float32), -4.5, 4.5)
    return 0.3 * base


def draw_touch_owner(key, part):
    key = jax.random.fold_in(key, 11)
    keys = jax.random.split(key, N_BUCKET * N_ROW)
    orders = jax.vmap(lambda single: jax.random.permutation(single, N_BUCKET))(keys)
    return orders[:, :TB].astype(jnp.int32)


def with_ends(array, stream_key, least, top_value):
    longest = array.shape.index(max(array.shape))
    spots = []
    for shift in (0, 1):
        where = [jax.random.randint(jax.random.fold_in(stream_key, axis), (), 0, length) for axis, length in enumerate(array.shape)]
        where[longest] = (where[longest] + shift) % array.shape[longest]
        spots.append(tuple(where))
    return array.at[spots[0]].set(least).at[spots[1]].set(top_value)


def rank_bounds(count, skew):
    portions = [(1 << 20) // math.isqrt(grade ** skew) + 1 for grade in range(1, count + 1)]
    deviation = 1 + sum(portions) // (1 << 30)
    return np.cumsum(np.array([max(1, weight // deviation) for weight in portions]))


def ranked_ids(rng, dims, number_of, slope):
    table = rank_bounds(number_of, slope)
    ticket = jax.random.randint(jax.random.fold_in(rng, 1), dims, 0, int(table[number_of - 1]))
    standing = jnp.searchsorted(jnp.asarray(table, jnp.int32), ticket, side="right")
    return jax.random.permutation(jax.random.fold_in(rng, 2), number_of)[standing].astype(jnp.int32)


def scatter_about(own_key, extent, deviation, reach, kind=jnp.bfloat16):
    values = jax.random.normal(own_key, extent, jnp.float32) * deviation
    return jnp.minimum(jnp.maximum(values, -reach), reach).astype(kind)


def setup_inputs(seed: int = 0) -> dict:
    seeds = jax.random.split(jax.random.key(seed), 10)
    entities = draw_entities(jax.random.fold_in(seeds[9], 71), 0)
    relations = scatter_about(seeds[1], (REL, D), 0.3, 1.35, jnp.float32)
    touch_owner = draw_touch_owner(jax.random.fold_in(seeds[9], 71), 0)
    touch_block = with_ends(jax.random.randint(seeds[3], (GROUPS, TB), 0, OWN), jax.random.fold_in(seeds[3], 1), 0, OWN - 1).astype(jnp.int32)
    head_ids = with_ends(jax.random.randint(seeds[4], (EDGES,), 0, TB * BLOCK), jax.random.fold_in(seeds[4], 1), 0, (TB * BLOCK) - 1).astype(jnp.int32)
    rel_ids = with_ends(ranked_ids(seeds[5], (EDGES,), REL, 2), jax.random.fold_in(seeds[5], 3), 0, REL - 1).astype(jnp.int32)
    tail_ids = with_ends(jax.random.randint(seeds[6], (EDGES,), 0, TB * BLOCK), jax.random.fold_in(seeds[6], 1), 0, (TB * BLOCK) - 1).astype(jnp.int32)
    neg_tail = with_ends(jax.random.randint(seeds[7], (GROUPS * EDGE_BLOCKS, NEG), 0, TB * BLOCK), jax.random.fold_in(seeds[7], 1), 0, (TB * BLOCK) - 1).astype(jnp.int32)
    neg_head = with_ends(jax.random.randint(seeds[8], (GROUPS * EDGE_BLOCKS, NEG), 0, TB * BLOCK), jax.random.fold_in(seeds[8], 1), 0, (TB * BLOCK) - 1).astype(jnp.int32)
    return {"entities": entities, "relations": relations, "touch_owner": touch_owner, "touch_block": touch_block, "head_ids": head_ids, "rel_ids": rel_ids, "tail_ids": tail_ids, "neg_tail": neg_tail, "neg_head": neg_head}


def side_weights(positive, scores):
    largest = jnp.maximum(positive, jnp.max(scores, axis=1))
    own_term = jnp.exp(positive - largest)
    others = jnp.exp(scores - largest[:, None])
    total = own_term + jnp.sum(others, axis=1)
    return own_term / total - 1.0, others / total[:, None]


def edge_block_grads(buffer, relations, head_ids, rel_ids, tail_ids, neg_tail, neg_head):
    middle = relations.shape[1] // 2
    head_rows = jnp.take(buffer, head_ids, axis=0).astype(jnp.float32)
    tail_rows = jnp.take(buffer, tail_ids, axis=0).astype(jnp.float32)
    rel_rows = jnp.take(relations, rel_ids, axis=0)
    rel_real, rel_imag = rel_rows[:, :middle], rel_rows[:, middle:]
    head_real, head_imag = head_rows[:, :middle], head_rows[:, middle:]
    tail_real, tail_imag = tail_rows[:, :middle], tail_rows[:, middle:]
    query = jnp.concatenate([head_real * rel_real - head_imag * rel_imag, head_real * rel_imag + head_imag * rel_real], axis=1)
    probe = jnp.concatenate([rel_real * tail_real + rel_imag * tail_imag, rel_real * tail_imag - rel_imag * tail_real], axis=1)
    positive = jnp.sum(query * tail_rows, axis=1)
    tail_negs = jnp.take(buffer, neg_tail, axis=0)
    head_negs = jnp.take(buffer, neg_head, axis=0)
    query_low = query.astype(jnp.bfloat16)
    probe_low = probe.astype(jnp.bfloat16)
    contract_last = (((1,), (1,)), ((), ()))
    contract_first = (((0,), (0,)), ((), ()))
    tail_scores = lax.dot_general(query_low, tail_negs, contract_last, preferred_element_type=jnp.float32)
    head_scores = lax.dot_general(probe_low, head_negs, contract_last, preferred_element_type=jnp.float32)
    tail_coef, tail_weights = side_weights(positive, tail_scores)
    head_coef, head_weights = side_weights(positive, head_scores)
    tail_low = tail_weights.astype(jnp.bfloat16)
    head_low = head_weights.astype(jnp.bfloat16)
    both_coef = (tail_coef + head_coef)[:, None]
    query_grad = both_coef * tail_rows + jnp.dot(tail_low, tail_negs, preferred_element_type=jnp.float32)
    probe_grad = jnp.dot(head_low, head_negs, preferred_element_type=jnp.float32)
    tail_neg_grad = lax.dot_general(tail_low, query_low, contract_first, preferred_element_type=jnp.float32)
    head_neg_grad = lax.dot_general(head_low, probe_low, contract_first, preferred_element_type=jnp.float32)
    qgrad_real, qgrad_imag = query_grad[:, :middle], query_grad[:, middle:]
    pgrad_real, pgrad_imag = probe_grad[:, :middle], probe_grad[:, middle:]
    head_grad = jnp.concatenate([qgrad_real * rel_real + qgrad_imag * rel_imag, qgrad_imag * rel_real - qgrad_real * rel_imag], axis=1)
    tail_grad = both_coef * query + jnp.concatenate([pgrad_real * rel_real - pgrad_imag * rel_imag, pgrad_real * rel_imag + pgrad_imag * rel_real], axis=1)
    rel_edge_grad = jnp.concatenate([
        qgrad_real * head_real + qgrad_imag * head_imag + pgrad_real * tail_real + pgrad_imag * tail_imag,
        qgrad_imag * head_real - qgrad_real * head_imag + pgrad_real * tail_imag - pgrad_imag * tail_real], axis=1)
    row_ids = jnp.concatenate([head_ids, tail_ids, neg_tail, neg_head])
    row_vals = jnp.concatenate([head_grad, tail_grad, tail_neg_grad, head_neg_grad], axis=0)
    return row_ids, row_vals, rel_edge_grad


def device_grads(buffer, relations, head_ids, rel_ids, tail_ids, neg_tail, neg_head):
    blocks_count = neg_tail.shape[0]
    block_edges = head_ids.shape[0] // blocks_count
    start_zero = (jnp.zeros(buffer.shape, jnp.float32), jnp.zeros(relations.shape, jnp.float32))

    def advance(totals, position):
        offset = position * block_edges
        heads_now = lax.dynamic_slice_in_dim(head_ids, offset, block_edges)
        rels_now = lax.dynamic_slice_in_dim(rel_ids, offset, block_edges)
        tails_now = lax.dynamic_slice_in_dim(tail_ids, offset, block_edges)
        row_ids, row_vals, rel_edge_grad = edge_block_grads(buffer, relations, heads_now, rels_now, tails_now, neg_tail[position], neg_head[position])
        return (totals[0].at[row_ids].add(row_vals), totals[1].at[rels_now].add(rel_edge_grad)), None

    totals, unused = lax.scan(advance, start_zero, jnp.arange(blocks_count, dtype=jnp.int32))
    return totals


def reference(entities, relations, touch_owner, touch_block, head_ids, rel_ids, tail_ids, neg_tail, neg_head):
    groups = touch_owner.shape[0]
    touched = touch_owner.shape[1]
    table = entities.reshape(-1, BLOCK, D)
    group_heads = head_ids.reshape(groups, -1)
    group_rels = rel_ids.reshape(groups, -1)
    group_tails = tail_ids.reshape(groups, -1)
    group_ntail = neg_tail.reshape(groups, -1, NEG)
    group_nhead = neg_head.reshape(groups, -1, NEG)

    def visit(totals, inputs):
        group, owners, wanted, heads_now, rels_now, tails_now, ntail_now, nhead_now = inputs
        row_index = group % N_ROW
        block_ids = ((owners * N_ROW + row_index) * OWN + wanted).astype(jnp.int32)
        buffer = jnp.take(table, block_ids, axis=0).astype(jnp.bfloat16).reshape(touched * BLOCK, D)
        buffer_grad, rel_part = device_grads(buffer, relations, heads_now, rels_now, tails_now, ntail_now, nhead_now)
        entity_total = totals[0].at[block_ids].add(buffer_grad.reshape(touched, BLOCK, D))
        return (entity_total, totals[1] + rel_part), None

    start_zero = (jnp.zeros(table.shape, jnp.float32), jnp.zeros(relations.shape, jnp.float32))
    totals, unused = lax.scan(visit, start_zero, (jnp.arange(groups, dtype=jnp.int32), touch_owner, touch_block,
                                                   group_heads, group_rels, group_tails, group_ntail, group_nhead))
    return totals[0].reshape(entities.shape), totals[1]
```

```python
import functools

import jax
import jax.numpy as jnp
from jax import lax
from jax.experimental import pallas as pl
from jax.experimental.pallas import tpu as pltpu
from jax.sharding import PartitionSpec as P

BLOCK = 128
WIDTH = 400
EDGES = 1024
NEG = 100
REL = 1300
REL_PAD = 1536
ALL = 2 * EDGES + 2 * BLOCK
XS, ZS, CS, YS = 4, 8, 2, 4
XG = XS * CS
TILES = 3
CAP = TILES * BLOCK
DIST = (0, 1, 7, 2, 6, 3, 5, 4)
FIRST_OF_TILE = (3, 6, 8)
TILES_OF = (0, 0, 0, 1, 1, 1, 2, 2)
HALF = 208
HALF_START = 192
BF = jnp.bfloat16
F32 = jnp.float32
I32 = jnp.int32
NT = (((1,), (1,)), ((), ()))
TN = (((0,), (0,)), ((), ()))
MIB = 1024 * 1024


def mm(a, b, dims=(((1,), (0,)), ((), ()))):
    return lax.dot_general(a, b, dims, preferred_element_type=F32)


def iota(shape, dim):
    return lax.broadcasted_iota(I32, shape, dim)


def hot(mask):
    return jnp.where(mask, 1.0, 0.0).astype(BF)


def place():
    b = lax.axis_index("bucket")
    return b // (ZS * CS), (b // CS) % ZS, b % CS, lax.axis_index("row")


def bucket_of(x, z, c):
    return (x * ZS + z) * CS + c


def x_peer(x, z, c, k):
    s = lax.rem(x * CS + c + k, XG)
    return s, {"bucket": bucket_of(s // CS, z, s % CS)}


def z_peer(x, z, c, k):
    other = lax.rem(z + k, ZS)
    return other, {"bucket": bucket_of(x, other, c)}


def greet(peers):
    barrier = pltpu.get_barrier_semaphore()
    for peer in peers:
        pl.semaphore_signal(barrier, inc=1, device_id=peer, device_id_type=pl.DeviceIdType.MESH)
    pl.semaphore_wait(barrier, len(peers))


def remote(src, dst, send, recv, peer):
    return pltpu.make_async_remote_copy(
        src_ref=src, dst_ref=dst, send_sem=send, recv_sem=recv,
        device_id=peer, device_id_type=pl.DeviceIdType.MESH,
    )


def plan_rows(ids, owners, blocks, z):
    slot = lax.shift_right_arithmetic(ids, 7)
    row = jnp.bitwise_and(ids, 127)
    slot_hot = hot(iota((64, ALL), 0) == slot)
    row_is = iota((BLOCK, ALL), 0) == row
    row_hot = hot(row_is)
    count = mm(slot_hot, row_hot, NT)
    wanted_slot = hot(count > 0.5)
    j = iota((64, 64), 0)
    s, q = j // 8, j % 8
    dist = jnp.where(q % 2 == 1, (q + 1) // 2, (8 - q // 2) % 8)
    target = bucket_of(s // CS, (z + dist) % ZS, s % CS)
    perm_is = owners == target
    perm = hot(perm_is)
    wanted = mm(perm, wanted_slot)
    block = jnp.sum(jnp.where(perm_is, blocks, 0), axis=1, keepdims=True)
    wanted_low = wanted.astype(BF)
    before = mm(wanted_low, hot(iota((BLOCK, BLOCK), 0) < iota((BLOCK, BLOCK), 1)))
    number = mm(wanted_low, jnp.ones((BLOCK, BLOCK), BF)).astype(BF)
    jj = iota((64, 64), 1)
    same = s == jj // 8
    qq = jj % 8

    def tile_of(position):
        return jnp.where(position < 3, 0, jnp.where(position < 6, 1, 2))

    lead = mm(hot(same & (tile_of(q) == tile_of(qq)) & (qq < q)), number)
    sums = [mm(hot(same & (tile_of(qq) == t)), number) for t in range(TILES)]
    start1 = jnp.maximum(float(BLOCK), sums[0])
    start2 = jnp.maximum(float(2 * BLOCK), start1 + sums[1])
    end = start2 + sums[2]
    q_wide = iota((64, BLOCK), 0) % 8
    start = jnp.where(q_wide < 3, 0.0, jnp.where(q_wide < 6, start1, start2))
    rank = (start + lead + before).astype(I32)
    codes = jnp.where(wanted > 0.5, block * 1024 + rank, -1)
    overflow = jnp.max(jnp.where(end > float(CAP), 1.0, 0.0))
    position = (iota((64, BLOCK), 0) // 8) * CAP + rank
    high = lax.shift_right_arithmetic(position, 7).astype(F32).astype(BF)
    low = jnp.bitwise_and(position, 127).astype(F32).astype(BF)
    high_slot = mm(perm, high, TN).astype(BF)
    low_slot = mm(perm, low, TN).astype(BF)
    high_ids = mm(high_slot, slot_hot, TN)
    low_ids = mm(low_slot, slot_hot, TN)
    value = jnp.sum(jnp.where(row_is, high_ids * 128.0 + low_ids, 0.0), axis=0, keepdims=True)
    places = jnp.where(slot >= 0, value.astype(I32), -1)
    return codes, places, overflow


def twice(row):
    return jnp.concatenate([row, row], axis=1)


def fetch_kernel(
    ent_ref, ids_ref, owner_ref, block_ref, rows_ref, place_ref, code_ref, flag_ref,
    tables, codes_mine, codes_in, stage, landed, total,
    ring_send, ring_recv, ask_send, ask_recv, tile_send, tile_recv,
):
    x, z, c, _ = place()
    me = x * CS + c
    _, right = z_peer(x, z, c, 1)
    _, left = z_peer(x, z, c, ZS - 1)
    peers = [x_peer(x, z, c, k) for k in range(XG)]
    for half in range(2):
        tables[0, half] = ent_ref[:, half * 256 : (half + 1) * 256].astype(BF)
    greet([right, left] + [peer for _, peer in peers[1:]])

    def ring(way, step, half):
        if way == 0:
            src, dst = (-step) % ZS, (-step - 1) % ZS
        else:
            src, dst = step, step + 1
        return remote(
            tables.at[src, half], tables.at[dst, half],
            ring_send.at[way, step, half], ring_recv.at[way, step, half],
            right if way == 0 else left,
        )

    def legs(step):
        if step < 3:
            return [(0, 0), (1, 0), (0, 1), (1, 1)]
        return [(0, 1), (1, 0)]

    for way, half in legs(0):
        ring(way, 0, half).start()

    def forward(step):
        for way, half in legs(step):
            ring(way, step, half).wait_recv()
            if step < 3 and (way, half) in legs(step + 1):
                ring(way, step + 1, half).start()

    codes, places, overflow = plan_rows(ids_ref[...], owner_ref[...], block_ref[...], z)
    codes_mine[...] = codes.reshape(XG, 8, BLOCK)
    place_ref[...] = places
    flag_ref[...] = jnp.zeros((8, BLOCK), F32) + overflow

    def ask(k):
        s, peer = peers[k]
        return remote(codes_mine.at[s], codes_in.at[me], ask_send.at[k], ask_recv.at[k], peer)

    for k in range(1, XG):
        ask(k).start()
    codes_in[me] = codes_mine[me]

    def tile(t, k):
        s, peer = peers[k]
        return remote(
            stage.at[t, k], landed.at[t, me], tile_send.at[t, k], tile_recv.at[t, k], peer
        )

    def select(t):
        parts = [(q, half) for q in range(FIRST_OF_TILE[t]) for half in range(2)]
        lhs = jnp.concatenate([tables[DIST[q], half] for q, half in parts], axis=1)
        key = (iota((BLOCK, 256), 1) // BLOCK) * 1024 + iota((BLOCK, 256), 0) + t * BLOCK
        for pair in range(XG // 2):
            both = (2 * pair + 1, (2 * pair + 2) % XG)
            chosen = []
            for k in both:
                code = codes_in[peers[k][0]]
                chosen.append(
                    jnp.concatenate(
                        [hot(twice(code[q : q + 1]) == key + 2048 * half) for q, half in parts],
                        axis=1,
                    )
                )
            rows = mm(lhs, jnp.concatenate(chosen, axis=0), NT).astype(BF)
            for i, k in enumerate(both):
                part = rows[:, i * BLOCK : (i + 1) * BLOCK]
                if k == 0:
                    landed[t, me] = part
                else:
                    stage[t, k] = part
                    tile(t, k).start()

    def gather(t):
        for k in range(1, XG):
            s = lax.rem(me + XG - k, XG)
            _, peer = peers[k]
            remote(
                stage.at[t, k], landed.at[t, s], tile_send.at[t, k], tile_recv.at[t, k], peer
            ).wait_recv()
        key = iota((XG * BLOCK, 256), 0)
        key = (key // BLOCK) * CAP + key % BLOCK + t * BLOCK

        def chunk(i, carry):
            lanes = pl.ds(pl.multiple_of(i * 256, 256), 256)
            lhs = jnp.concatenate([landed[t, s] for s in range(XG)], axis=1)
            rows = mm(lhs, hot(key == place_ref[:, lanes]))
            if t == 0:
                total[:, lanes] = rows
            elif t < TILES - 1:
                total[:, lanes] += rows
            else:
                rows_ref[:, lanes] = (total[:, lanes] + rows).astype(BF)
            return carry

        lax.fori_loop(0, ALL // 256, chunk, 0)

    forward(0)
    for k in range(1, XG):
        s = lax.rem(me + XG - k, XG)
        remote(
            codes_mine.at[s], codes_in.at[s], ask_send.at[k], ask_recv.at[k], peers[k][1]
        ).wait_recv()
    code_ref[...] = codes_in[...]
    select(0)
    forward(1)
    gather(0)
    forward(2)
    select(1)
    forward(3)
    select(2)
    gather(1)
    gather(2)
    for step in range(4):
        for way, half in legs(step):
            ring(way, step, half).wait_send()
    for k in range(1, XG):
        ask(k).wait_send()
        for t in range(TILES):
            tile(t, k).wait_send()


def vmem():
    return pl.BlockSpec(memory_space=pltpu.VMEM)


def fetch(ent, ids, owners, blocks):
    dma = pltpu.SemaphoreType.DMA
    return pl.pallas_call(
        fetch_kernel,
        out_shape=(
            jax.ShapeDtypeStruct((WIDTH, ALL), BF),
            jax.ShapeDtypeStruct((1, ALL), I32),
            jax.ShapeDtypeStruct((XG, 8, BLOCK), I32),
            jax.ShapeDtypeStruct((8, BLOCK), F32),
        ),
        in_specs=[vmem()] * 4,
        out_specs=[vmem()] * 4,
        scratch_shapes=[
            pltpu.VMEM((ZS, 2, WIDTH, 256), BF),
            pltpu.VMEM((XG, 8, BLOCK), I32),
            pltpu.VMEM((XG, 8, BLOCK), I32),
            pltpu.VMEM((TILES, XG, WIDTH, BLOCK), BF),
            pltpu.VMEM((TILES, XG, WIDTH, BLOCK), BF),
            pltpu.VMEM((WIDTH, ALL), F32),
            dma((2, 4, 2)), dma((2, 4, 2)),
            dma((XG,)), dma((XG,)),
            dma((TILES, XG)), dma((TILES, XG)),
        ],
        compiler_params=pltpu.CompilerParams(
            collective_id=0, has_side_effects=True, vmem_limit_bytes=56 * MIB
        ),
        name="fetch",
    )(ent, ids, owners, blocks)


def side(positive, scores, valid):
    largest = jnp.maximum(
        positive, jnp.max(jnp.where(valid, scores, -3e38), axis=0, keepdims=True)
    )
    own = jnp.exp(positive - largest)
    others = jnp.where(valid, jnp.exp(scores - largest), 0.0)
    total = own + jnp.sum(others, axis=0, keepdims=True)
    return own / total - 1.0, others / total


def edge_kernel(rows_ref, rel_ref, rel_ids_ref, flag_ref, grads_ref, relg_ref, hot_rel, high, low, edge_rel, neg_sum):
    mid = WIDTH // 2
    high[...] = jnp.zeros_like(high)
    low[...] = jnp.zeros_like(low)
    rel = rel_ref[...]
    rel_high = rel.astype(BF)
    high[:, 0:REL] = rel_high
    low[:, 0:REL] = (rel - rel_high.astype(F32)).astype(BF)
    neg_sum[...] = jnp.zeros_like(neg_sum)
    step = 256

    def chunk(i, carry):
        lanes = pl.ds(pl.multiple_of(i * step, step), step)
        tail_lanes = pl.ds(pl.multiple_of(EDGES + i * step, step), step)
        which = hot(iota((REL_PAD, step), 0) == rel_ids_ref[:, lanes])
        hot_rel[:, lanes] = which
        relation = mm(high[...], which) + mm(low[...], which)
        a, b = relation[:mid], relation[mid:]
        head = rows_ref[:, lanes].astype(F32)
        tail = rows_ref[:, tail_lanes].astype(F32)
        hr, hi = head[:mid], head[mid:]
        tr, ti = tail[:mid], tail[mid:]
        query = jnp.concatenate([hr * a - hi * b, hr * b + hi * a], axis=0)
        probe = jnp.concatenate([a * tr + b * ti, a * ti - b * tr], axis=0)
        positive = jnp.sum(query * tail, axis=0, keepdims=True)
        query_low, probe_low = query.astype(BF), probe.astype(BF)
        tail_neg = rows_ref[:, 2 * EDGES : 2 * EDGES + BLOCK]
        head_neg = rows_ref[:, 2 * EDGES + BLOCK : 2 * EDGES + 2 * BLOCK]
        valid = iota((BLOCK, step), 0) < NEG
        tail_coef, tail_weights = side(positive, mm(tail_neg, query_low, TN), valid)
        head_coef, head_weights = side(positive, mm(head_neg, probe_low, TN), valid)
        tail_low, head_low = tail_weights.astype(BF), head_weights.astype(BF)
        both = tail_coef + head_coef
        qg = both * tail + mm(tail_neg, tail_low)
        pg = mm(head_neg, head_low)
        neg_sum[0] += mm(query_low, tail_low, NT)
        neg_sum[1] += mm(probe_low, head_low, NT)
        qr, qi = qg[:mid], qg[mid:]
        pr, pi = pg[:mid], pg[mid:]
        grads_ref[:, lanes] = jnp.concatenate(
            [qr * a + qi * b, qi * a - qr * b], axis=0
        ).astype(BF)
        grads_ref[:, tail_lanes] = (
            both * query + jnp.concatenate([pr * a - pi * b, pr * b + pi * a], axis=0)
        ).astype(BF)
        edge_rel[:, lanes] = jnp.concatenate(
            [
                qr * hr + qi * hi + pr * tr + pi * ti,
                qi * hr - qr * hi + pr * ti - pi * tr,
            ],
            axis=0,
        ).astype(BF)
        return carry

    lax.fori_loop(0, EDGES // step, chunk, 0)
    grads_ref[:, 2 * EDGES : 2 * EDGES + BLOCK] = neg_sum[0].astype(BF)
    grads_ref[:, 2 * EDGES + BLOCK : 2 * EDGES + 2 * BLOCK] = neg_sum[1].astype(BF)

    def scatter(i, carry):
        lanes = pl.ds(pl.multiple_of(i * 256, 256), 256)
        relg_ref[:, lanes] = mm(edge_rel[...], hot_rel[lanes, :], NT)
        return carry

    lax.fori_loop(0, REL_PAD // 256, scatter, 0)
    spare = iota((WIDTH, BLOCK), 1) + (REL_PAD - BLOCK) >= REL
    relg_ref[:, REL_PAD - BLOCK :] = jnp.where(
        spare, flag_ref[0:1, :], relg_ref[:, REL_PAD - BLOCK :]
    )


def edge_grads(rows, rel, rel_ids, flag):
    return pl.pallas_call(
        edge_kernel,
        out_shape=(
            jax.ShapeDtypeStruct((WIDTH, ALL), BF),
            jax.ShapeDtypeStruct((WIDTH, REL_PAD), F32),
        ),
        in_specs=[vmem()] * 4,
        out_specs=[vmem()] * 2,
        scratch_shapes=[
            pltpu.VMEM((REL_PAD, EDGES), BF),
            pltpu.VMEM((WIDTH, REL_PAD), BF),
            pltpu.VMEM((WIDTH, REL_PAD), BF),
            pltpu.VMEM((WIDTH, EDGES), BF),
            pltpu.VMEM((2, WIDTH, BLOCK), F32),
        ],
        compiler_params=pltpu.CompilerParams(vmem_limit_bytes=56 * MIB),
        name="edges",
    )(rows, rel, rel_ids, flag)


def give_kernel(
    grads_ref, place_ref, code_ref, relg_ref, ent_ref, rel_ref, flag_ref,
    stage, landed, ring_out, ring_in,
    core_out, core_in, y_out, y_in, z_out, z_in, x_out, x_in, zg_out, zg_in, yg_out, yg_in, cg_in,
    sum_core, sum_y,
    tile_send, tile_recv, ring_send, ring_recv,
    core_send, core_recv, y_send, y_recv, z_send, z_recv, x_send, x_recv,
    zg_send, zg_recv, yg_send, yg_recv, cg_send, cg_recv,
):
    x, z, c, y = place()
    me = x * CS + c
    z_peers = [z_peer(x, z, c, k) for k in range(ZS)]
    x_peers = [x_peer(x, z, c, k) for k in range(XG)]
    y_peers = [(lax.rem(y + k, YS), {"row": lax.rem(y + k, YS)}) for k in range(YS)]
    same_core = [
        (lax.rem(x + k, XS), {"bucket": bucket_of(lax.rem(x + k, XS), z, c)}) for k in range(XS)
    ]
    mate = {"bucket": bucket_of(x, z, 1 - c)}
    right, left = z_peers[1][1], z_peers[ZS - 1][1]
    greet([p for _, p in z_peers[1:]] + [p for _, p in x_peers[1:]] + [p for _, p in y_peers[1:]])

    def core_copy():
        return remote(core_out, core_in, core_send, core_recv, mate)

    def rel_core():
        core_out[...] = relg_ref[pl.ds(pl.multiple_of((1 - c) * HALF_START, 16), HALF), :].astype(BF)
        core_copy().start()

    def y_copy(k):
        return remote(y_out.at[k], y_in.at[k], y_send.at[k], y_recv.at[k], y_peers[k][1])

    def rel_y():
        core_copy().wait_recv()
        mine = pl.ds(pl.multiple_of(c * HALF_START, 16), HALF)
        sum_core[...] = relg_ref[mine, :] + core_in[...].astype(F32)
        for k in range(1, YS):
            other = y_peers[k][0]
            y_out[k] = sum_core[:, pl.ds(pl.multiple_of(other * 384, 128), 384)].astype(BF)
            y_copy(k).start()

    def z_copy(k):
        return remote(z_out.at[k], z_in.at[k], z_send.at[k], z_recv.at[k], z_peers[k][1])

    def rel_z():
        for k in range(1, YS):
            y_copy(k).wait_recv()
        summed = sum_core[:, pl.ds(pl.multiple_of(y * 384, 128), 384)]
        for k in range(1, YS):
            summed = summed + y_in[k].astype(F32)
        sum_y[...] = jnp.zeros_like(sum_y)
        sum_y[0:HALF, :] = summed
        for k in range(1, ZS):
            other = z_peers[k][0]
            z_out[k] = sum_y[pl.ds(pl.multiple_of(other * 32, 32), 32), :].astype(BF)
            z_copy(k).start()

    def x_copy(k):
        return remote(x_out, x_in.at[x], x_send.at[k], x_recv.at[k], same_core[k][1])

    def rel_x():
        for k in range(1, ZS):
            z_copy(k).wait_recv()
        summed = sum_y[pl.ds(pl.multiple_of(z * 32, 32), 32), :]
        for k in range(1, ZS):
            summed = summed + z_in[k].astype(F32)
        x_out[...] = summed
        x_in[x] = summed
        for k in range(1, XS):
            x_copy(k).start()

    def zg_copy(k):
        return remote(zg_out, zg_in.at[z], zg_send.at[k], zg_recv.at[k], z_peers[k][1])

    def rel_zg():
        for k in range(1, XS):
            s = lax.rem(x + XS - k, XS)
            remote(x_out, x_in.at[s], x_send.at[k], x_recv.at[k], same_core[k][1]).wait_recv()
        summed = ((x_in[0] + x_in[1]) + (x_in[2] + x_in[3])).astype(BF)
        zg_out[...] = summed
        zg_in[z] = summed
        for k in range(1, ZS):
            zg_copy(k).start()

    def yg_copy(k):
        return remote(yg_out, yg_in.at[y], yg_send.at[k], yg_recv.at[k], y_peers[k][1])

    def rel_yg():
        for k in range(1, ZS):
            s = lax.rem(z + ZS - k, ZS)
            remote(zg_out, zg_in.at[s], zg_send.at[k], zg_recv.at[k], z_peers[k][1]).wait_recv()
        whole = jnp.concatenate([zg_in[i] for i in range(ZS)], axis=0)[0:HALF]
        yg_out[...] = whole
        yg_in[y] = whole
        for k in range(1, YS):
            yg_copy(k).start()

    def cg_copy():
        return remote(yg_in, cg_in, cg_send, cg_recv, mate)

    def rel_cg():
        for k in range(1, YS):
            s = lax.rem(y + YS - k, YS)
            remote(yg_out, yg_in.at[s], yg_send.at[k], yg_recv.at[k], y_peers[k][1]).wait_recv()
        cg_copy().start()

    def rel_end():
        cg_copy().wait_recv()
        for i in range(YS):
            mine, other = yg_in[i].astype(F32), cg_in[i].astype(F32)
            first = jnp.where(c == 0, mine, other)
            second = jnp.where(c == 0, other, mine)
            whole = jnp.concatenate([first, second[HALF - HALF_START :]], axis=0)
            if i < YS - 1:
                rel_ref[:, i * 384 : (i + 1) * 384] = whole
            else:
                rel_ref[:, i * 384 : REL] = whole[:, : REL - i * 384]
                flag_ref[...] = whole[0:8, 256:384]

    def tile(t, k):
        return remote(
            stage.at[t, k], landed.at[t, me], tile_send.at[t, k], tile_recv.at[t, k], x_peers[k][1]
        )

    def scatter(t):
        for pair in range(XG // 2):
            both = (2 * pair + 1, (2 * pair + 2) % XG)
            row = iota((BLOCK, ALL), 0) + t * BLOCK
            which = jnp.concatenate(
                [hot(row + x_peers[k][0] * CAP == place_ref[...]) for k in both], axis=0
            )
            rows = mm(grads_ref[...], which, NT).astype(BF)
            for i, k in enumerate(both):
                part = rows[:, i * BLOCK : (i + 1) * BLOCK]
                if k == 0:
                    landed[t, me] = part
                else:
                    stage[t, k] = part
                    tile(t, k).start()

    def arrive(t):
        for k in range(1, XG):
            s = lax.rem(me + XG - k, XG)
            remote(
                stage.at[t, k], landed.at[t, s], tile_send.at[t, k], tile_recv.at[t, k],
                x_peers[k][1],
            ).wait_recv()

    def partial(dist, half):
        q = DIST.index(dist)
        parts = [(t, s) for t in range(TILES_OF[q], TILES) for s in range(XG)]
        lhs = jnp.concatenate([landed[t, s] for t, s in parts], axis=1)
        key = (iota((BLOCK, 256), 1) // BLOCK + 2 * half) * 1024 + iota((BLOCK, 256), 0)
        which = jnp.concatenate(
            [hot(twice(code_ref[s, q : q + 1]) == key + t * BLOCK) for t, s in parts], axis=0
        )
        return mm(lhs, which)

    def ring(way, step, half):
        return remote(
            ring_out.at[way, step, half], ring_in.at[way, step, half],
            ring_send.at[way, step, half], ring_recv.at[way, step, half],
            right if way == 0 else left,
        )

    def has(way, step, half):
        return 0 < step or half == 1 - way

    def push(step, way):
        dist = 4 - step if way == 0 else (4 + step) % ZS
        order = (0, 1) if way == 0 else (1, 0)
        for half in order:
            if not has(way, step, half):
                continue
            value = partial(dist, half)
            if step > 0 and has(way, step - 1, half):
                ring(way, step - 1, half).wait_recv()
                value = value + ring_in[way, step - 1, half].astype(F32)
            ring_out[way, step, half] = value.astype(BF)
            ring(way, step, half).start()

    rel_core()
    scatter(2)
    rel_y()
    scatter(1)
    scatter(0)
    arrive(2)
    push(0, 0)
    push(0, 1)
    push(1, 1)
    rel_z()
    arrive(1)
    push(1, 0)
    rel_x()
    push(2, 1)
    push(2, 0)
    rel_zg()
    arrive(0)
    push(3, 1)
    push(3, 0)
    rel_yg()
    own = [partial(0, half) for half in range(2)]
    rel_cg()
    for half in range(2):
        ring(0, 3, half).wait_recv()
        ring(1, 3, half).wait_recv()
        ent_ref[:, half * 256 : (half + 1) * 256] = (
            own[half] + ring_in[0, 3, half].astype(F32) + ring_in[1, 3, half].astype(F32)
        )
    rel_end()

    core_copy().wait_send()
    cg_copy().wait_send()
    for k in range(1, YS):
        y_copy(k).wait_send()
        yg_copy(k).wait_send()
    for k in range(1, ZS):
        z_copy(k).wait_send()
        zg_copy(k).wait_send()
    for k in range(1, XS):
        x_copy(k).wait_send()
    for k in range(1, XG):
        for t in range(TILES):
            tile(t, k).wait_send()
    for way in range(2):
        for step in range(4):
            for half in range(2):
                if has(way, step, half):
                    ring(way, step, half).wait_send()


def give(grads, places, codes, relg):
    dma = pltpu.SemaphoreType.DMA
    v = pltpu.VMEM
    return pl.pallas_call(
        give_kernel,
        out_shape=(
            jax.ShapeDtypeStruct((WIDTH, 512), F32),
            jax.ShapeDtypeStruct((WIDTH, REL), F32),
            jax.ShapeDtypeStruct((8, BLOCK), F32),
        ),
        in_specs=[vmem()] * 4,
        out_specs=[vmem()] * 3,
        scratch_shapes=[
            v((TILES, XG, WIDTH, BLOCK), BF), v((TILES, XG, WIDTH, BLOCK), BF),
            v((2, 4, 2, WIDTH, 256), BF), v((2, 4, 2, WIDTH, 256), BF),
            v((HALF, REL_PAD), BF), v((HALF, REL_PAD), BF),
            v((YS, HALF, 384), BF), v((YS, HALF, 384), BF),
            v((ZS, 32, 384), BF), v((ZS, 32, 384), BF),
            v((32, 384), F32), v((XS, 32, 384), F32),
            v((32, 384), BF), v((ZS, 32, 384), BF),
            v((HALF, 384), BF), v((YS, HALF, 384), BF), v((YS, HALF, 384), BF),
            v((HALF, REL_PAD), F32), v((256, 384), F32),
            dma((TILES, XG)), dma((TILES, XG)), dma((2, 4, 2)), dma((2, 4, 2)),
            dma, dma, dma((YS,)), dma((YS,)), dma((ZS,)), dma((ZS,)), dma((XS,)), dma((XS,)),
            dma((ZS,)), dma((ZS,)), dma((YS,)), dma((YS,)), dma, dma,
        ],
        compiler_params=pltpu.CompilerParams(
            collective_id=1, has_side_effects=True, vmem_limit_bytes=56 * MIB
        ),
        name="give",
    )(grads, places, codes, relg)


def side_weights(positive, scores):
    largest = jnp.maximum(positive, jnp.max(scores, axis=1))
    own_term = jnp.exp(positive - largest)
    others = jnp.exp(scores - largest[:, None])
    total = own_term + jnp.sum(others, axis=1)
    return (own_term / total - 1.0, others / total[:, None])


def edge_block_grads(buffer, relations, head_ids, rel_ids, tail_ids, neg_tail, neg_head):
    middle = relations.shape[1] // 2
    head_rows = jnp.take(buffer, head_ids, axis=0).astype(jnp.float32)
    tail_rows = jnp.take(buffer, tail_ids, axis=0).astype(jnp.float32)
    rel_rows = jnp.take(relations, rel_ids, axis=0)
    rel_real, rel_imag = (rel_rows[:, :middle], rel_rows[:, middle:])
    head_real, head_imag = (head_rows[:, :middle], head_rows[:, middle:])
    tail_real, tail_imag = (tail_rows[:, :middle], tail_rows[:, middle:])
    query = jnp.concatenate(
        [head_real * rel_real - head_imag * rel_imag, head_real * rel_imag + head_imag * rel_real],
        axis=1,
    )
    probe = jnp.concatenate(
        [rel_real * tail_real + rel_imag * tail_imag, rel_real * tail_imag - rel_imag * tail_real],
        axis=1,
    )
    positive = jnp.sum(query * tail_rows, axis=1)
    tail_negs = jnp.take(buffer, neg_tail, axis=0)
    head_negs = jnp.take(buffer, neg_head, axis=0)
    query_low = query.astype(jnp.bfloat16)
    probe_low = probe.astype(jnp.bfloat16)
    contract_last = (((1,), (1,)), ((), ()))
    contract_first = (((0,), (0,)), ((), ()))
    tail_scores = lax.dot_general(
        query_low, tail_negs, contract_last, preferred_element_type=jnp.float32
    )
    head_scores = lax.dot_general(
        probe_low, head_negs, contract_last, preferred_element_type=jnp.float32
    )
    tail_coef, tail_weights = side_weights(positive, tail_scores)
    head_coef, head_weights = side_weights(positive, head_scores)
    tail_low = tail_weights.astype(jnp.bfloat16)
    head_low = head_weights.astype(jnp.bfloat16)
    both_coef = (tail_coef + head_coef)[:, None]
    query_grad = both_coef * tail_rows + jnp.dot(
        tail_low, tail_negs, preferred_element_type=jnp.float32
    )
    probe_grad = jnp.dot(head_low, head_negs, preferred_element_type=jnp.float32)
    tail_neg_grad = lax.dot_general(
        tail_low, query_low, contract_first, preferred_element_type=jnp.float32
    )
    head_neg_grad = lax.dot_general(
        head_low, probe_low, contract_first, preferred_element_type=jnp.float32
    )
    qgrad_real, qgrad_imag = (query_grad[:, :middle], query_grad[:, middle:])
    pgrad_real, pgrad_imag = (probe_grad[:, :middle], probe_grad[:, middle:])
    head_grad = jnp.concatenate(
        [
            qgrad_real * rel_real + qgrad_imag * rel_imag,
            qgrad_imag * rel_real - qgrad_real * rel_imag,
        ],
        axis=1,
    )
    tail_grad = both_coef * query + jnp.concatenate(
        [
            pgrad_real * rel_real - pgrad_imag * rel_imag,
            pgrad_real * rel_imag + pgrad_imag * rel_real,
        ],
        axis=1,
    )
    rel_edge_grad = jnp.concatenate(
        [
            qgrad_real * head_real
            + qgrad_imag * head_imag
            + pgrad_real * tail_real
            + pgrad_imag * tail_imag,
            qgrad_imag * head_real
            - qgrad_real * head_imag
            + pgrad_real * tail_imag
            - pgrad_imag * tail_real,
        ],
        axis=1,
    )
    row_ids = jnp.concatenate([head_ids, tail_ids, neg_tail, neg_head])
    row_vals = jnp.concatenate([head_grad, tail_grad, tail_neg_grad, head_neg_grad], axis=0)
    return (row_ids, row_vals, rel_edge_grad)


def device_grads(buffer, relations, head_ids, rel_ids, tail_ids, neg_tail, neg_head):
    blocks_count = neg_tail.shape[0]
    start_zero = (jnp.zeros(buffer.shape, jnp.float32), jnp.zeros(relations.shape, jnp.float32))

    def advance(totals, position):
        row_ids, row_vals, rel_edge_grad = edge_block_grads(
            buffer, relations, head_ids, rel_ids, tail_ids, neg_tail[position], neg_head[position]
        )
        return (
            (totals[0].at[row_ids].add(row_vals), totals[1].at[rel_ids].add(rel_edge_grad)),
            None,
        )

    totals, unused = lax.scan(advance, start_zero, jnp.arange(blocks_count, dtype=jnp.int32))
    return totals


def dense_step(
    entities, relations, touch_owner, touch_block, head_ids, rel_ids, tail_ids, neg_tail, neg_head
):
    bucket_count = lax.axis_size("bucket")
    block_rows = BLOCK
    width = entities.shape[1]
    owned = entities.shape[0] // block_rows
    owners = touch_owner[0]
    wanted = touch_block[0]
    touched = owners.shape[0]
    slot_ids = jnp.arange(bucket_count, dtype=jnp.int32)
    matches = owners[:, None] == slot_ids[None, :]
    request = jnp.sum(jnp.where(matches, wanted[:, None] + 1, 0), axis=0) - 1
    incoming = lax.all_to_all(request, "bucket", split_axis=0, concat_axis=0, tiled=True)
    selector = (incoming[:, None] == jnp.arange(owned, dtype=jnp.int32)[None, :]).astype(
        jnp.float32
    )
    owned_flat = entities.reshape(owned, block_rows * width)
    reply = jnp.dot(selector, owned_flat, precision=lax.Precision.HIGHEST).astype(jnp.bfloat16)
    reply = reply.reshape(bucket_count, block_rows, width)
    fetched = lax.all_to_all(reply, "bucket", split_axis=0, concat_axis=0, tiled=True)
    buffer = jnp.take(fetched, owners, axis=0).reshape(touched * block_rows, width)
    buffer_grad, rel_part = device_grads(
        buffer, relations, head_ids, rel_ids, tail_ids, neg_tail, neg_head
    )
    outgoing = jnp.zeros((bucket_count, block_rows, width), jnp.float32)
    outgoing = outgoing.at[owners].set(buffer_grad.reshape(touched, block_rows, width))
    returned = lax.all_to_all(outgoing, "bucket", split_axis=0, concat_axis=0, tiled=True)
    entity_grad = lax.dot_general(
        selector,
        returned.reshape(bucket_count, block_rows * width),
        (((0,), (0,)), ((), ())),
        precision=lax.Precision.HIGHEST,
    )
    entity_grad = entity_grad.reshape(owned * block_rows, width)
    relation_grad = lax.psum(rel_part, ("bucket", "row"))
    return (entity_grad, relation_grad)


def per_device(
    entities, relations, touch_owner, touch_block, head_ids, rel_ids, tail_ids, neg_tail, neg_head
):
    spare = jnp.full((BLOCK - NEG,), -1, I32)
    ids = jnp.concatenate([head_ids, tail_ids, neg_tail[0], spare, neg_head[0], spare])[None, :]
    rows, places, codes, flag = fetch(entities.T, ids, touch_owner, touch_block)
    grads, relg = edge_grads(rows, relations.T, rel_ids[None, :], flag)
    ent, rel, over = give(grads, places, codes, relg)
    return lax.cond(
        over[0, 0] > 0.5,
        lambda: dense_step(
            entities, relations, touch_owner, touch_block, head_ids, rel_ids, tail_ids,
            neg_tail, neg_head,
        ),
        lambda: (ent.T, rel.T),
    )


def solution(mesh):
    return jax.shard_map(
        per_device,
        mesh=mesh,
        in_specs=(
            P(("bucket", "row"), None),
            P(),
            P(("bucket", "row"), None),
            P(("bucket", "row"), None),
            P(("bucket", "row")),
            P(("bucket", "row")),
            P(("bucket", "row")),
            P(("bucket", "row"), None),
            P(("bucket", "row"), None),
        ),
        out_specs=(P(("bucket", "row"), None), P()),
        check_vma=False,
    )
```

```python
import functools

import jax
import jax.numpy as jnp
from jax import lax
from jax.experimental import pallas as pl
from jax.experimental.pallas import tpu as pltpu
from jax.sharding import PartitionSpec as P

BLOCK = 128
WIDTH = 400
EDGES = 1024
NEG = 100
REL = 1300
REL_PAD = 1536
ALL = 2 * EDGES + 2 * BLOCK
XS, ZS, CS, YS = 4, 8, 2, 4
XG = XS * CS
TILES = 3
CAP = TILES * BLOCK
DIST = (0, 1, 7, 2, 6, 3, 5, 4)
FIRST_OF_TILE = (3, 6, 8)
TILES_OF = (0, 0, 0, 1, 1, 1, 2, 2)
HALF = 208
HALF_START = 192
BF = jnp.bfloat16
F32 = jnp.float32
I32 = jnp.int32
NT = (((1,), (1,)), ((), ()))
TN = (((0,), (0,)), ((), ()))
MIB = 1024 * 1024


def mm(a, b, dims=(((1,), (0,)), ((), ()))):
    return lax.dot_general(a, b, dims, preferred_element_type=F32)


def iota(shape, dim):
    return lax.broadcasted_iota(I32, shape, dim)


def hot(mask):
    return jnp.where(mask, 1.0, 0.0).astype(BF)


def place():
    b = lax.axis_index("bucket")
    return b // (ZS * CS), (b // CS) % ZS, b % CS, lax.axis_index("row")


def bucket_of(x, z, c):
    return (x * ZS + z) * CS + c


def x_peer(x, z, c, k):
    s = lax.rem(x * CS + c + k, XG)
    return s, {"bucket": bucket_of(s // CS, z, s % CS)}


def z_peer(x, z, c, k):
    other = lax.rem(z + k, ZS)
    return other, {"bucket": bucket_of(x, other, c)}


def greet(peers):
    barrier = pltpu.get_barrier_semaphore()
    for peer in peers:
        pl.semaphore_signal(barrier, inc=1, device_id=peer, device_id_type=pl.DeviceIdType.MESH)
    pl.semaphore_wait(barrier, len(peers))


def remote(src, dst, send, recv, peer):
    return pltpu.make_async_remote_copy(
        src_ref=src, dst_ref=dst, send_sem=send, recv_sem=recv,
        device_id=peer, device_id_type=pl.DeviceIdType.MESH,
    )


def plan_rows(ids, owners, blocks, z):
    slot = lax.shift_right_arithmetic(ids, 7)
    row = jnp.bitwise_and(ids, 127)
    slot_hot = hot(iota((64, ALL), 0) == slot)
    row_is = iota((BLOCK, ALL), 0) == row
    row_hot = hot(row_is)
    count = mm(slot_hot, row_hot, NT)
    wanted_slot = hot(count > 0.5)
    j = iota((64, 64), 0)
    s, q = j // 8, j % 8
    dist = jnp.where(q % 2 == 1, (q + 1) // 2, (8 - q // 2) % 8)
    target = bucket_of(s // CS, (z + dist) % ZS, s % CS)
    perm_is = owners == target
    perm = hot(perm_is)
    wanted = mm(perm, wanted_slot)
    block = jnp.sum(jnp.where(perm_is, blocks, 0), axis=1, keepdims=True)
    wanted_low = wanted.astype(BF)
    before = mm(wanted_low, hot(iota((BLOCK, BLOCK), 0) < iota((BLOCK, BLOCK), 1)))
    number = mm(wanted_low, jnp.ones((BLOCK, BLOCK), BF)).astype(BF)
    jj = iota((64, 64), 1)
    same = s == jj // 8
    qq = jj % 8

    def tile_of(position):
        return jnp.where(position < 3, 0, jnp.where(position < 6, 1, 2))

    lead = mm(hot(same & (tile_of(q) == tile_of(qq)) & (qq < q)), number)
    sums = [mm(hot(same & (tile_of(qq) == t)), number) for t in range(TILES)]
    start1 = jnp.maximum(float(BLOCK), sums[0])
    start2 = jnp.maximum(float(2 * BLOCK), start1 + sums[1])
    end = start2 + sums[2]
    q_wide = iota((64, BLOCK), 0) % 8
    start = jnp.where(q_wide < 3, 0.0, jnp.where(q_wide < 6, start1, start2))
    rank = (start + lead + before).astype(I32)
    codes = jnp.where(wanted > 0.5, block * 1024 + rank, -1)
    overflow = jnp.max(jnp.where(end > float(CAP), 1.0, 0.0))
    position = (iota((64, BLOCK), 0) // 8) * CAP + rank
    high = lax.shift_right_arithmetic(position, 7).astype(F32).astype(BF)
    low = jnp.bitwise_and(position, 127).astype(F32).astype(BF)
    high_slot = mm(perm, high, TN).astype(BF)
    low_slot = mm(perm, low, TN).astype(BF)
    high_ids = mm(high_slot, slot_hot, TN)
    low_ids = mm(low_slot, slot_hot, TN)
    value = jnp.sum(jnp.where(row_is, high_ids * 128.0 + low_ids, 0.0), axis=0, keepdims=True)
    places = jnp.where(slot >= 0, value.astype(I32), -1)
    return codes, places, overflow


def twice(row):
    return jnp.concatenate([row, row], axis=1)


def side(positive, scores, valid):
    largest = jnp.maximum(
        positive, jnp.max(jnp.where(valid, scores, -3e38), axis=0, keepdims=True)
    )
    own = jnp.exp(positive - largest)
    others = jnp.where(valid, jnp.exp(scores - largest), 0.0)
    total = own + jnp.sum(others, axis=0, keepdims=True)
    return own / total - 1.0, others / total


def step_kernel(
    ent_ref, rel_in_ref, owner_ref, block_ref, head_ref, rel_ids_ref, tail_ref, ntail_ref, nhead_ref,
    ent_ref_a, ent_ref_b, rel_ref, flag_ref,
    tables, codes_mine, codes_in, fstage, flanded, total, ids_ref, place_ref, rows_ref,
    hot_rel, high, low, relation, edge_rel, neg_sum, grads_ref, relg_ref,
    stage, landed, ring_out, ring_in,
    core_out, core_in, y_out, y_in, z_out, z_in, x_out, x_in, zg_out, zg_in, yg_out, yg_in, cg_in,
    sum_core, sum_y,
    gring_send, gring_recv, ask_send, ask_recv, ftile_send, ftile_recv,
    tile_send, tile_recv, ring_send, ring_recv,
    core_send, core_recv, y_send, y_recv, z_send, z_recv, x_send, x_recv,
    zg_send, zg_recv, yg_send, yg_recv, cg_send, cg_recv,
):
    x, z, c, y = place()
    me = x * CS + c
    z_peers = [z_peer(x, z, c, k) for k in range(ZS)]
    x_peers = [x_peer(x, z, c, k) for k in range(XG)]
    y_peers = [(lax.rem(y + k, YS), {"row": lax.rem(y + k, YS)}) for k in range(YS)]
    same_core = [
        (lax.rem(x + k, XS), {"bucket": bucket_of(lax.rem(x + k, XS), z, c)}) for k in range(XS)
    ]
    mate = {"bucket": bucket_of(x, z, 1 - c)}
    right, left = z_peers[1][1], z_peers[ZS - 1][1]
    mid = WIDTH // 2

    for half in range(2):
        tables[0, half] = ent_ref[:, half * 256 : (half + 1) * 256].astype(BF)
    greet([p for _, p in z_peers[1:]] + [p for _, p in x_peers[1:]] + [p for _, p in y_peers[1:]])

    def gring(way, step, half):
        if way == 0:
            src, dst = (-step) % ZS, (-step - 1) % ZS
        else:
            src, dst = step, step + 1
        return remote(
            tables.at[src, half], tables.at[dst, half],
            gring_send.at[way, step, half], gring_recv.at[way, step, half],
            right if way == 0 else left,
        )

    def legs(step):
        if step < 3:
            return [(0, 0), (1, 0), (0, 1), (1, 1)]
        return [(0, 1), (1, 0)]

    def forward(step, halves=(0, 1)):
        for way, half in legs(step):
            if half not in halves:
                continue
            gring(way, step, half).wait_recv()
            if step < 3 and (way, half) in legs(step + 1):
                gring(way, step + 1, half).start()

    def ask(k):
        s, peer = x_peers[k]
        return remote(codes_mine.at[s], codes_in.at[me], ask_send.at[k], ask_recv.at[k], peer)

    def ftile(t, k):
        return remote(
            fstage.at[t, k], flanded.at[t, me], ftile_send.at[t, k], ftile_recv.at[t, k],
            x_peers[k][1],
        )

    def select(t, first, last, send):
        parts = [(q, half) for q in range(first, last) for half in range(2)]
        lhs = jnp.concatenate([tables[DIST[q], half] for q, half in parts], axis=1)
        key = (iota((BLOCK, 256), 1) // BLOCK) * 1024 + iota((BLOCK, 256), 0) + t * BLOCK
        for pair in range(XG // 2):
            both = (2 * pair + 1, (2 * pair + 2) % XG)
            chosen = []
            for k in both:
                code = codes_in[x_peers[k][0]]
                chosen.append(
                    jnp.concatenate(
                        [hot(twice(code[q : q + 1]) == key + 2048 * half) for q, half in parts],
                        axis=1,
                    )
                )
            rows = mm(lhs, jnp.concatenate(chosen, axis=0), NT).astype(BF)
            for i, k in enumerate(both):
                part = rows[:, i * BLOCK : (i + 1) * BLOCK]
                if first > 0:
                    part = part + fstage[t, k]
                if send and k == 0:
                    flanded[t, me] = part
                else:
                    fstage[t, k] = part
                    if send:
                        ftile(t, k).start()

    def gather(t):
        for k in range(1, XG):
            s = lax.rem(me + XG - k, XG)
            remote(
                fstage.at[t, k], flanded.at[t, s], ftile_send.at[t, k], ftile_recv.at[t, k],
                x_peers[k][1],
            ).wait_recv()
        key = iota((XG * BLOCK, 256), 0)
        key = (key // BLOCK) * CAP + key % BLOCK + t * BLOCK

        def chunk(i, carry):
            lanes = pl.ds(pl.multiple_of(i * 256, 256), 256)
            lhs = jnp.concatenate([flanded[t, s] for s in range(XG)], axis=1)
            rows = mm(lhs, hot(key == place_ref[:, lanes]))
            if t == 0:
                total[:, lanes] = rows
            elif t < TILES - 1:
                total[:, lanes] += rows
            else:
                rows_ref[:, lanes] = (total[:, lanes] + rows).astype(BF)
            return carry

        lax.fori_loop(0, ALL // 256, chunk, 0)

    def relation_rows():
        high[...] = jnp.zeros_like(high)
        low[...] = jnp.zeros_like(low)
        rel = rel_in_ref[...]
        rel_high = rel.astype(BF)
        high[:, 0:REL] = rel_high
        low[:, 0:REL] = (rel - rel_high.astype(F32)).astype(BF)

        def chunk(i, carry):
            lanes = pl.ds(pl.multiple_of(i * 256, 256), 256)
            which = hot(iota((REL_PAD, 256), 0) == rel_ids_ref[:, lanes])
            hot_rel[:, lanes] = which
            relation[:, lanes] = mm(high[...], which) + mm(low[...], which)
            return carry

        lax.fori_loop(0, EDGES // 256, chunk, 0)

    def edges():
        neg_sum[...] = jnp.zeros_like(neg_sum)
        step = 256

        def chunk(i, carry):
            lanes = pl.ds(pl.multiple_of(i * step, step), step)
            tail_lanes = pl.ds(pl.multiple_of(EDGES + i * step, step), step)
            a, b = relation[0:mid, lanes], relation[mid:WIDTH, lanes]
            head = rows_ref[:, lanes].astype(F32)
            tail = rows_ref[:, tail_lanes].astype(F32)
            hr, hi = head[:mid], head[mid:]
            tr, ti = tail[:mid], tail[mid:]
            query = jnp.concatenate([hr * a - hi * b, hr * b + hi * a], axis=0)
            probe = jnp.concatenate([a * tr + b * ti, a * ti - b * tr], axis=0)
            positive = jnp.sum(query * tail, axis=0, keepdims=True)
            query_low, probe_low = query.astype(BF), probe.astype(BF)
            tail_neg = rows_ref[:, 2 * EDGES : 2 * EDGES + BLOCK]
            head_neg = rows_ref[:, 2 * EDGES + BLOCK : 2 * EDGES + 2 * BLOCK]
            valid = iota((BLOCK, step), 0) < NEG
            tail_coef, tail_weights = side(positive, mm(tail_neg, query_low, TN), valid)
            head_coef, head_weights = side(positive, mm(head_neg, probe_low, TN), valid)
            tail_low, head_low = tail_weights.astype(BF), head_weights.astype(BF)
            both = tail_coef + head_coef
            qg = both * tail + mm(tail_neg, tail_low)
            pg = mm(head_neg, head_low)
            neg_sum[0] += mm(query_low, tail_low, NT)
            neg_sum[1] += mm(probe_low, head_low, NT)
            qr, qi = qg[:mid], qg[mid:]
            pr, pi = pg[:mid], pg[mid:]
            grads_ref[:, lanes] = jnp.concatenate(
                [qr * a + qi * b, qi * a - qr * b], axis=0
            ).astype(BF)
            grads_ref[:, tail_lanes] = (
                both * query + jnp.concatenate([pr * a - pi * b, pr * b + pi * a], axis=0)
            ).astype(BF)
            edge_rel[:, lanes] = jnp.concatenate(
                [
                    qr * hr + qi * hi + pr * tr + pi * ti,
                    qi * hr - qr * hi + pr * ti - pi * tr,
                ],
                axis=0,
            ).astype(BF)
            return carry

        lax.fori_loop(0, EDGES // step, chunk, 0)
        grads_ref[:, 2 * EDGES : 2 * EDGES + BLOCK] = neg_sum[0].astype(BF)
        grads_ref[:, 2 * EDGES + BLOCK : 2 * EDGES + 2 * BLOCK] = neg_sum[1].astype(BF)

    def relation_scatter(overflow):
        def chunk(i, carry):
            lanes = pl.ds(pl.multiple_of(i * 256, 256), 256)
            relg_ref[:, lanes] = mm(edge_rel[...], hot_rel[lanes, :], NT)
            return carry

        lax.fori_loop(0, REL_PAD // 256, chunk, 0)
        relg_ref[:, REL_PAD - BLOCK :] = jnp.zeros((WIDTH, BLOCK), F32) + overflow

    def core_copy():
        return remote(core_out, core_in, core_send, core_recv, mate)

    def rel_core():
        core_out[...] = relg_ref[pl.ds(pl.multiple_of((1 - c) * HALF_START, 16), HALF), :].astype(BF)
        core_copy().start()

    def y_copy(k):
        return remote(y_out.at[k], y_in.at[k], y_send.at[k], y_recv.at[k], y_peers[k][1])

    def rel_y():
        core_copy().wait_recv()
        mine = pl.ds(pl.multiple_of(c * HALF_START, 16), HALF)
        sum_core[...] = relg_ref[mine, :] + core_in[...].astype(F32)
        for k in range(1, YS):
            other = y_peers[k][0]
            y_out[k] = sum_core[:, pl.ds(pl.multiple_of(other * 384, 128), 384)].astype(BF)
            y_copy(k).start()

    def z_copy(k):
        return remote(z_out.at[k], z_in.at[k], z_send.at[k], z_recv.at[k], z_peers[k][1])

    def rel_z():
        for k in range(1, YS):
            y_copy(k).wait_recv()
        summed = sum_core[:, pl.ds(pl.multiple_of(y * 384, 128), 384)]
        for k in range(1, YS):
            summed = summed + y_in[k].astype(F32)
        sum_y[...] = jnp.zeros_like(sum_y)
        sum_y[0:HALF, :] = summed
        for k in range(1, ZS):
            other = z_peers[k][0]
            z_out[k] = sum_y[pl.ds(pl.multiple_of(other * 32, 32), 32), :].astype(BF)
            z_copy(k).start()

    def x_copy(k):
        return remote(x_out, x_in.at[x], x_send.at[k], x_recv.at[k], same_core[k][1])

    def rel_x():
        for k in range(1, ZS):
            z_copy(k).wait_recv()
        summed = sum_y[pl.ds(pl.multiple_of(z * 32, 32), 32), :]
        for k in range(1, ZS):
            summed = summed + z_in[k].astype(F32)
        x_out[...] = summed
        x_in[x] = summed
        for k in range(1, XS):
            x_copy(k).start()

    def zg_copy(k):
        return remote(zg_out, zg_in.at[z], zg_send.at[k], zg_recv.at[k], z_peers[k][1])

    def rel_zg():
        for k in range(1, XS):
            s = lax.rem(x + XS - k, XS)
            remote(x_out, x_in.at[s], x_send.at[k], x_recv.at[k], same_core[k][1]).wait_recv()
        summed = ((x_in[0] + x_in[1]) + (x_in[2] + x_in[3])).astype(BF)
        zg_out[...] = summed
        zg_in[z] = summed
        for k in range(1, ZS):
            zg_copy(k).start()

    def yg_copy(k):
        return remote(yg_out, yg_in.at[y], yg_send.at[k], yg_recv.at[k], y_peers[k][1])

    def rel_yg():
        for k in range(1, ZS):
            s = lax.rem(z + ZS - k, ZS)
            remote(zg_out, zg_in.at[s], zg_send.at[k], zg_recv.at[k], z_peers[k][1]).wait_recv()
        whole = jnp.concatenate([zg_in[i] for i in range(ZS)], axis=0)[0:HALF]
        yg_out[...] = whole
        yg_in[y] = whole
        for k in range(1, YS):
            yg_copy(k).start()

    def cg_copy():
        return remote(yg_in, cg_in, cg_send, cg_recv, mate)

    def rel_cg():
        for k in range(1, YS):
            s = lax.rem(y + YS - k, YS)
            remote(yg_out, yg_in.at[s], yg_send.at[k], yg_recv.at[k], y_peers[k][1]).wait_recv()
        cg_copy().start()

    def rel_end():
        cg_copy().wait_recv()
        for i in range(YS):
            mine, other = yg_in[i], cg_in[i]
            first = jnp.where(c == 0, mine, other)
            second = jnp.where(c == 0, other, mine)
            whole = jnp.concatenate([first, second[HALF - HALF_START :]], axis=0)
            if i < YS - 1:
                rel_ref[:, i * 384 : (i + 1) * 384] = whole
            else:
                rel_ref[:, i * 384 : REL] = whole[:, : REL - i * 384]
                flag_ref[0, 0] = jnp.max(whole[0:16, 256:384].astype(F32))

    def tile(t, k):
        return remote(
            stage.at[t, k], landed.at[t, me], tile_send.at[t, k], tile_recv.at[t, k], x_peers[k][1]
        )

    def scatter(t):
        for pair in range(XG // 2):
            both = (2 * pair + 1, (2 * pair + 2) % XG)
            row = iota((BLOCK, ALL), 0) + t * BLOCK
            which = jnp.concatenate(
                [hot(row + x_peers[k][0] * CAP == place_ref[...]) for k in both], axis=0
            )
            rows = mm(grads_ref[...], which, NT).astype(BF)
            for i, k in enumerate(both):
                part = rows[:, i * BLOCK : (i + 1) * BLOCK]
                if k == 0:
                    landed[t, me] = part
                else:
                    stage[t, k] = part
                    if t == TILES - 1:
                        tile(t, k).start()

    def send(t):
        for k in range(1, XG):
            tile(t, k).start()

    def arrive(t):
        for k in range(1, XG):
            s = lax.rem(me + XG - k, XG)
            remote(
                stage.at[t, k], landed.at[t, s], tile_send.at[t, k], tile_recv.at[t, k],
                x_peers[k][1],
            ).wait_recv()

    def partial(dist, half):
        q = DIST.index(dist)
        parts = [(t, s) for t in range(TILES_OF[q], TILES) for s in range(XG)]
        lhs = jnp.concatenate([landed[t, s] for t, s in parts], axis=1)
        key = (iota((BLOCK, 256), 1) // BLOCK + 2 * half) * 1024 + iota((BLOCK, 256), 0)
        which = jnp.concatenate(
            [hot(twice(codes_in[s, q : q + 1]) == key + t * BLOCK) for t, s in parts], axis=0
        )
        return mm(lhs, which)

    def ring(way, step, half):
        return remote(
            ring_out.at[way, step, half], ring_in.at[way, step, half],
            ring_send.at[way, step, half], ring_recv.at[way, step, half],
            right if way == 0 else left,
        )

    def has(way, step, half):
        return 0 < step or half == 1 - way

    def push(step, way):
        dist = 4 - step if way == 0 else (4 + step) % ZS
        order = (0, 1) if way == 0 else (1, 0)
        for half in order:
            if not has(way, step, half):
                continue
            value = partial(dist, half)
            if step > 0 and has(way, step - 1, half):
                ring(way, step - 1, half).wait_recv()
                value = value + ring_in[way, step - 1, half].astype(F32)
            ring_out[way, step, half] = value.astype(BF)
            ring(way, step, half).start()

    for way, half in legs(0):
        gring(way, 0, half).start()
    ids_ref[:, 0:EDGES] = head_ref[...]
    ids_ref[:, EDGES : 2 * EDGES] = tail_ref[...]
    ids_ref[:, 2 * EDGES :] = jnp.full((1, 2 * BLOCK), -1, I32)
    ids_ref[:, 2 * EDGES : 2 * EDGES + NEG] = ntail_ref[...]
    ids_ref[:, 2 * EDGES + BLOCK : 2 * EDGES + BLOCK + NEG] = nhead_ref[...]
    codes, places, overflow = plan_rows(ids_ref[...], owner_ref[...], block_ref[...], z)
    codes_mine[...] = codes.reshape(XG, 8, BLOCK)
    place_ref[...] = places
    for k in range(1, XG):
        ask(k).start()
    codes_in[me] = codes_mine[me]
    forward(0, (0,))
    relation_rows()
    forward(0, (1,))
    for k in range(1, XG):
        s = lax.rem(me + XG - k, XG)
        remote(
            codes_mine.at[s], codes_in.at[s], ask_send.at[k], ask_recv.at[k], x_peers[k][1]
        ).wait_recv()
    select(0, 0, 3, True)
    forward(1, (0,))
    select(1, 0, 3, False)
    forward(1, (1,))
    gather(0)
    select(2, 0, 3, False)
    forward(2, (0,))
    forward(2, (1,))
    select(1, 3, 6, True)
    select(2, 3, 6, False)
    forward(3)
    select(2, 6, 8, True)
    gather(1)
    gather(2)
    edges()

    scatter(2)
    relation_scatter(overflow)
    rel_core()
    scatter(1)
    rel_y()
    arrive(2)
    send(1)
    push(0, 0)
    push(0, 1)
    push(1, 1)
    scatter(0)
    rel_z()
    arrive(1)
    send(0)
    push(1, 0)
    rel_x()
    push(2, 1)
    rel_zg()
    push(2, 0)
    arrive(0)
    rel_yg()
    push(3, 1)
    push(3, 0)
    own = [partial(0, half) for half in range(2)]
    rel_cg()
    for half in range(2):
        lanes = slice(half * 256, (half + 1) * 256)
        ring(0, 3, half).wait_recv()
        ent_ref_a[:, lanes] = own[half] + ring_in[0, 3, half].astype(F32)
        ring(1, 3, half).wait_recv()
        ent_ref_b[:, lanes] = ring_in[1, 3, half]
    rel_end()

    for k in range(1, XG):
        ask(k).wait_send()
        for t in range(TILES):
            ftile(t, k).wait_send()
            tile(t, k).wait_send()
    core_copy().wait_send()
    cg_copy().wait_send()
    for k in range(1, YS):
        y_copy(k).wait_send()
        yg_copy(k).wait_send()
    for k in range(1, ZS):
        z_copy(k).wait_send()
        zg_copy(k).wait_send()
    for k in range(1, XS):
        x_copy(k).wait_send()
    for step in range(4):
        for way, half in legs(step):
            gring(way, step, half).wait_send()
        for way in range(2):
            for half in range(2):
                if has(way, step, half):
                    ring(way, step, half).wait_send()


def vmem():
    return pl.BlockSpec(memory_space=pltpu.VMEM)


def fast_step(ent, rel, owners, blocks, heads, rel_ids, tails, ntail, nhead):
    dma = pltpu.SemaphoreType.DMA
    v = pltpu.VMEM
    return pl.pallas_call(
        step_kernel,
        out_shape=(
            jax.ShapeDtypeStruct((WIDTH, 512), F32),
            jax.ShapeDtypeStruct((WIDTH, 512), BF),
            jax.ShapeDtypeStruct((WIDTH, REL), BF),
            jax.ShapeDtypeStruct((1, 1), F32),
        ),
        in_specs=[vmem()] * 9,
        out_specs=[vmem()] * 3 + [pl.BlockSpec(memory_space=pltpu.SMEM)],
        scratch_shapes=[
            v((ZS, 2, WIDTH, 256), BF),
            v((XG, 8, BLOCK), I32), v((XG, 8, BLOCK), I32),
            v((TILES, XG, WIDTH, BLOCK), BF), v((TILES, XG, WIDTH, BLOCK), BF),
            v((WIDTH, ALL), F32), v((1, ALL), I32), v((1, ALL), I32), v((WIDTH, ALL), BF),
            v((REL_PAD, EDGES), BF), v((WIDTH, REL_PAD), BF), v((WIDTH, REL_PAD), BF),
            v((WIDTH, EDGES), F32), v((WIDTH, EDGES), BF), v((2, WIDTH, BLOCK), F32),
            v((WIDTH, ALL), BF), v((WIDTH, REL_PAD), F32),
            v((TILES, XG, WIDTH, BLOCK), BF), v((TILES, XG, WIDTH, BLOCK), BF),
            v((2, 4, 2, WIDTH, 256), BF), v((2, 4, 2, WIDTH, 256), BF),
            v((HALF, REL_PAD), BF), v((HALF, REL_PAD), BF),
            v((YS, HALF, 384), BF), v((YS, HALF, 384), BF),
            v((ZS, 32, 384), BF), v((ZS, 32, 384), BF),
            v((32, 384), F32), v((XS, 32, 384), F32),
            v((32, 384), BF), v((ZS, 32, 384), BF),
            v((HALF, 384), BF), v((YS, HALF, 384), BF), v((YS, HALF, 384), BF),
            v((HALF, REL_PAD), F32), v((256, 384), F32),
            dma((2, 4, 2)), dma((2, 4, 2)), dma((XG,)), dma((XG,)),
            dma((TILES, XG)), dma((TILES, XG)),
            dma((TILES, XG)), dma((TILES, XG)), dma((2, 4, 2)), dma((2, 4, 2)),
            dma, dma, dma((YS,)), dma((YS,)), dma((ZS,)), dma((ZS,)), dma((XS,)), dma((XS,)),
            dma((ZS,)), dma((ZS,)), dma((YS,)), dma((YS,)), dma, dma,
        ],
        compiler_params=pltpu.CompilerParams(
            collective_id=0, has_side_effects=True, vmem_limit_bytes=60 * MIB
        ),
        name="step",
    )(ent, rel, owners, blocks, heads, rel_ids, tails, ntail, nhead)


def sum_everywhere(part):
    rows = part.shape[0]
    for axis in ("row", "bucket"):
        count = lax.axis_size(axis)
        each = -(-rows // count)
        padded = jnp.pad(part, ((0, each * count - rows), (0, 0)))
        pieces = lax.all_to_all(padded, axis, split_axis=0, concat_axis=0, tiled=True)
        piece = jnp.sum(pieces.reshape(count, each, -1), axis=0)
        copies = jnp.tile(piece, (count, 1))
        part = lax.all_to_all(copies, axis, split_axis=0, concat_axis=0, tiled=True)[:rows]
    return part


def side_weights(positive, scores):
    largest = jnp.maximum(positive, jnp.max(scores, axis=1))
    own_term = jnp.exp(positive - largest)
    others = jnp.exp(scores - largest[:, None])
    total = own_term + jnp.sum(others, axis=1)
    return (own_term / total - 1.0, others / total[:, None])


def edge_block_grads(buffer, relations, head_ids, rel_ids, tail_ids, neg_tail, neg_head):
    middle = relations.shape[1] // 2
    head_rows = jnp.take(buffer, head_ids, axis=0).astype(jnp.float32)
    tail_rows = jnp.take(buffer, tail_ids, axis=0).astype(jnp.float32)
    rel_rows = jnp.take(relations, rel_ids, axis=0)
    rel_real, rel_imag = (rel_rows[:, :middle], rel_rows[:, middle:])
    head_real, head_imag = (head_rows[:, :middle], head_rows[:, middle:])
    tail_real, tail_imag = (tail_rows[:, :middle], tail_rows[:, middle:])
    query = jnp.concatenate(
        [head_real * rel_real - head_imag * rel_imag, head_real * rel_imag + head_imag * rel_real],
        axis=1,
    )
    probe = jnp.concatenate(
        [rel_real * tail_real + rel_imag * tail_imag, rel_real * tail_imag - rel_imag * tail_real],
        axis=1,
    )
    positive = jnp.sum(query * tail_rows, axis=1)
    tail_negs = jnp.take(buffer, neg_tail, axis=0)
    head_negs = jnp.take(buffer, neg_head, axis=0)
    query_low = query.astype(jnp.bfloat16)
    probe_low = probe.astype(jnp.bfloat16)
    contract_last = (((1,), (1,)), ((), ()))
    contract_first = (((0,), (0,)), ((), ()))
    tail_scores = lax.dot_general(
        query_low, tail_negs, contract_last, preferred_element_type=jnp.float32
    )
    head_scores = lax.dot_general(
        probe_low, head_negs, contract_last, preferred_element_type=jnp.float32
    )
    tail_coef, tail_weights = side_weights(positive, tail_scores)
    head_coef, head_weights = side_weights(positive, head_scores)
    tail_low = tail_weights.astype(jnp.bfloat16)
    head_low = head_weights.astype(jnp.bfloat16)
    both_coef = (tail_coef + head_coef)[:, None]
    query_grad = both_coef * tail_rows + jnp.dot(
        tail_low, tail_negs, preferred_element_type=jnp.float32
    )
    probe_grad = jnp.dot(head_low, head_negs, preferred_element_type=jnp.float32)
    tail_neg_grad = lax.dot_general(
        tail_low, query_low, contract_first, preferred_element_type=jnp.float32
    )
    head_neg_grad = lax.dot_general(
        head_low, probe_low, contract_first, preferred_element_type=jnp.float32
    )
    qgrad_real, qgrad_imag = (query_grad[:, :middle], query_grad[:, middle:])
    pgrad_real, pgrad_imag = (probe_grad[:, :middle], probe_grad[:, middle:])
    head_grad = jnp.concatenate(
        [
            qgrad_real * rel_real + qgrad_imag * rel_imag,
            qgrad_imag * rel_real - qgrad_real * rel_imag,
        ],
        axis=1,
    )
    tail_grad = both_coef * query + jnp.concatenate(
        [
            pgrad_real * rel_real - pgrad_imag * rel_imag,
            pgrad_real * rel_imag + pgrad_imag * rel_real,
        ],
        axis=1,
    )
    rel_edge_grad = jnp.concatenate(
        [
            qgrad_real * head_real
            + qgrad_imag * head_imag
            + pgrad_real * tail_real
            + pgrad_imag * tail_imag,
            qgrad_imag * head_real
            - qgrad_real * head_imag
            + pgrad_real * tail_imag
            - pgrad_imag * tail_real,
        ],
        axis=1,
    )
    row_ids = jnp.concatenate([head_ids, tail_ids, neg_tail, neg_head])
    row_vals = jnp.concatenate([head_grad, tail_grad, tail_neg_grad, head_neg_grad], axis=0)
    return (row_ids, row_vals, rel_edge_grad)


def device_grads(buffer, relations, head_ids, rel_ids, tail_ids, neg_tail, neg_head):
    blocks_count = neg_tail.shape[0]
    start_zero = (jnp.zeros(buffer.shape, jnp.float32), jnp.zeros(relations.shape, jnp.float32))

    def advance(totals, position):
        row_ids, row_vals, rel_edge_grad = edge_block_grads(
            buffer, relations, head_ids, rel_ids, tail_ids, neg_tail[position], neg_head[position]
        )
        return (
            (totals[0].at[row_ids].add(row_vals), totals[1].at[rel_ids].add(rel_edge_grad)),
            None,
        )

    totals, unused = lax.scan(advance, start_zero, jnp.arange(blocks_count, dtype=jnp.int32))
    return totals


def dense_step(
    entities, relations, touch_owner, touch_block, head_ids, rel_ids, tail_ids, neg_tail, neg_head
):
    bucket_count = lax.axis_size("bucket")
    block_rows = BLOCK
    width = entities.shape[1]
    owned = entities.shape[0] // block_rows
    owners = touch_owner[0]
    wanted = touch_block[0]
    touched = owners.shape[0]
    slot_ids = jnp.arange(bucket_count, dtype=jnp.int32)
    matches = owners[:, None] == slot_ids[None, :]
    request = jnp.sum(jnp.where(matches, wanted[:, None] + 1, 0), axis=0) - 1
    incoming = lax.all_to_all(request, "bucket", split_axis=0, concat_axis=0, tiled=True)
    selector = (incoming[:, None] == jnp.arange(owned, dtype=jnp.int32)[None, :]).astype(
        jnp.float32
    )
    owned_flat = entities.reshape(owned, block_rows * width)
    reply = jnp.dot(selector, owned_flat, precision=lax.Precision.HIGHEST).astype(jnp.bfloat16)
    reply = reply.reshape(bucket_count, block_rows, width)
    fetched = lax.all_to_all(reply, "bucket", split_axis=0, concat_axis=0, tiled=True)
    buffer = jnp.take(fetched, owners, axis=0).reshape(touched * block_rows, width)
    buffer_grad, rel_part = device_grads(
        buffer, relations, head_ids, rel_ids, tail_ids, neg_tail, neg_head
    )
    outgoing = jnp.zeros((bucket_count, block_rows, width), jnp.float32)
    outgoing = outgoing.at[owners].set(buffer_grad.reshape(touched, block_rows, width))
    returned = lax.all_to_all(outgoing, "bucket", split_axis=0, concat_axis=0, tiled=True)
    entity_grad = lax.dot_general(
        selector,
        returned.reshape(bucket_count, block_rows * width),
        (((0,), (0,)), ((), ())),
        precision=lax.Precision.HIGHEST,
    )
    entity_grad = entity_grad.reshape(owned * block_rows, width)
    relation_grad = sum_everywhere(rel_part)
    return (entity_grad, relation_grad)


def per_device(
    entities, relations, touch_owner, touch_block, head_ids, rel_ids, tail_ids, neg_tail, neg_head
):
    ent_a, ent_b, rel, over = fast_step(
        entities.T, relations.T, touch_owner, touch_block,
        head_ids[None, :], rel_ids[None, :], tail_ids[None, :], neg_tail, neg_head,
    )
    return lax.cond(
        over[0, 0] > 0.5,
        lambda: dense_step(
            entities, relations, touch_owner, touch_block, head_ids, rel_ids, tail_ids,
            neg_tail, neg_head,
        ),
        lambda: ((ent_a + ent_b.astype(F32)).T, rel.astype(F32).T),
    )


def solution(mesh):
    return jax.shard_map(
        per_device,
        mesh=mesh,
        in_specs=(
            P(("bucket", "row"), None),
            P(),
            P(("bucket", "row"), None),
            P(("bucket", "row"), None),
            P(("bucket", "row")),
            P(("bucket", "row")),
            P(("bucket", "row")),
            P(("bucket", "row"), None),
            P(("bucket", "row"), None),
        ),
        out_specs=(P(("bucket", "row"), None), P()),
        check_vma=False,
    )
```

```python
import functools

import jax
import jax.numpy as jnp
from jax import lax
from jax.experimental import pallas as pl
from jax.experimental.pallas import tpu as pltpu
from jax.sharding import PartitionSpec as P

BLOCK = 128
WIDTH = 400
EDGES = 1024
NEG = 100
REL = 1300
REL_PAD = 1536
ALL = 2 * EDGES + 2 * BLOCK
XS, ZS, CS, YS = 4, 8, 2, 4
XG = XS * CS
TILES = 3
CAP = TILES * BLOCK
DIST = (0, 1, 7, 2, 6, 3, 5, 4)
FIRST_OF_TILE = (3, 6, 8)
TILES_OF = (0, 0, 0, 1, 1, 1, 2, 2)
HELD = ()
HALF = 208
HALF_START = 192
BF = jnp.bfloat16
F32 = jnp.float32
I32 = jnp.int32
NT = (((1,), (1,)), ((), ()))
TN = (((0,), (0,)), ((), ()))
MIB = 1024 * 1024


def mm(a, b, dims=(((1,), (0,)), ((), ()))):
    return lax.dot_general(a, b, dims, preferred_element_type=F32)


def iota(shape, dim):
    return lax.broadcasted_iota(I32, shape, dim)


def hot(mask):
    return jnp.where(mask, 1.0, 0.0).astype(BF)


def place():
    b = lax.axis_index("bucket")
    return b // (ZS * CS), (b // CS) % ZS, b % CS, lax.axis_index("row")


def bucket_of(x, z, c):
    return (x * ZS + z) * CS + c


def x_peer(x, z, c, k):
    s = lax.rem(x * CS + c + k, XG)
    return s, {"bucket": bucket_of(s // CS, z, s % CS)}


def z_peer(x, z, c, k):
    other = lax.rem(z + k, ZS)
    return other, {"bucket": bucket_of(x, other, c)}


def greet(peers):
    for peer in peers:
        pl.semaphore_signal(
            pltpu.get_barrier_semaphore(), inc=1, device_id=peer,
            device_id_type=pl.DeviceIdType.MESH,
        )


def remote(src, dst, send, recv, peer):
    return pltpu.make_async_remote_copy(
        src_ref=src, dst_ref=dst, send_sem=send, recv_sem=recv,
        device_id=peer, device_id_type=pl.DeviceIdType.MESH,
    )


def plan_rows(ids, owners, blocks, z):
    slot = lax.shift_right_arithmetic(ids, 7)
    row = jnp.bitwise_and(ids, 127)
    slot_hot = hot(iota((64, ALL), 0) == slot)
    row_is = iota((BLOCK, ALL), 0) == row
    row_hot = hot(row_is)
    count = mm(slot_hot, row_hot, NT)
    wanted_slot = hot(count > 0.5)
    j = iota((64, 64), 0)
    s, q = j // 8, j % 8
    dist = jnp.where(q % 2 == 1, (q + 1) // 2, (8 - q // 2) % 8)
    target = bucket_of(s // CS, (z + dist) % ZS, s % CS)
    perm_is = owners == target
    perm = hot(perm_is)
    wanted = mm(perm, wanted_slot)
    block = jnp.sum(jnp.where(perm_is, blocks, 0), axis=1, keepdims=True)
    wanted_low = wanted.astype(BF)
    before = mm(wanted_low, hot(iota((BLOCK, BLOCK), 0) < iota((BLOCK, BLOCK), 1)))
    number = mm(wanted_low, jnp.ones((BLOCK, BLOCK), BF)).astype(BF)
    jj = iota((64, 64), 1)
    same = s == jj // 8
    qq = jj % 8

    def tile_of(position):
        return jnp.where(position < 3, 0, jnp.where(position < 6, 1, 2))

    lead = mm(hot(same & (tile_of(q) == tile_of(qq)) & (qq < q)), number)
    sums = [mm(hot(same & (tile_of(qq) == t)), number) for t in range(TILES)]
    start1 = jnp.maximum(float(BLOCK), sums[0])
    start2 = jnp.maximum(float(2 * BLOCK), start1 + sums[1])
    end = start2 + sums[2]
    q_wide = iota((64, BLOCK), 0) % 8
    start = jnp.where(q_wide < 3, 0.0, jnp.where(q_wide < 6, start1, start2))
    rank = (start + lead + before).astype(I32)
    codes = jnp.where(wanted > 0.5, block * 1024 + rank, -1)
    overflow = jnp.max(jnp.where(end > float(CAP), 1.0, 0.0))
    position = (iota((64, BLOCK), 0) // 8) * CAP + rank
    high = lax.shift_right_arithmetic(position, 7).astype(F32).astype(BF)
    low = jnp.bitwise_and(position, 127).astype(F32).astype(BF)
    high_slot = mm(perm, high, TN).astype(BF)
    low_slot = mm(perm, low, TN).astype(BF)
    high_ids = mm(high_slot, slot_hot, TN)
    low_ids = mm(low_slot, slot_hot, TN)
    value = jnp.sum(jnp.where(row_is, high_ids * 128.0 + low_ids, 0.0), axis=0, keepdims=True)
    places = jnp.where(slot >= 0, value.astype(I32), -1)
    return codes, places, overflow


def twice(row):
    return jnp.concatenate([row, row], axis=1)


def side(positive, scores, valid):
    largest = jnp.maximum(
        positive, jnp.max(jnp.where(valid, scores, -3e38), axis=0, keepdims=True)
    )
    own = jnp.exp(positive - largest)
    others = jnp.where(valid, jnp.exp(scores - largest), 0.0)
    total = own + jnp.sum(others, axis=0, keepdims=True)
    return own / total - 1.0, others / total


def step_kernel(
    ent_ref, rel_in_ref, owner_ref, block_ref, head_ref, rel_ids_ref, tail_ref, ntail_ref, nhead_ref,
    ent_ref_a, ent_ref_b, rel_ref, flag_ref,
    tables, codes_mine, codes_in, fstage, flanded, total, ids_ref, place_ref, rows_ref,
    hot_rel, high, low, relation, edge_rel, neg_sum, grads_ref, relg_ref,
    stage, landed, ring_out, ring_in,
    core_out, core_in, y_out, y_in, x_out, x_in, z_in, zg_out, zg_in, xg_out, xg_in, yg_out, yg_in, cg_in,
    sum_core, sum_y, sum_x, over_ref, ent_in, rel_in,
    gring_send, gring_recv, ask_send, ask_recv, ftile_send, ftile_recv,
    tile_send, tile_recv, ring_send, ring_recv,
    core_send, core_recv, y_send, y_recv, z_send, z_recv, x_send, x_recv,
    zg_send, zg_recv, xg_send, xg_recv, yg_send, yg_recv, cg_send, cg_recv, in_sem,
):
    x, z, c, y = place()
    me = x * CS + c
    z_peers = [z_peer(x, z, c, k) for k in range(ZS)]
    x_peers = [x_peer(x, z, c, k) for k in range(XG)]
    y_peers = [(lax.rem(y + k, YS), {"row": lax.rem(y + k, YS)}) for k in range(YS)]
    same_core = [
        (lax.rem(x + k, XS), {"bucket": bucket_of(lax.rem(x + k, XS), z, c)}) for k in range(XS)
    ]
    mate = {"bucket": bucket_of(x, z, 1 - c)}
    right, left = z_peers[1][1], z_peers[ZS - 1][1]
    mid = WIDTH // 2
    pending = []

    def go(copy):
        copy.start()
        pending.append(copy)

    everyone = [p for _, p in z_peers[1:]] + [p for _, p in x_peers[1:]] + [p for _, p in y_peers[1:]]
    greet(everyone)

    def load(half):
        lanes = pl.ds(half * 256, 256)
        return pltpu.make_async_copy(ent_ref.at[:, lanes], ent_in.at[:, lanes], in_sem.at[half])

    rel_load = pltpu.make_async_copy(rel_in_ref, rel_in, in_sem.at[2])
    load(0).start()
    load(1).start()
    rel_load.start()
    load(0).wait()
    tables[0, 0] = ent_in[:, 0:256].astype(BF)
    pl.semaphore_wait(pltpu.get_barrier_semaphore(), len(everyone))

    def gring(way, step, half):
        if way == 0:
            src, dst = (-step) % ZS, (-step - 1) % ZS
        else:
            src, dst = step, step + 1
        return remote(
            tables.at[src, half], tables.at[dst, half],
            gring_send.at[way, step, half], gring_recv.at[way, step, half],
            right if way == 0 else left,
        )

    def legs(step):
        if step < 3:
            return [(0, 0), (1, 0), (0, 1), (1, 1)]
        return [(0, 1), (1, 0)]

    def forward(step, halves=(0, 1)):
        for way, half in legs(step):
            if half not in halves:
                continue
            gring(way, step, half).wait_recv()
            if step < 3 and (way, half) in legs(step + 1):
                go(gring(way, step + 1, half))

    def ask(k):
        s, peer = x_peers[k]
        return remote(codes_mine.at[s], codes_in.at[me], ask_send.at[k], ask_recv.at[k], peer)

    def ftile(t, k):
        return remote(
            fstage.at[t, k], flanded.at[t, me], ftile_send.at[t, k], ftile_recv.at[t, k],
            x_peers[k][1],
        )

    def select(t, first, last, send):
        parts = [(q, half) for q in range(first, last) for half in range(2)]
        lhs = jnp.concatenate([tables[DIST[q], half] for q, half in parts], axis=1)
        key = (iota((BLOCK, 256), 1) // BLOCK) * 1024 + iota((BLOCK, 256), 0) + t * BLOCK
        for pair in range(XG // 2):
            both = (2 * pair + 1, (2 * pair + 2) % XG)
            chosen = []
            for k in both:
                code = codes_in[x_peers[k][0]]
                chosen.append(
                    jnp.concatenate(
                        [hot(twice(code[q : q + 1]) == key + 2048 * half) for q, half in parts],
                        axis=1,
                    )
                )
            rows = mm(lhs, jnp.concatenate(chosen, axis=0), NT).astype(BF)
            for i, k in enumerate(both):
                part = rows[:, i * BLOCK : (i + 1) * BLOCK]
                if first > 0:
                    part = part + fstage[t, k]
                if send and k == 0:
                    flanded[t, me] = part
                else:
                    fstage[t, k] = part
                    if send:
                        go(ftile(t, k))

    def gather(t):
        for k in range(1, XG):
            s = lax.rem(me + XG - k, XG)
            remote(
                fstage.at[t, k], flanded.at[t, s], ftile_send.at[t, k], ftile_recv.at[t, k],
                x_peers[k][1],
            ).wait_recv()
        key = iota((XG * BLOCK, 256), 0)
        key = (key // BLOCK) * CAP + key % BLOCK + t * BLOCK

        def chunk(i, carry):
            lanes = pl.ds(pl.multiple_of(i * 256, 256), 256)
            lhs = jnp.concatenate([flanded[t, s] for s in range(XG)], axis=1)
            rows = mm(lhs, hot(key == place_ref[:, lanes]))
            if t == 0:
                total[:, lanes] = rows
            elif t < TILES - 1:
                total[:, lanes] += rows
            else:
                rows_ref[:, lanes] = (total[:, lanes] + rows).astype(BF)
            return carry

        lax.fori_loop(0, ALL // 256, chunk, 0)

    def relation_rows():
        high[...] = jnp.zeros_like(high)
        low[...] = jnp.zeros_like(low)
        rel_load.wait()
        rel = rel_in[...]
        rel_high = rel.astype(BF)
        high[:, 0:REL] = rel_high
        low[:, 0:REL] = (rel - rel_high.astype(F32)).astype(BF)

        def chunk(i, carry):
            lanes = pl.ds(pl.multiple_of(i * 256, 256), 256)
            which = hot(iota((REL_PAD, 256), 0) == rel_ids_ref[:, lanes])
            hot_rel[:, lanes] = which
            relation[:, lanes] = mm(high[...], which) + mm(low[...], which)
            return carry

        lax.fori_loop(0, EDGES // 256, chunk, 0)

    def edges():
        neg_sum[...] = jnp.zeros_like(neg_sum)
        step = 256

        def chunk(i, carry):
            lanes = pl.ds(pl.multiple_of(i * step, step), step)
            tail_lanes = pl.ds(pl.multiple_of(EDGES + i * step, step), step)
            a, b = relation[0:mid, lanes], relation[mid:WIDTH, lanes]
            head = rows_ref[:, lanes].astype(F32)
            tail = rows_ref[:, tail_lanes].astype(F32)
            hr, hi = head[:mid], head[mid:]
            tr, ti = tail[:mid], tail[mid:]
            query = jnp.concatenate([hr * a - hi * b, hr * b + hi * a], axis=0)
            probe = jnp.concatenate([a * tr + b * ti, a * ti - b * tr], axis=0)
            positive = jnp.sum(query * tail, axis=0, keepdims=True)
            query_low, probe_low = query.astype(BF), probe.astype(BF)
            tail_neg = rows_ref[:, 2 * EDGES : 2 * EDGES + BLOCK]
            head_neg = rows_ref[:, 2 * EDGES + BLOCK : 2 * EDGES + 2 * BLOCK]
            valid = iota((BLOCK, step), 0) < NEG
            tail_coef, tail_weights = side(positive, mm(tail_neg, query_low, TN), valid)
            head_coef, head_weights = side(positive, mm(head_neg, probe_low, TN), valid)
            tail_low, head_low = tail_weights.astype(BF), head_weights.astype(BF)
            both = tail_coef + head_coef
            qg = both * tail + mm(tail_neg, tail_low)
            pg = mm(head_neg, head_low)
            neg_sum[0] += mm(query_low, tail_low, NT)
            neg_sum[1] += mm(probe_low, head_low, NT)
            qr, qi = qg[:mid], qg[mid:]
            pr, pi = pg[:mid], pg[mid:]
            grads_ref[:, lanes] = jnp.concatenate(
                [qr * a + qi * b, qi * a - qr * b], axis=0
            ).astype(BF)
            grads_ref[:, tail_lanes] = (
                both * query + jnp.concatenate([pr * a - pi * b, pr * b + pi * a], axis=0)
            ).astype(BF)
            edge_rel[:, lanes] = jnp.concatenate(
                [
                    qr * hr + qi * hi + pr * tr + pi * ti,
                    qi * hr - qr * hi + pr * ti - pi * tr,
                ],
                axis=0,
            ).astype(BF)
            return carry

        lax.fori_loop(0, EDGES // step, chunk, 0)
        grads_ref[:, 2 * EDGES : 2 * EDGES + BLOCK] = neg_sum[0].astype(BF)
        grads_ref[:, 2 * EDGES + BLOCK : 2 * EDGES + 2 * BLOCK] = neg_sum[1].astype(BF)

    def relation_scatter():
        def chunk(i, carry):
            lanes = pl.ds(pl.multiple_of(i * 256, 256), 256)
            relg_ref[:, lanes] = mm(edge_rel[...], hot_rel[lanes, :], NT)
            return carry

        lax.fori_loop(0, REL_PAD // 256, chunk, 0)
        relg_ref[:, REL_PAD - BLOCK :] = jnp.zeros((WIDTH, BLOCK), F32) + over_ref[0:1, :]

    def core_copy():
        return remote(core_out, core_in, core_send, core_recv, mate)

    def rel_core():
        core_out[...] = relg_ref[pl.ds(pl.multiple_of((1 - c) * HALF_START, 16), HALF), :].astype(BF)
        go(core_copy())

    def y_copy(k):
        return remote(y_out.at[k], y_in.at[k], y_send.at[k], y_recv.at[k], y_peers[k][1])

    def rel_y():
        core_copy().wait_recv()
        mine = pl.ds(pl.multiple_of(c * HALF_START, 16), HALF)
        sum_core[...] = relg_ref[mine, :] + core_in[...].astype(F32)
        for k in range(1, YS):
            other = y_peers[k][0]
            y_out[k] = sum_core[:, pl.ds(pl.multiple_of(other * 384, 128), 384)].astype(BF)
            go(y_copy(k))

    def x_copy(k):
        return remote(x_out.at[k], x_in.at[k], x_send.at[k], x_recv.at[k], same_core[k][1])

    def rel_x():
        for k in range(1, YS):
            y_copy(k).wait_recv()
        summed = sum_core[:, pl.ds(pl.multiple_of(y * 384, 128), 384)]
        for k in range(1, YS):
            summed = summed + y_in[k].astype(F32)
        sum_y[HALF:, :] = jnp.zeros((256 - HALF, 384), F32)
        sum_y[0:HALF, :] = summed
        for k in range(1, XS):
            other = same_core[k][0]
            x_out[k] = sum_y[pl.ds(pl.multiple_of(other * 64, 64), 64), :].astype(BF)
            go(x_copy(k))

    def z_copy(k):
        return remote(
            sum_x.at[pl.ds(pl.multiple_of(z_peers[k][0] * 8, 8), 8)], z_in.at[k],
            z_send.at[k], z_recv.at[k], z_peers[k][1],
        )

    def rel_z():
        for k in range(1, XS):
            x_copy(k).wait_recv()
        summed = sum_y[pl.ds(pl.multiple_of(x * 64, 64), 64), :]
        for k in range(1, XS):
            summed = summed + x_in[k].astype(F32)
        sum_x[...] = summed
        for k in range(1, ZS):
            go(z_copy(k))

    def zg_copy(k):
        return remote(zg_out, zg_in.at[z], zg_send.at[k], zg_recv.at[k], z_peers[k][1])

    def rel_zg():
        for k in range(1, ZS):
            z_copy(k).wait_recv()
        summed = sum_x[pl.ds(pl.multiple_of(z * 8, 8), 8), :]
        for k in range(1, ZS):
            summed = summed + z_in[k]
        zg_out[...] = summed
        zg_in[z] = summed
        for k in range(1, ZS):
            go(zg_copy(k))

    def xg_copy(k):
        return remote(xg_out, xg_in.at[x], xg_send.at[k], xg_recv.at[k], same_core[k][1])

    def rel_xg():
        for k in range(1, ZS):
            s = lax.rem(z + ZS - k, ZS)
            remote(zg_out, zg_in.at[s], zg_send.at[k], zg_recv.at[k], z_peers[k][1]).wait_recv()
        whole = jnp.concatenate([zg_in[i] for i in range(ZS)], axis=0).astype(BF)
        xg_out[...] = whole
        xg_in[x] = whole
        for k in range(1, XS):
            go(xg_copy(k))

    def yg_copy(k):
        return remote(yg_out, yg_in.at[y], yg_send.at[k], yg_recv.at[k], y_peers[k][1])

    def rel_yg():
        for k in range(1, XS):
            s = lax.rem(x + XS - k, XS)
            remote(xg_out, xg_in.at[s], xg_send.at[k], xg_recv.at[k], same_core[k][1]).wait_recv()
        whole = jnp.concatenate([xg_in[i] for i in range(XS)], axis=0)[0:HALF]
        yg_out[...] = whole
        yg_in[y] = whole
        for k in range(1, YS):
            go(yg_copy(k))

    def cg_copy():
        return remote(yg_in, cg_in, cg_send, cg_recv, mate)

    def rel_cg():
        for k in range(1, YS):
            s = lax.rem(y + YS - k, YS)
            remote(yg_out, yg_in.at[s], yg_send.at[k], yg_recv.at[k], y_peers[k][1]).wait_recv()
        go(cg_copy())

    def rel_end():
        cg_copy().wait_recv()
        for i in range(YS):
            mine, other = yg_in[i], cg_in[i]
            first = jnp.where(c == 0, mine, other)
            second = jnp.where(c == 0, other, mine)
            whole = jnp.concatenate([first, second[HALF - HALF_START :]], axis=0)
            if i < YS - 1:
                rel_ref[:, i * 384 : (i + 1) * 384] = whole
            else:
                rel_ref[:, i * 384 : REL] = whole[:, : REL - i * 384]
                flag_ref[0, 0] = jnp.max(whole[0:16, 256:384].astype(F32))

    def tile(t, k):
        return remote(
            stage.at[t, k], landed.at[t, me], tile_send.at[t, k], tile_recv.at[t, k], x_peers[k][1]
        )

    def scatter(t):
        for pair in range(XG // 2):
            both = (2 * pair + 1, (2 * pair + 2) % XG)
            row = iota((BLOCK, ALL), 0) + t * BLOCK
            which = jnp.concatenate(
                [hot(row + x_peers[k][0] * CAP == place_ref[...]) for k in both], axis=0
            )
            rows = mm(grads_ref[...], which, NT).astype(BF)
            for i, k in enumerate(both):
                part = rows[:, i * BLOCK : (i + 1) * BLOCK]
                if k == 0:
                    landed[t, me] = part
                else:
                    stage[t, k] = part
                    if t not in HELD:
                        go(tile(t, k))

    def send(t):
        for k in range(1, XG):
            go(tile(t, k))

    def arrive(t):
        for k in range(1, XG):
            s = lax.rem(me + XG - k, XG)
            remote(
                stage.at[t, k], landed.at[t, s], tile_send.at[t, k], tile_recv.at[t, k],
                x_peers[k][1],
            ).wait_recv()

    def partial(dist, half):
        q = DIST.index(dist)
        parts = [(t, s) for t in range(TILES_OF[q], TILES) for s in range(XG)]
        lhs = jnp.concatenate([landed[t, s] for t, s in parts], axis=1)
        key = (iota((BLOCK, 256), 1) // BLOCK + 2 * half) * 1024 + iota((BLOCK, 256), 0)
        which = jnp.concatenate(
            [hot(twice(codes_in[s, q : q + 1]) == key + t * BLOCK) for t, s in parts], axis=0
        )
        return mm(lhs, which)

    def ring(way, step, half):
        return remote(
            ring_out.at[way, step, half], ring_in.at[way, step, half],
            ring_send.at[way, step, half], ring_recv.at[way, step, half],
            right if way == 0 else left,
        )

    def has(way, step, half):
        return 0 < step or half == 1 - way

    def push(step, way):
        dist = 4 - step if way == 0 else (4 + step) % ZS
        order = (0, 1) if way == 0 else (1, 0)
        for half in order:
            if not has(way, step, half):
                continue
            value = partial(dist, half)
            if step > 0 and has(way, step - 1, half):
                ring(way, step - 1, half).wait_recv()
                value = value + ring_in[way, step - 1, half].astype(F32)
            ring_out[way, step, half] = value.astype(BF)
            go(ring(way, step, half))

    def begin():
        for way in range(2):
            go(gring(way, 0, 0))
        load(1).wait()
        tables[0, 1] = ent_in[:, 256:512].astype(BF)
        for way in range(2):
            go(gring(way, 0, 1))

    def plan():
        ids_ref[:, 0:EDGES] = head_ref[...]
        ids_ref[:, EDGES : 2 * EDGES] = tail_ref[...]
        ids_ref[:, 2 * EDGES :] = jnp.full((1, 2 * BLOCK), -1, I32)
        ids_ref[:, 2 * EDGES : 2 * EDGES + NEG] = ntail_ref[...]
        ids_ref[:, 2 * EDGES + BLOCK : 2 * EDGES + BLOCK + NEG] = nhead_ref[...]
        codes, places, overflow = plan_rows(ids_ref[...], owner_ref[...], block_ref[...], z)
        codes_mine[...] = codes.reshape(XG, 8, BLOCK)
        place_ref[...] = places
        over_ref[...] = jnp.zeros((8, BLOCK), F32) + overflow
        for k in range(1, XG):
            go(ask(k))
        codes_in[me] = codes_mine[me]

    def asked():
        for k in range(1, XG):
            s = lax.rem(me + XG - k, XG)
            remote(
                codes_mine.at[s], codes_in.at[s], ask_send.at[k], ask_recv.at[k], x_peers[k][1]
            ).wait_recv()

    def finish():
        for half in range(2):
            lanes = slice(half * 256, (half + 1) * 256)
            own = partial(0, half)
            ring(0, 3, half).wait_recv()
            ent_ref_a[:, lanes] = own + ring_in[0, 3, half].astype(F32)
            ring(1, 3, half).wait_recv()
            ent_ref_b[:, lanes] = ring_in[1, 3, half]

    order = [
        (begin,), (plan,), (forward, 0, (0,)), (relation_rows,), (forward, 0, (1,)), (asked,),
        (select, 0, 0, 3, True), (forward, 1, (0,)), (select, 1, 0, 3, False),
        (forward, 1, (1,)), (select, 2, 0, 3, False), (forward, 2, (0,)), (gather, 0),
        (forward, 2, (1,)), (select, 1, 3, 6, True), (select, 2, 3, 6, False), (forward, 3),
        (select, 2, 6, 8, True), (gather, 1), (gather, 2), (edges,),
        (scatter, 2), (relation_scatter,), (rel_core,), (scatter, 1), (rel_y,), (scatter, 0),
        (arrive, 2), (push, 0, 0), (push, 0, 1), (push, 1, 1), (rel_x,),
        (arrive, 1), (push, 1, 0), (rel_z,), (push, 2, 1), (rel_zg,), (push, 2, 0), (rel_xg,),
        (arrive, 0), (push, 3, 1), (rel_yg,), (push, 3, 0), (rel_cg,), (finish,), (rel_end,),
    ]
    for function, *values in order:
        function(*values)
    for copy in pending:
        copy.wait_send()


def vmem():
    return pl.BlockSpec(memory_space=pltpu.VMEM)


def fast_step(ent, rel, owners, blocks, heads, rel_ids, tails, ntail, nhead):
    dma = pltpu.SemaphoreType.DMA
    v = pltpu.VMEM
    return pl.pallas_call(
        step_kernel,
        out_shape=(
            jax.ShapeDtypeStruct((WIDTH, 512), F32),
            jax.ShapeDtypeStruct((WIDTH, 512), BF),
            jax.ShapeDtypeStruct((WIDTH, REL), BF),
            jax.ShapeDtypeStruct((1, 1), F32),
        ),
        in_specs=[pl.BlockSpec(memory_space=pl.ANY)] * 2 + [vmem()] * 7,
        out_specs=[vmem()] * 3 + [pl.BlockSpec(memory_space=pltpu.SMEM)],
        scratch_shapes=[
            v((ZS, 2, WIDTH, 256), BF),
            v((XG, 8, BLOCK), I32), v((XG, 8, BLOCK), I32),
            v((TILES, XG, WIDTH, BLOCK), BF), v((TILES, XG, WIDTH, BLOCK), BF),
            v((WIDTH, ALL), F32), v((1, ALL), I32), v((1, ALL), I32), v((WIDTH, ALL), BF),
            v((REL_PAD, EDGES), BF), v((WIDTH, REL_PAD), BF), v((WIDTH, REL_PAD), BF),
            v((WIDTH, EDGES), F32), v((WIDTH, EDGES), BF), v((2, WIDTH, BLOCK), F32),
            v((WIDTH, ALL), BF), v((WIDTH, REL_PAD), F32),
            v((TILES, XG, WIDTH, BLOCK), BF), v((TILES, XG, WIDTH, BLOCK), BF),
            v((2, 4, 2, WIDTH, 256), BF), v((2, 4, 2, WIDTH, 256), BF),
            v((HALF, REL_PAD), BF), v((HALF, REL_PAD), BF),
            v((YS, HALF, 384), BF), v((YS, HALF, 384), BF),
            v((XS, 64, 384), BF), v((XS, 64, 384), BF),
            v((ZS, 8, 384), F32), v((8, 384), F32), v((ZS, 8, 384), F32),
            v((64, 384), BF), v((XS, 64, 384), BF),
            v((HALF, 384), BF), v((YS, HALF, 384), BF), v((YS, HALF, 384), BF),
            v((HALF, REL_PAD), F32), v((256, 384), F32), v((64, 384), F32), v((8, BLOCK), F32),
            v((WIDTH, 512), F32), v((WIDTH, REL), F32),
            dma((2, 4, 2)), dma((2, 4, 2)), dma((XG,)), dma((XG,)),
            dma((TILES, XG)), dma((TILES, XG)),
            dma((TILES, XG)), dma((TILES, XG)), dma((2, 4, 2)), dma((2, 4, 2)),
            dma, dma, dma((YS,)), dma((YS,)), dma((ZS,)), dma((ZS,)), dma((XS,)), dma((XS,)),
            dma((ZS,)), dma((ZS,)), dma((XS,)), dma((XS,)), dma((YS,)), dma((YS,)), dma, dma, dma((3,)),
        ],
        compiler_params=pltpu.CompilerParams(
            collective_id=0, has_side_effects=True, vmem_limit_bytes=60 * MIB
        ),
        name="step",
    )(ent, rel, owners, blocks, heads, rel_ids, tails, ntail, nhead)


def widen_kernel(ent_a_ref, ent_b_ref, rel_in_ref, ent_ref, rel_ref):
    ent_ref[...] = ent_a_ref[...] + ent_b_ref[...].astype(F32)
    rel_ref[...] = rel_in_ref[...].astype(F32)


def widen(ent_a, ent_b, rel):
    return pl.pallas_call(
        widen_kernel,
        out_shape=(
            jax.ShapeDtypeStruct((WIDTH, 512), F32), jax.ShapeDtypeStruct((WIDTH, REL), F32)
        ),
        in_specs=[vmem()] * 3,
        out_specs=[vmem()] * 2,
        compiler_params=pltpu.CompilerParams(vmem_limit_bytes=16 * MIB),
        name="widen",
    )(ent_a, ent_b, rel)


def sum_everywhere(part):
    rows = part.shape[0]
    for axis in ("row", "bucket"):
        count = lax.axis_size(axis)
        each = -(-rows // count)
        padded = jnp.pad(part, ((0, each * count - rows), (0, 0)))
        pieces = lax.all_to_all(padded, axis, split_axis=0, concat_axis=0, tiled=True)
        piece = jnp.sum(pieces.reshape(count, each, -1), axis=0)
        copies = jnp.tile(piece, (count, 1))
        part = lax.all_to_all(copies, axis, split_axis=0, concat_axis=0, tiled=True)[:rows]
    return part


def side_weights(positive, scores):
    largest = jnp.maximum(positive, jnp.max(scores, axis=1))
    own_term = jnp.exp(positive - largest)
    others = jnp.exp(scores - largest[:, None])
    total = own_term + jnp.sum(others, axis=1)
    return (own_term / total - 1.0, others / total[:, None])


def edge_block_grads(buffer, relations, head_ids, rel_ids, tail_ids, neg_tail, neg_head):
    middle = relations.shape[1] // 2
    head_rows = jnp.take(buffer, head_ids, axis=0).astype(jnp.float32)
    tail_rows = jnp.take(buffer, tail_ids, axis=0).astype(jnp.float32)
    rel_rows = jnp.take(relations, rel_ids, axis=0)
    rel_real, rel_imag = (rel_rows[:, :middle], rel_rows[:, middle:])
    head_real, head_imag = (head_rows[:, :middle], head_rows[:, middle:])
    tail_real, tail_imag = (tail_rows[:, :middle], tail_rows[:, middle:])
    query = jnp.concatenate(
        [head_real * rel_real - head_imag * rel_imag, head_real * rel_imag + head_imag * rel_real],
        axis=1,
    )
    probe = jnp.concatenate(
        [rel_real * tail_real + rel_imag * tail_imag, rel_real * tail_imag - rel_imag * tail_real],
        axis=1,
    )
    positive = jnp.sum(query * tail_rows, axis=1)
    tail_negs = jnp.take(buffer, neg_tail, axis=0)
    head_negs = jnp.take(buffer, neg_head, axis=0)
    query_low = query.astype(jnp.bfloat16)
    probe_low = probe.astype(jnp.bfloat16)
    contract_last = (((1,), (1,)), ((), ()))
    contract_first = (((0,), (0,)), ((), ()))
    tail_scores = lax.dot_general(
        query_low, tail_negs, contract_last, preferred_element_type=jnp.float32
    )
    head_scores = lax.dot_general(
        probe_low, head_negs, contract_last, preferred_element_type=jnp.float32
    )
    tail_coef, tail_weights = side_weights(positive, tail_scores)
    head_coef, head_weights = side_weights(positive, head_scores)
    tail_low = tail_weights.astype(jnp.bfloat16)
    head_low = head_weights.astype(jnp.bfloat16)
    both_coef = (tail_coef + head_coef)[:, None]
    query_grad = both_coef * tail_rows + jnp.dot(
        tail_low, tail_negs, preferred_element_type=jnp.float32
    )
    probe_grad = jnp.dot(head_low, head_negs, preferred_element_type=jnp.float32)
    tail_neg_grad = lax.dot_general(
        tail_low, query_low, contract_first, preferred_element_type=jnp.float32
    )
    head_neg_grad = lax.dot_general(
        head_low, probe_low, contract_first, preferred_element_type=jnp.float32
    )
    qgrad_real, qgrad_imag = (query_grad[:, :middle], query_grad[:, middle:])
    pgrad_real, pgrad_imag = (probe_grad[:, :middle], probe_grad[:, middle:])
    head_grad = jnp.concatenate(
        [
            qgrad_real * rel_real + qgrad_imag * rel_imag,
            qgrad_imag * rel_real - qgrad_real * rel_imag,
        ],
        axis=1,
    )
    tail_grad = both_coef * query + jnp.concatenate(
        [
            pgrad_real * rel_real - pgrad_imag * rel_imag,
            pgrad_real * rel_imag + pgrad_imag * rel_real,
        ],
        axis=1,
    )
    rel_edge_grad = jnp.concatenate(
        [
            qgrad_real * head_real
            + qgrad_imag * head_imag
            + pgrad_real * tail_real
            + pgrad_imag * tail_imag,
            qgrad_imag * head_real
            - qgrad_real * head_imag
            + pgrad_real * tail_imag
            - pgrad_imag * tail_real,
        ],
        axis=1,
    )
    row_ids = jnp.concatenate([head_ids, tail_ids, neg_tail, neg_head])
    row_vals = jnp.concatenate([head_grad, tail_grad, tail_neg_grad, head_neg_grad], axis=0)
    return (row_ids, row_vals, rel_edge_grad)


def device_grads(buffer, relations, head_ids, rel_ids, tail_ids, neg_tail, neg_head):
    blocks_count = neg_tail.shape[0]
    start_zero = (jnp.zeros(buffer.shape, jnp.float32), jnp.zeros(relations.shape, jnp.float32))

    def advance(totals, position):
        row_ids, row_vals, rel_edge_grad = edge_block_grads(
            buffer, relations, head_ids, rel_ids, tail_ids, neg_tail[position], neg_head[position]
        )
        return (
            (totals[0].at[row_ids].add(row_vals), totals[1].at[rel_ids].add(rel_edge_grad)),
            None,
        )

    totals, unused = lax.scan(advance, start_zero, jnp.arange(blocks_count, dtype=jnp.int32))
    return totals


def dense_step(
    entities, relations, touch_owner, touch_block, head_ids, rel_ids, tail_ids, neg_tail, neg_head
):
    bucket_count = lax.axis_size("bucket")
    block_rows = BLOCK
    width = entities.shape[1]
    owned = entities.shape[0] // block_rows
    owners = touch_owner[0]
    wanted = touch_block[0]
    touched = owners.shape[0]
    slot_ids = jnp.arange(bucket_count, dtype=jnp.int32)
    matches = owners[:, None] == slot_ids[None, :]
    request = jnp.sum(jnp.where(matches, wanted[:, None] + 1, 0), axis=0) - 1
    incoming = lax.all_to_all(request, "bucket", split_axis=0, concat_axis=0, tiled=True)
    selector = (incoming[:, None] == jnp.arange(owned, dtype=jnp.int32)[None, :]).astype(
        jnp.float32
    )
    owned_flat = entities.reshape(owned, block_rows * width)
    reply = jnp.dot(selector, owned_flat, precision=lax.Precision.HIGHEST).astype(jnp.bfloat16)
    reply = reply.reshape(bucket_count, block_rows, width)
    fetched = lax.all_to_all(reply, "bucket", split_axis=0, concat_axis=0, tiled=True)
    buffer = jnp.take(fetched, owners, axis=0).reshape(touched * block_rows, width)
    buffer_grad, rel_part = device_grads(
        buffer, relations, head_ids, rel_ids, tail_ids, neg_tail, neg_head
    )
    outgoing = jnp.zeros((bucket_count, block_rows, width), jnp.float32)
    outgoing = outgoing.at[owners].set(buffer_grad.reshape(touched, block_rows, width))
    returned = lax.all_to_all(outgoing, "bucket", split_axis=0, concat_axis=0, tiled=True)
    entity_grad = lax.dot_general(
        selector,
        returned.reshape(bucket_count, block_rows * width),
        (((0,), (0,)), ((), ())),
        precision=lax.Precision.HIGHEST,
    )
    entity_grad = entity_grad.reshape(owned * block_rows, width)
    relation_grad = sum_everywhere(rel_part)
    return (entity_grad, relation_grad)


def per_device(
    entities, relations, touch_owner, touch_block, head_ids, rel_ids, tail_ids, neg_tail, neg_head
):
    ent_a, ent_b, rel, over = fast_step(
        entities.T, relations.T, touch_owner, touch_block,
        head_ids[None, :], rel_ids[None, :], tail_ids[None, :], neg_tail, neg_head,
    )
    ent, rel = lax.cond(
        over[0, 0] > 0.5,
        lambda: tuple(
            part.T
            for part in dense_step(
                entities, relations, touch_owner, touch_block, head_ids, rel_ids, tail_ids,
                neg_tail, neg_head,
            )
        ),
        lambda: widen(ent_a, ent_b, rel),
    )
    return (ent.T, rel.T)


def solution(mesh):
    return jax.shard_map(
        per_device,
        mesh=mesh,
        in_specs=(
            P(("bucket", "row"), None),
            P(),
            P(("bucket", "row"), None),
            P(("bucket", "row"), None),
            P(("bucket", "row")),
            P(("bucket", "row")),
            P(("bucket", "row")),
            P(("bucket", "row"), None),
            P(("bucket", "row"), None),
        ),
        out_specs=(P(("bucket", "row"), None), P()),
        check_vma=False,
    )
```

```python
import functools

import jax
import jax.numpy as jnp
from jax import lax
from jax.experimental import pallas as pl
from jax.experimental.pallas import tpu as pltpu
from jax.sharding import PartitionSpec as P

BLOCK = 128
WIDTH = 400
EDGES = 1024
NEG = 100
REL = 1300
REL_PAD = 1536
ALL = 2 * EDGES + 2 * BLOCK
XS, ZS, CS, YS = 4, 8, 2, 4
XG = XS * CS
TILES = 3
CAP = TILES * BLOCK
DIST = (0, 1, 7, 2, 6, 3, 5, 4)
PARTS = (
    ((0, 0), (0, 1), (1, 0), (1, 1), (2, 0), (2, 1)),
    ((3, 0), (3, 1), (4, 0), (4, 1), (5, 0), (6, 0)),
    ((5, 1), (6, 1), (7, 0), (7, 1)),
)
HALF = 208
HALF_START = 192
BF = jnp.bfloat16
F32 = jnp.float32
I32 = jnp.int32
NT = (((1,), (1,)), ((), ()))
TN = (((0,), (0,)), ((), ()))
MIB = 1024 * 1024


def mm(a, b, dims=(((1,), (0,)), ((), ()))):
    return lax.dot_general(a, b, dims, preferred_element_type=F32)


def iota(shape, dim):
    return lax.broadcasted_iota(I32, shape, dim)


def hot(mask):
    return jnp.where(mask, 1.0, 0.0).astype(BF)


def place():
    b = lax.axis_index("bucket")
    return b // (ZS * CS), (b // CS) % ZS, b % CS, lax.axis_index("row")


def bucket_of(x, z, c):
    return (x * ZS + z) * CS + c


def x_peer(x, z, c, k):
    s = lax.rem(x * CS + c + k, XG)
    return s, {"bucket": bucket_of(s // CS, z, s % CS)}


def z_peer(x, z, c, k):
    other = lax.rem(z + k, ZS)
    return other, {"bucket": bucket_of(x, other, c)}


def greet(peers):
    for peer in peers:
        pl.semaphore_signal(
            pltpu.get_barrier_semaphore(), inc=1, device_id=peer,
            device_id_type=pl.DeviceIdType.MESH,
        )


def remote(src, dst, send, recv, peer):
    return pltpu.make_async_remote_copy(
        src_ref=src, dst_ref=dst, send_sem=send, recv_sem=recv,
        device_id=peer, device_id_type=pl.DeviceIdType.MESH,
    )


def plan_rows(ids, owners, blocks, z):
    slot = lax.shift_right_arithmetic(ids, 7)
    row = jnp.bitwise_and(ids, 127)
    slot_hot = hot(iota((64, ALL), 0) == slot)
    row_is = iota((BLOCK, ALL), 0) == row
    row_hot = hot(row_is)
    count = mm(slot_hot, row_hot, NT)
    wanted_slot = hot(count > 0.5)
    j = iota((64, 64), 0)
    s, q = j // 8, j % 8
    dist = jnp.where(q % 2 == 1, (q + 1) // 2, (8 - q // 2) % 8)
    target = bucket_of(s // CS, (z + dist) % ZS, s % CS)
    perm_is = owners == target
    perm = hot(perm_is)
    wanted = mm(perm, wanted_slot)
    block = jnp.sum(jnp.where(perm_is, blocks, 0), axis=1, keepdims=True)
    wanted_low = wanted.astype(BF)
    before = mm(wanted_low, hot(iota((BLOCK, BLOCK), 0) < iota((BLOCK, BLOCK), 1)))
    number = mm(wanted_low, jnp.ones((BLOCK, BLOCK), BF))
    jj = iota((64, 64), 1)
    same = hot(s == jj // 8)
    ahead = hot((s == jj // 8) & (jj % 8 < q))
    q_wide = iota((64, BLOCK), 0) % 8
    late = (q_wide == 7) | ((q_wide >= 5) & (jnp.zeros((64, BLOCK), I32) + block >= 2))
    tile_of = jnp.where(q_wide < 3, 0, jnp.where(late, 2, 1))
    lead = jnp.zeros((64, BLOCK), F32)
    sums = []
    for t in range(TILES):
        part = jnp.where(tile_of == t, number, 0.0).astype(BF)
        lead = jnp.where(tile_of == t, mm(ahead, part), lead)
        sums.append(mm(same, part))
    start1 = jnp.maximum(float(BLOCK), sums[0])
    start2 = jnp.maximum(float(2 * BLOCK), start1 + sums[1])
    end = start2 + sums[2]
    start = jnp.where(tile_of == 0, 0.0, jnp.where(tile_of == 1, start1, start2))
    rank = (start + lead + before).astype(I32)
    codes = jnp.where(wanted > 0.5, block * 1024 + rank, -1)
    overflow = jnp.max(jnp.where(end > float(CAP), 1.0, 0.0))
    position = (iota((64, BLOCK), 0) // 8) * CAP + rank
    high = lax.shift_right_arithmetic(position, 7).astype(F32).astype(BF)
    low = jnp.bitwise_and(position, 127).astype(F32).astype(BF)
    high_slot = mm(perm, high, TN).astype(BF)
    low_slot = mm(perm, low, TN).astype(BF)
    high_ids = mm(high_slot, slot_hot, TN)
    low_ids = mm(low_slot, slot_hot, TN)
    value = jnp.sum(jnp.where(row_is, high_ids * 128.0 + low_ids, 0.0), axis=0, keepdims=True)
    places = jnp.where(slot >= 0, value.astype(I32), -1)
    return codes, places, overflow


def twice(row):
    return jnp.concatenate([row, row], axis=1)


def side(positive, scores, valid):
    largest = jnp.maximum(
        positive, jnp.max(jnp.where(valid, scores, -3e38), axis=0, keepdims=True)
    )
    own = jnp.exp(positive - largest)
    others = jnp.where(valid, jnp.exp(scores - largest), 0.0)
    total = own + jnp.sum(others, axis=0, keepdims=True)
    return own / total - 1.0, others / total


def step_kernel(
    ent_ref, rel_in_ref, owner_ref, block_ref, head_ref, rel_ids_ref, tail_ref, ntail_ref, nhead_ref,
    ent_ref_a, ent_ref_b, rel_ref, flag_ref,
    tables, codes_mine, codes_in, fstage, flanded, total, ids_ref, place_ref, rows_ref,
    hot_rel, high, low, relation, edge_rel, neg_sum, grads_ref, relg_ref,
    stage, landed, ring_out, ring_in,
    core_out, core_in, y_out, y_in, x_out, x_in, z_in, zg_out, zg_in, xg_out, xg_in, yg_out, yg_in, cg_in,
    sum_core, sum_y, sum_x, over_ref, ent_in, rel_in, last_hot,
    gring_send, gring_recv, ask_send, ask_recv, ftile_send, ftile_recv,
    tile_send, tile_recv, ring_send, ring_recv,
    core_send, core_recv, y_send, y_recv, z_send, z_recv, x_send, x_recv,
    zg_send, zg_recv, xg_send, xg_recv, yg_send, yg_recv, cg_send, cg_recv, in_sem,
):
    x, z, c, y = place()
    me = x * CS + c
    z_peers = [z_peer(x, z, c, k) for k in range(ZS)]
    x_peers = [x_peer(x, z, c, k) for k in range(XG)]
    y_peers = [(lax.rem(y + k, YS), {"row": lax.rem(y + k, YS)}) for k in range(YS)]
    same_core = [
        (lax.rem(x + k, XS), {"bucket": bucket_of(lax.rem(x + k, XS), z, c)}) for k in range(XS)
    ]
    mate = {"bucket": bucket_of(x, z, 1 - c)}
    right, left = z_peers[1][1], z_peers[ZS - 1][1]
    mid = WIDTH // 2
    pending = []

    def go(copy):
        copy.start()
        pending.append(copy)

    everyone = [p for _, p in z_peers[1:]] + [p for _, p in x_peers[1:]] + [p for _, p in y_peers[1:]]
    greet(everyone)

    def load(half):
        lanes = pl.ds(half * 256, 256)
        return pltpu.make_async_copy(ent_ref.at[:, lanes], ent_in.at[:, lanes], in_sem.at[half])

    rel_load = pltpu.make_async_copy(rel_in_ref, rel_in, in_sem.at[2])
    load(0).start()
    load(1).start()
    rel_load.start()
    load(0).wait()
    tables[0, 0] = ent_in[:, 0:256].astype(BF)
    pl.semaphore_wait(pltpu.get_barrier_semaphore(), len(everyone))

    def gring(way, step, half):
        if way == 0:
            src, dst = (-step) % ZS, (-step - 1) % ZS
        else:
            src, dst = step, step + 1
        return remote(
            tables.at[src, half], tables.at[dst, half],
            gring_send.at[way, step, half], gring_recv.at[way, step, half],
            right if way == 0 else left,
        )

    def legs(step):
        if step < 3:
            return [(0, 0), (1, 0), (0, 1), (1, 1)]
        return [(0, 1), (1, 0)]

    def forward(step, halves=(0, 1)):
        for way, half in legs(step):
            if half not in halves:
                continue
            gring(way, step, half).wait_recv()
            if step < 3 and (way, half) in legs(step + 1):
                go(gring(way, step + 1, half))

    def ask(k):
        s, peer = x_peers[k]
        return remote(codes_mine.at[s], codes_in.at[me], ask_send.at[k], ask_recv.at[k], peer)

    def ftile(t, k):
        return remote(
            fstage.at[t, k], flanded.at[t, me], ftile_send.at[t, k], ftile_recv.at[t, k],
            x_peers[k][1],
        )

    def select(t, group, send):
        parts = PARTS[group]
        lhs = jnp.concatenate([tables[DIST[q], half] for q, half in parts], axis=1)
        key = (iota((BLOCK, 256), 1) // BLOCK) * 1024 + iota((BLOCK, 256), 0) + t * BLOCK
        for pair in range(XG // 2):
            both = (2 * pair + 1, (2 * pair + 2) % XG)
            chosen = []
            for k in both:
                code = codes_in[x_peers[k][0]]
                chosen.append(
                    jnp.concatenate(
                        [hot(twice(code[q : q + 1]) == key + 2048 * half) for q, half in parts],
                        axis=1,
                    )
                )
            rows = mm(lhs, jnp.concatenate(chosen, axis=0), NT).astype(BF)
            for i, k in enumerate(both):
                part = rows[:, i * BLOCK : (i + 1) * BLOCK]
                if group > 0:
                    part = part + fstage[t, k]
                if send and k == 0:
                    flanded[t, me] = part
                else:
                    fstage[t, k] = part
                    if send:
                        go(ftile(t, k))

    def gather(t):
        for k in range(1, XG):
            s = lax.rem(me + XG - k, XG)
            remote(
                fstage.at[t, k], flanded.at[t, s], ftile_send.at[t, k], ftile_recv.at[t, k],
                x_peers[k][1],
            ).wait_recv()
        key = iota((XG * BLOCK, 256), 0)
        key = (key // BLOCK) * CAP + key % BLOCK + t * BLOCK

        def chunk(i, carry):
            lanes = pl.ds(pl.multiple_of(i * 256, 256), 256)
            lhs = jnp.concatenate([flanded[t, s] for s in range(XG)], axis=1)
            if t < TILES - 1:
                rows = mm(lhs, hot(key == place_ref[:, lanes]))
            else:
                rows = mm(lhs, last_hot[:, lanes])
            if t == 0:
                total[:, lanes] = rows
            elif t < TILES - 1:
                total[:, lanes] += rows
            else:
                rows_ref[:, lanes] = (total[:, lanes] + rows).astype(BF)
            return carry

        lax.fori_loop(0, ALL // 256, chunk, 0)

    def prepare():
        key = iota((XG * BLOCK, 256), 0)
        key = (key // BLOCK) * CAP + key % BLOCK + (TILES - 1) * BLOCK

        def chunk(i, carry):
            lanes = pl.ds(pl.multiple_of(i * 256, 256), 256)
            last_hot[:, lanes] = hot(key == place_ref[:, lanes])
            return carry

        lax.fori_loop(0, ALL // 256, chunk, 0)

    def relation_rows():
        high[...] = jnp.zeros_like(high)
        low[...] = jnp.zeros_like(low)
        rel_load.wait()
        rel = rel_in[...]
        rel_high = rel.astype(BF)
        high[:, 0:REL] = rel_high
        low[:, 0:REL] = (rel - rel_high.astype(F32)).astype(BF)

        def chunk(i, carry):
            lanes = pl.ds(pl.multiple_of(i * 256, 256), 256)
            which = hot(iota((REL_PAD, 256), 0) == rel_ids_ref[:, lanes])
            hot_rel[:, lanes] = which
            relation[:, lanes] = mm(high[...], which) + mm(low[...], which)
            return carry

        lax.fori_loop(0, EDGES // 256, chunk, 0)

    def edges():
        neg_sum[...] = jnp.zeros_like(neg_sum)
        step = 256

        def chunk(i, carry):
            lanes = pl.ds(pl.multiple_of(i * step, step), step)
            tail_lanes = pl.ds(pl.multiple_of(EDGES + i * step, step), step)
            a, b = relation[0:mid, lanes], relation[mid:WIDTH, lanes]
            head = rows_ref[:, lanes].astype(F32)
            tail = rows_ref[:, tail_lanes].astype(F32)
            hr, hi = head[:mid], head[mid:]
            tr, ti = tail[:mid], tail[mid:]
            query = jnp.concatenate([hr * a - hi * b, hr * b + hi * a], axis=0)
            probe = jnp.concatenate([a * tr + b * ti, a * ti - b * tr], axis=0)
            positive = jnp.sum(query * tail, axis=0, keepdims=True)
            query_low, probe_low = query.astype(BF), probe.astype(BF)
            tail_neg = rows_ref[:, 2 * EDGES : 2 * EDGES + BLOCK]
            head_neg = rows_ref[:, 2 * EDGES + BLOCK : 2 * EDGES + 2 * BLOCK]
            valid = iota((BLOCK, step), 0) < NEG
            tail_coef, tail_weights = side(positive, mm(tail_neg, query_low, TN), valid)
            head_coef, head_weights = side(positive, mm(head_neg, probe_low, TN), valid)
            tail_low, head_low = tail_weights.astype(BF), head_weights.astype(BF)
            both = tail_coef + head_coef
            qg = both * tail + mm(tail_neg, tail_low)
            pg = mm(head_neg, head_low)
            neg_sum[0] += mm(query_low, tail_low, NT)
            neg_sum[1] += mm(probe_low, head_low, NT)
            qr, qi = qg[:mid], qg[mid:]
            pr, pi = pg[:mid], pg[mid:]
            grads_ref[:, lanes] = jnp.concatenate(
                [qr * a + qi * b, qi * a - qr * b], axis=0
            ).astype(BF)
            grads_ref[:, tail_lanes] = (
                both * query + jnp.concatenate([pr * a - pi * b, pr * b + pi * a], axis=0)
            ).astype(BF)
            edge_rel[:, lanes] = jnp.concatenate(
                [
                    qr * hr + qi * hi + pr * tr + pi * ti,
                    qi * hr - qr * hi + pr * ti - pi * tr,
                ],
                axis=0,
            ).astype(BF)
            return carry

        lax.fori_loop(0, EDGES // step, chunk, 0)
        grads_ref[:, 2 * EDGES : 2 * EDGES + BLOCK] = neg_sum[0].astype(BF)
        grads_ref[:, 2 * EDGES + BLOCK : 2 * EDGES + 2 * BLOCK] = neg_sum[1].astype(BF)

    def relation_scatter():
        def chunk(i, carry):
            lanes = pl.ds(pl.multiple_of(i * 256, 256), 256)
            relg_ref[:, lanes] = mm(edge_rel[...], hot_rel[lanes, :], NT)
            return carry

        lax.fori_loop(0, REL_PAD // 256, chunk, 0)
        relg_ref[:, REL_PAD - BLOCK :] = jnp.zeros((WIDTH, BLOCK), F32) + over_ref[0:1, :]

    def core_copy():
        return remote(core_out, core_in, core_send, core_recv, mate)

    def rel_core():
        core_out[...] = relg_ref[pl.ds(pl.multiple_of((1 - c) * HALF_START, 16), HALF), :].astype(BF)
        go(core_copy())

    def y_copy(k):
        return remote(y_out.at[k], y_in.at[k], y_send.at[k], y_recv.at[k], y_peers[k][1])

    def rel_y():
        core_copy().wait_recv()
        mine = pl.ds(pl.multiple_of(c * HALF_START, 16), HALF)
        sum_core[...] = relg_ref[mine, :] + core_in[...].astype(F32)
        for k in range(1, YS):
            other = y_peers[k][0]
            y_out[k] = sum_core[:, pl.ds(pl.multiple_of(other * 384, 128), 384)].astype(BF)
            go(y_copy(k))

    def x_copy(k):
        return remote(x_out.at[k], x_in.at[k], x_send.at[k], x_recv.at[k], same_core[k][1])

    def rel_x():
        for k in range(1, YS):
            y_copy(k).wait_recv()
        summed = sum_core[:, pl.ds(pl.multiple_of(y * 384, 128), 384)]
        for k in range(1, YS):
            summed = summed + y_in[k].astype(F32)
        sum_y[HALF:, :] = jnp.zeros((256 - HALF, 384), F32)
        sum_y[0:HALF, :] = summed
        for k in range(1, XS):
            other = same_core[k][0]
            x_out[k] = sum_y[pl.ds(pl.multiple_of(other * 64, 64), 64), :].astype(BF)
            go(x_copy(k))

    def z_copy(k):
        return remote(
            sum_x.at[pl.ds(pl.multiple_of(z_peers[k][0] * 8, 8), 8)], z_in.at[k],
            z_send.at[k], z_recv.at[k], z_peers[k][1],
        )

    def rel_z():
        for k in range(1, XS):
            x_copy(k).wait_recv()
        summed = sum_y[pl.ds(pl.multiple_of(x * 64, 64), 64), :]
        for k in range(1, XS):
            summed = summed + x_in[k].astype(F32)
        sum_x[...] = summed
        for k in range(1, ZS):
            go(z_copy(k))

    def zg_copy(k):
        return remote(zg_out, zg_in.at[z], zg_send.at[k], zg_recv.at[k], z_peers[k][1])

    def rel_zg():
        for k in range(1, ZS):
            z_copy(k).wait_recv()
        summed = sum_x[pl.ds(pl.multiple_of(z * 8, 8), 8), :]
        for k in range(1, ZS):
            summed = summed + z_in[k]
        zg_out[...] = summed
        zg_in[z] = summed
        for k in range(1, ZS):
            go(zg_copy(k))

    def xg_copy(k):
        return remote(xg_out, xg_in.at[x], xg_send.at[k], xg_recv.at[k], same_core[k][1])

    def rel_xg():
        for k in range(1, ZS):
            s = lax.rem(z + ZS - k, ZS)
            remote(zg_out, zg_in.at[s], zg_send.at[k], zg_recv.at[k], z_peers[k][1]).wait_recv()
        whole = jnp.concatenate([zg_in[i] for i in range(ZS)], axis=0).astype(BF)
        xg_out[...] = whole
        xg_in[x] = whole
        for k in range(1, XS):
            go(xg_copy(k))

    def yg_copy(k):
        return remote(yg_out, yg_in.at[y], yg_send.at[k], yg_recv.at[k], y_peers[k][1])

    def rel_yg():
        for k in range(1, XS):
            s = lax.rem(x + XS - k, XS)
            remote(xg_out, xg_in.at[s], xg_send.at[k], xg_recv.at[k], same_core[k][1]).wait_recv()
        whole = jnp.concatenate([xg_in[i] for i in range(XS)], axis=0)[0:HALF]
        yg_out[...] = whole
        yg_in[y] = whole
        for k in range(1, YS):
            go(yg_copy(k))

    def cg_copy():
        return remote(yg_in, cg_in, cg_send, cg_recv, mate)

    def rel_cg():
        for k in range(1, YS):
            s = lax.rem(y + YS - k, YS)
            remote(yg_out, yg_in.at[s], yg_send.at[k], yg_recv.at[k], y_peers[k][1]).wait_recv()
        go(cg_copy())

    def rel_end():
        cg_copy().wait_recv()
        for i in range(YS):
            mine, other = yg_in[i], cg_in[i]
            first = jnp.where(c == 0, mine, other)
            second = jnp.where(c == 0, other, mine)
            whole = jnp.concatenate([first, second[HALF - HALF_START :]], axis=0)
            if i < YS - 1:
                rel_ref[:, i * 384 : (i + 1) * 384] = whole
            else:
                rel_ref[:, i * 384 : REL] = whole[:, : REL - i * 384]
                flag_ref[0, 0] = jnp.max(whole[0:16, 256:384].astype(F32))

    def tile(t, k):
        return remote(
            stage.at[t, k], landed.at[t, me], tile_send.at[t, k], tile_recv.at[t, k], x_peers[k][1]
        )

    def scatter(t):
        for pair in range(XG // 2):
            both = (2 * pair + 1, (2 * pair + 2) % XG)
            if t < TILES - 1:
                row = iota((BLOCK, ALL), 0) + t * BLOCK
                which = [hot(row + x_peers[k][0] * CAP == place_ref[...]) for k in both]
            else:
                which = [
                    last_hot[pl.ds(pl.multiple_of(x_peers[k][0] * BLOCK, BLOCK), BLOCK), :]
                    for k in both
                ]
            which = jnp.concatenate(which, axis=0)
            rows = mm(grads_ref[...], which, NT).astype(BF)
            for i, k in enumerate(both):
                part = rows[:, i * BLOCK : (i + 1) * BLOCK]
                if k == 0:
                    landed[t, me] = part
                else:
                    stage[t, k] = part
                    go(tile(t, k))

    def arrive(t):
        for k in range(1, XG):
            s = lax.rem(me + XG - k, XG)
            remote(
                stage.at[t, k], landed.at[t, s], tile_send.at[t, k], tile_recv.at[t, k],
                x_peers[k][1],
            ).wait_recv()

    def partial(dist, half):
        q = DIST.index(dist)
        least = [t for t in range(TILES) if (q, half) in PARTS[t]][0]
        parts = [(t, s) for t in range(least, TILES) for s in range(XG)]
        lhs = jnp.concatenate([landed[t, s] for t, s in parts], axis=1)
        key = (iota((BLOCK, 256), 1) // BLOCK + 2 * half) * 1024 + iota((BLOCK, 256), 0)
        which = jnp.concatenate(
            [hot(twice(codes_in[s, q : q + 1]) == key + t * BLOCK) for t, s in parts], axis=0
        )
        return mm(lhs, which)

    def ring(way, step, half):
        return remote(
            ring_out.at[way, step, half], ring_in.at[way, step, half],
            ring_send.at[way, step, half], ring_recv.at[way, step, half],
            right if way == 0 else left,
        )

    def has(way, step, half):
        return 0 < step or half == 1 - way

    def push(step, way, half):
        value = partial(4 - step if way == 0 else (4 + step) % ZS, half)
        if step > 0 and has(way, step - 1, half):
            ring(way, step - 1, half).wait_recv()
            value = value + ring_in[way, step - 1, half].astype(F32)
        ring_out[way, step, half] = value.astype(BF)
        go(ring(way, step, half))

    def begin():
        for way in range(2):
            go(gring(way, 0, 0))
        load(1).wait()
        tables[0, 1] = ent_in[:, 256:512].astype(BF)
        for way in range(2):
            go(gring(way, 0, 1))

    def plan():
        ids_ref[:, 0:EDGES] = head_ref[...]
        ids_ref[:, EDGES : 2 * EDGES] = tail_ref[...]
        ids_ref[:, 2 * EDGES :] = jnp.full((1, 2 * BLOCK), -1, I32)
        ids_ref[:, 2 * EDGES : 2 * EDGES + NEG] = ntail_ref[...]
        ids_ref[:, 2 * EDGES + BLOCK : 2 * EDGES + BLOCK + NEG] = nhead_ref[...]
        codes, places, overflow = plan_rows(ids_ref[...], owner_ref[...], block_ref[...], z)
        codes_mine[...] = codes.reshape(XG, 8, BLOCK)
        place_ref[...] = places
        over_ref[...] = jnp.zeros((8, BLOCK), F32) + overflow
        for k in range(1, XG):
            go(ask(k))
        codes_in[me] = codes_mine[me]

    def asked():
        for k in range(1, XG):
            s = lax.rem(me + XG - k, XG)
            remote(
                codes_mine.at[s], codes_in.at[s], ask_send.at[k], ask_recv.at[k], x_peers[k][1]
            ).wait_recv()

    def finish():
        for half in range(2):
            lanes = slice(half * 256, (half + 1) * 256)
            own = partial(0, half)
            ring(0, 3, half).wait_recv()
            ent_ref_a[:, lanes] = own + ring_in[0, 3, half].astype(F32)
            ring(1, 3, half).wait_recv()
            ent_ref_b[:, lanes] = ring_in[1, 3, half]

    order = [
        (begin,), (plan,), (forward, 0, (0,)), (relation_rows,), (forward, 0, (1,)), (asked,),
        (select, 0, 0, True), (forward, 1, (0,)), (select, 1, 0, False),
        (forward, 1, (1,)), (select, 2, 0, False), (forward, 2, (0,)), (select, 1, 1, True),
        (forward, 2, (1,)), (gather, 0), (select, 2, 1, False), (forward, 3),
        (select, 2, 2, True), (prepare,), (gather, 1), (gather, 2), (edges,),
        (scatter, 2), (relation_scatter,), (rel_core,), (scatter, 1), (rel_y,), (scatter, 0),
        (arrive, 2), (push, 0, 0, 1), (push, 0, 1, 0), (push, 1, 1, 1), (push, 1, 0, 1),
        (rel_x,), (arrive, 1), (push, 1, 0, 0), (push, 1, 1, 0), (rel_z,),
        (push, 2, 1, 1), (push, 2, 0, 1), (rel_zg,), (push, 2, 0, 0), (push, 2, 1, 0), (rel_xg,),
        (arrive, 0), (push, 3, 1, 1), (push, 3, 0, 1), (push, 3, 0, 0), (push, 3, 1, 0),
        (rel_yg,), (rel_cg,), (finish,), (rel_end,),
    ]
    for function, *values in order:
        function(*values)
    for copy in pending:
        copy.wait_send()


def vmem():
    return pl.BlockSpec(memory_space=pltpu.VMEM)


def fast_step(ent, rel, owners, blocks, heads, rel_ids, tails, ntail, nhead):
    dma = pltpu.SemaphoreType.DMA
    v = pltpu.VMEM
    return pl.pallas_call(
        step_kernel,
        out_shape=(
            jax.ShapeDtypeStruct((WIDTH, 512), F32),
            jax.ShapeDtypeStruct((WIDTH, 512), BF),
            jax.ShapeDtypeStruct((WIDTH, REL), BF),
            jax.ShapeDtypeStruct((1, 1), F32),
        ),
        in_specs=[pl.BlockSpec(memory_space=pl.ANY)] * 2 + [vmem()] * 7,
        out_specs=[vmem()] * 3 + [pl.BlockSpec(memory_space=pltpu.SMEM)],
        scratch_shapes=[
            v((ZS, 2, WIDTH, 256), BF),
            v((XG, 8, BLOCK), I32), v((XG, 8, BLOCK), I32),
            v((TILES, XG, WIDTH, BLOCK), BF), v((TILES, XG, WIDTH, BLOCK), BF),
            v((WIDTH, ALL), F32), v((1, ALL), I32), v((1, ALL), I32), v((WIDTH, ALL), BF),
            v((REL_PAD, EDGES), BF), v((WIDTH, REL_PAD), BF), v((WIDTH, REL_PAD), BF),
            v((WIDTH, EDGES), F32), v((WIDTH, EDGES), BF), v((2, WIDTH, BLOCK), F32),
            v((WIDTH, ALL), BF), v((WIDTH, REL_PAD), F32),
            v((TILES, XG, WIDTH, BLOCK), BF), v((TILES, XG, WIDTH, BLOCK), BF),
            v((2, 4, 2, WIDTH, 256), BF), v((2, 4, 2, WIDTH, 256), BF),
            v((HALF, REL_PAD), BF), v((HALF, REL_PAD), BF),
            v((YS, HALF, 384), BF), v((YS, HALF, 384), BF),
            v((XS, 64, 384), BF), v((XS, 64, 384), BF),
            v((ZS, 8, 384), F32), v((8, 384), F32), v((ZS, 8, 384), F32),
            v((64, 384), BF), v((XS, 64, 384), BF),
            v((HALF, 384), BF), v((YS, HALF, 384), BF), v((YS, HALF, 384), BF),
            v((HALF, REL_PAD), F32), v((256, 384), F32), v((64, 384), F32), v((8, BLOCK), F32),
            v((WIDTH, 512), F32), v((WIDTH, REL), F32), v((XG * BLOCK, ALL), BF),
            dma((2, 4, 2)), dma((2, 4, 2)), dma((XG,)), dma((XG,)),
            dma((TILES, XG)), dma((TILES, XG)),
            dma((TILES, XG)), dma((TILES, XG)), dma((2, 4, 2)), dma((2, 4, 2)),
            dma, dma, dma((YS,)), dma((YS,)), dma((ZS,)), dma((ZS,)), dma((XS,)), dma((XS,)),
            dma((ZS,)), dma((ZS,)), dma((XS,)), dma((XS,)), dma((YS,)), dma((YS,)), dma, dma, dma((3,)),
        ],
        compiler_params=pltpu.CompilerParams(
            collective_id=0, has_side_effects=True, vmem_limit_bytes=60 * MIB
        ),
        name="step",
    )(ent, rel, owners, blocks, heads, rel_ids, tails, ntail, nhead)


def widen_kernel(ent_a_ref, ent_b_ref, rel_in_ref, ent_ref, rel_ref):
    ent_ref[...] = ent_a_ref[...] + ent_b_ref[...].astype(F32)
    rel_ref[...] = rel_in_ref[...].astype(F32)


def widen(ent_a, ent_b, rel):
    return pl.pallas_call(
        widen_kernel,
        out_shape=(
            jax.ShapeDtypeStruct((WIDTH, 512), F32), jax.ShapeDtypeStruct((WIDTH, REL), F32)
        ),
        in_specs=[vmem()] * 3,
        out_specs=[vmem()] * 2,
        compiler_params=pltpu.CompilerParams(vmem_limit_bytes=16 * MIB),
        name="widen",
    )(ent_a, ent_b, rel)


def sum_everywhere(part):
    rows = part.shape[0]
    for axis in ("row", "bucket"):
        count = lax.axis_size(axis)
        each = -(-rows // count)
        padded = jnp.pad(part, ((0, each * count - rows), (0, 0)))
        pieces = lax.all_to_all(padded, axis, split_axis=0, concat_axis=0, tiled=True)
        piece = jnp.sum(pieces.reshape(count, each, -1), axis=0)
        copies = jnp.tile(piece, (count, 1))
        part = lax.all_to_all(copies, axis, split_axis=0, concat_axis=0, tiled=True)[:rows]
    return part


def side_weights(positive, scores):
    largest = jnp.maximum(positive, jnp.max(scores, axis=1))
    own_term = jnp.exp(positive - largest)
    others = jnp.exp(scores - largest[:, None])
    total = own_term + jnp.sum(others, axis=1)
    return (own_term / total - 1.0, others / total[:, None])


def edge_block_grads(buffer, relations, head_ids, rel_ids, tail_ids, neg_tail, neg_head):
    middle = relations.shape[1] // 2
    head_rows = jnp.take(buffer, head_ids, axis=0).astype(jnp.float32)
    tail_rows = jnp.take(buffer, tail_ids, axis=0).astype(jnp.float32)
    rel_rows = jnp.take(relations, rel_ids, axis=0)
    rel_real, rel_imag = (rel_rows[:, :middle], rel_rows[:, middle:])
    head_real, head_imag = (head_rows[:, :middle], head_rows[:, middle:])
    tail_real, tail_imag = (tail_rows[:, :middle], tail_rows[:, middle:])
    query = jnp.concatenate(
        [head_real * rel_real - head_imag * rel_imag, head_real * rel_imag + head_imag * rel_real],
        axis=1,
    )
    probe = jnp.concatenate(
        [rel_real * tail_real + rel_imag * tail_imag, rel_real * tail_imag - rel_imag * tail_real],
        axis=1,
    )
    positive = jnp.sum(query * tail_rows, axis=1)
    tail_negs = jnp.take(buffer, neg_tail, axis=0)
    head_negs = jnp.take(buffer, neg_head, axis=0)
    query_low = query.astype(jnp.bfloat16)
    probe_low = probe.astype(jnp.bfloat16)
    contract_last = (((1,), (1,)), ((), ()))
    contract_first = (((0,), (0,)), ((), ()))
    tail_scores = lax.dot_general(
        query_low, tail_negs, contract_last, preferred_element_type=jnp.float32
    )
    head_scores = lax.dot_general(
        probe_low, head_negs, contract_last, preferred_element_type=jnp.float32
    )
    tail_coef, tail_weights = side_weights(positive, tail_scores)
    head_coef, head_weights = side_weights(positive, head_scores)
    tail_low = tail_weights.astype(jnp.bfloat16)
    head_low = head_weights.astype(jnp.bfloat16)
    both_coef = (tail_coef + head_coef)[:, None]
    query_grad = both_coef * tail_rows + jnp.dot(
        tail_low, tail_negs, preferred_element_type=jnp.float32
    )
    probe_grad = jnp.dot(head_low, head_negs, preferred_element_type=jnp.float32)
    tail_neg_grad = lax.dot_general(
        tail_low, query_low, contract_first, preferred_element_type=jnp.float32
    )
    head_neg_grad = lax.dot_general(
        head_low, probe_low, contract_first, preferred_element_type=jnp.float32
    )
    qgrad_real, qgrad_imag = (query_grad[:, :middle], query_grad[:, middle:])
    pgrad_real, pgrad_imag = (probe_grad[:, :middle], probe_grad[:, middle:])
    head_grad = jnp.concatenate(
        [
            qgrad_real * rel_real + qgrad_imag * rel_imag,
            qgrad_imag * rel_real - qgrad_real * rel_imag,
        ],
        axis=1,
    )
    tail_grad = both_coef * query + jnp.concatenate(
        [
            pgrad_real * rel_real - pgrad_imag * rel_imag,
            pgrad_real * rel_imag + pgrad_imag * rel_real,
        ],
        axis=1,
    )
    rel_edge_grad = jnp.concatenate(
        [
            qgrad_real * head_real
            + qgrad_imag * head_imag
            + pgrad_real * tail_real
            + pgrad_imag * tail_imag,
            qgrad_imag * head_real
            - qgrad_real * head_imag
            + pgrad_real * tail_imag
            - pgrad_imag * tail_real,
        ],
        axis=1,
    )
    row_ids = jnp.concatenate([head_ids, tail_ids, neg_tail, neg_head])
    row_vals = jnp.concatenate([head_grad, tail_grad, tail_neg_grad, head_neg_grad], axis=0)
    return (row_ids, row_vals, rel_edge_grad)


def device_grads(buffer, relations, head_ids, rel_ids, tail_ids, neg_tail, neg_head):
    blocks_count = neg_tail.shape[0]
    start_zero = (jnp.zeros(buffer.shape, jnp.float32), jnp.zeros(relations.shape, jnp.float32))

    def advance(totals, position):
        row_ids, row_vals, rel_edge_grad = edge_block_grads(
            buffer, relations, head_ids, rel_ids, tail_ids, neg_tail[position], neg_head[position]
        )
        return (
            (totals[0].at[row_ids].add(row_vals), totals[1].at[rel_ids].add(rel_edge_grad)),
            None,
        )

    totals, unused = lax.scan(advance, start_zero, jnp.arange(blocks_count, dtype=jnp.int32))
    return totals


def dense_step(
    entities, relations, touch_owner, touch_block, head_ids, rel_ids, tail_ids, neg_tail, neg_head
):
    bucket_count = lax.axis_size("bucket")
    block_rows = BLOCK
    width = entities.shape[1]
    owned = entities.shape[0] // block_rows
    owners = touch_owner[0]
    wanted = touch_block[0]
    touched = owners.shape[0]
    slot_ids = jnp.arange(bucket_count, dtype=jnp.int32)
    matches = owners[:, None] == slot_ids[None, :]
    request = jnp.sum(jnp.where(matches, wanted[:, None] + 1, 0), axis=0) - 1
    incoming = lax.all_to_all(request, "bucket", split_axis=0, concat_axis=0, tiled=True)
    selector = (incoming[:, None] == jnp.arange(owned, dtype=jnp.int32)[None, :]).astype(
        jnp.float32
    )
    owned_flat = entities.reshape(owned, block_rows * width)
    reply = jnp.dot(selector, owned_flat, precision=lax.Precision.HIGHEST).astype(jnp.bfloat16)
    reply = reply.reshape(bucket_count, block_rows, width)
    fetched = lax.all_to_all(reply, "bucket", split_axis=0, concat_axis=0, tiled=True)
    buffer = jnp.take(fetched, owners, axis=0).reshape(touched * block_rows, width)
    buffer_grad, rel_part = device_grads(
        buffer, relations, head_ids, rel_ids, tail_ids, neg_tail, neg_head
    )
    outgoing = jnp.zeros((bucket_count, block_rows, width), jnp.float32)
    outgoing = outgoing.at[owners].set(buffer_grad.reshape(touched, block_rows, width))
    returned = lax.all_to_all(outgoing, "bucket", split_axis=0, concat_axis=0, tiled=True)
    entity_grad = lax.dot_general(
        selector,
        returned.reshape(bucket_count, block_rows * width),
        (((0,), (0,)), ((), ())),
        precision=lax.Precision.HIGHEST,
    )
    entity_grad = entity_grad.reshape(owned * block_rows, width)
    relation_grad = sum_everywhere(rel_part)
    return (entity_grad, relation_grad)


def per_device(
    entities, relations, touch_owner, touch_block, head_ids, rel_ids, tail_ids, neg_tail, neg_head
):
    ent_a, ent_b, rel, over = fast_step(
        entities.T, relations.T, touch_owner, touch_block,
        head_ids[None, :], rel_ids[None, :], tail_ids[None, :], neg_tail, neg_head,
    )
    ent, rel = lax.cond(
        over[0, 0] > 0.5,
        lambda: tuple(
            part.T
            for part in dense_step(
                entities, relations, touch_owner, touch_block, head_ids, rel_ids, tail_ids,
                neg_tail, neg_head,
            )
        ),
        lambda: widen(ent_a, ent_b, rel),
    )
    return (ent.T, rel.T)


def solution(mesh):
    return jax.shard_map(
        per_device,
        mesh=mesh,
        in_specs=(
            P(("bucket", "row"), None),
            P(),
            P(("bucket", "row"), None),
            P(("bucket", "row"), None),
            P(("bucket", "row")),
            P(("bucket", "row")),
            P(("bucket", "row")),
            P(("bucket", "row"), None),
            P(("bucket", "row"), None),
        ),
        out_specs=(P(("bucket", "row"), None), P()),
        check_vma=False,
    )
```

```python
import functools

import jax
import jax.numpy as jnp
from jax import lax
from jax.experimental import pallas as pl
from jax.experimental.pallas import tpu as pltpu
from jax.sharding import PartitionSpec as P

BLOCK = 128
WIDTH = 400
EDGES = 1024
NEG = 100
REL = 1300
REL_PAD = 1536
ALL = 2 * EDGES + 2 * BLOCK
XS, ZS, CS, YS = 4, 8, 2, 4
XG = XS * CS
TILES = 3
CAP = TILES * BLOCK
DIST = (0, 1, 7, 2, 6, 3, 5, 4)
PARTS = (
    ((0, 0), (0, 1), (1, 0), (1, 1), (2, 0), (2, 1)),
    ((3, 0), (3, 1), (4, 0), (4, 1), (5, 0), (6, 0)),
    ((5, 1), (6, 1), (7, 0), (7, 1)),
)
PAIRS = ((4, 3), (5, 2), (6, 1), (7, 0))
HALF = 208
HALF_START = 192
BF = jnp.bfloat16
F32 = jnp.float32
I32 = jnp.int32
NT = (((1,), (1,)), ((), ()))
TN = (((0,), (0,)), ((), ()))
MIB = 1024 * 1024


def mm(a, b, dims=(((1,), (0,)), ((), ()))):
    return lax.dot_general(a, b, dims, preferred_element_type=F32)


def iota(shape, dim):
    return lax.broadcasted_iota(I32, shape, dim)


def hot(mask):
    return jnp.where(mask, 1.0, 0.0).astype(BF)


def place():
    b = lax.axis_index("bucket")
    return b // (ZS * CS), (b // CS) % ZS, b % CS, lax.axis_index("row")


def bucket_of(x, z, c):
    return (x * ZS + z) * CS + c


def x_peer(x, z, c, k):
    s = lax.rem(x * CS + c + k, XG)
    return s, {"bucket": bucket_of(s // CS, z, s % CS)}


def z_peer(x, z, c, k):
    other = lax.rem(z + k, ZS)
    return other, {"bucket": bucket_of(x, other, c)}


def greet(peers):
    for peer in peers:
        pl.semaphore_signal(
            pltpu.get_barrier_semaphore(), inc=1, device_id=peer,
            device_id_type=pl.DeviceIdType.MESH,
        )


def remote(src, dst, send, recv, peer):
    return pltpu.make_async_remote_copy(
        src_ref=src, dst_ref=dst, send_sem=send, recv_sem=recv,
        device_id=peer, device_id_type=pl.DeviceIdType.MESH,
    )


def plan_rows(ids, owners, blocks, z):
    slot = lax.shift_right_arithmetic(ids, 7)
    row = jnp.bitwise_and(ids, 127)
    slot_hot = hot(iota((64, ALL), 0) == slot)
    row_is = iota((BLOCK, ALL), 0) == row
    row_hot = hot(row_is)
    count = mm(slot_hot, row_hot, NT)
    wanted_slot = hot(count > 0.5)
    j = iota((64, 64), 0)
    s, q = j // 8, j % 8
    dist = jnp.where(q % 2 == 1, (q + 1) // 2, (8 - q // 2) % 8)
    target = bucket_of(s // CS, (z + dist) % ZS, s % CS)
    perm_is = owners == target
    perm = hot(perm_is)
    wanted = mm(perm, wanted_slot)
    block = jnp.sum(jnp.where(perm_is, blocks, 0), axis=1, keepdims=True)
    wanted_low = wanted.astype(BF)
    before = mm(wanted_low, hot(iota((BLOCK, BLOCK), 0) < iota((BLOCK, BLOCK), 1)))
    number = mm(wanted_low, jnp.ones((BLOCK, BLOCK), BF))
    jj = iota((64, 64), 1)
    same = hot(s == jj // 8)
    ahead = hot((s == jj // 8) & (jj % 8 < q))
    q_wide = iota((64, BLOCK), 0) % 8
    late = (q_wide == 7) | ((q_wide >= 5) & (jnp.zeros((64, BLOCK), I32) + block >= 2))
    tile_of = jnp.where(q_wide < 3, 0, jnp.where(late, 2, 1))
    lead = jnp.zeros((64, BLOCK), F32)
    sums = []
    for t in range(TILES):
        part = jnp.where(tile_of == t, number, 0.0).astype(BF)
        lead = jnp.where(tile_of == t, mm(ahead, part), lead)
        sums.append(mm(same, part))
    start1 = jnp.maximum(float(BLOCK), sums[0])
    start2 = jnp.maximum(float(2 * BLOCK), start1 + sums[1])
    end = start2 + sums[2]
    start = jnp.where(tile_of == 0, 0.0, jnp.where(tile_of == 1, start1, start2))
    rank = (start + lead + before).astype(I32)
    codes = jnp.where(wanted > 0.5, block * 1024 + rank, -1)
    overflow = jnp.max(jnp.where(end > float(CAP), 1.0, 0.0))
    position = (iota((64, BLOCK), 0) // 8) * CAP + rank
    high = lax.shift_right_arithmetic(position, 7).astype(F32).astype(BF)
    low = jnp.bitwise_and(position, 127).astype(F32).astype(BF)
    high_slot = mm(perm, high, TN).astype(BF)
    low_slot = mm(perm, low, TN).astype(BF)
    high_ids = mm(high_slot, slot_hot, TN)
    low_ids = mm(low_slot, slot_hot, TN)
    value = jnp.sum(jnp.where(row_is, high_ids * 128.0 + low_ids, 0.0), axis=0, keepdims=True)
    places = jnp.where(slot >= 0, value.astype(I32), -1)
    return codes, places, overflow


def twice(row):
    return jnp.concatenate([row, row], axis=1)


def side(positive, scores, valid):
    largest = jnp.maximum(
        positive, jnp.max(jnp.where(valid, scores, -3e38), axis=0, keepdims=True)
    )
    own = jnp.exp(positive - largest)
    others = jnp.where(valid, jnp.exp(scores - largest), 0.0)
    total = own + jnp.sum(others, axis=0, keepdims=True)
    return own / total - 1.0, others / total


def step_kernel(
    ent_ref, rel_in_ref, owner_ref, block_ref, head_ref, rel_ids_ref, tail_ref, ntail_ref, nhead_ref,
    ent_ref_a, ent_ref_b, rel_ref, flag_ref,
    tables, codes_mine, codes_in, fstage, flanded, total, ids_ref, place_ref, rows_ref,
    hot_rel, high, low, relation, edge_rel, neg_sum, grads_ref,
    stage, landed, ring_out, ring_in,
    core_out, core_in, y_out, y_in, x_out, x_in, z_in, zg_out, zg_in, xg_out, xg_in, yg_out, yg_in, cg_in,
    sum_core, sum_y, sum_x, over_ref, ent_in, rel_in, last_hot,
    gring_send, gring_recv, ask_send, ask_recv, ftile_send, ftile_recv,
    tile_send, tile_recv, ring_send, ring_recv,
    core_send, core_recv, y_send, y_recv, z_send, z_recv, x_send, x_recv,
    zg_send, zg_recv, xg_send, xg_recv, yg_send, yg_recv, cg_send, cg_recv, in_sem,
):
    x, z, c, y = place()
    me = x * CS + c
    z_peers = [z_peer(x, z, c, k) for k in range(ZS)]
    x_peers = [x_peer(x, z, c, k) for k in range(XG)]
    y_peers = [(lax.rem(y + k, YS), {"row": lax.rem(y + k, YS)}) for k in range(YS)]
    same_core = [
        (lax.rem(x + k, XS), {"bucket": bucket_of(lax.rem(x + k, XS), z, c)}) for k in range(XS)
    ]
    mate = {"bucket": bucket_of(x, z, 1 - c)}
    right, left = z_peers[1][1], z_peers[ZS - 1][1]
    mid = WIDTH // 2
    pending = []

    def go(copy):
        copy.start()
        pending.append(copy)

    everyone = [p for _, p in z_peers[1:]] + [p for _, p in x_peers[1:]] + [p for _, p in y_peers[1:]]
    greet(everyone)

    def load(half):
        lanes = pl.ds(half * 256, 256)
        return pltpu.make_async_copy(ent_ref.at[:, lanes], ent_in.at[:, lanes], in_sem.at[half])

    rel_load = pltpu.make_async_copy(rel_in_ref, rel_in, in_sem.at[2])
    load(0).start()
    load(1).start()
    rel_load.start()
    load(0).wait()
    tables[0, 0] = ent_in[:, 0:256].astype(BF)
    pl.semaphore_wait(pltpu.get_barrier_semaphore(), len(everyone))

    def gring(way, step, half):
        if way == 0:
            src, dst = (-step) % ZS, (-step - 1) % ZS
        else:
            src, dst = step, step + 1
        return remote(
            tables.at[src, half], tables.at[dst, half],
            gring_send.at[way, step, half], gring_recv.at[way, step, half],
            right if way == 0 else left,
        )

    def legs(step):
        if step < 3:
            return [(0, 0), (1, 0), (0, 1), (1, 1)]
        return [(0, 1), (1, 0)]

    def forward(step, halves=(0, 1)):
        for way, half in legs(step):
            if half not in halves:
                continue
            gring(way, step, half).wait_recv()
            if step < 3 and (way, half) in legs(step + 1):
                go(gring(way, step + 1, half))

    def ask(k):
        s, peer = x_peers[k]
        return remote(codes_mine.at[s], codes_in.at[me], ask_send.at[k], ask_recv.at[k], peer)

    def ftile(t, k):
        return remote(
            fstage.at[t, k], flanded.at[t, me], ftile_send.at[t, k], ftile_recv.at[t, k],
            x_peers[k][1],
        )

    def select(t, group, send):
        parts = PARTS[group]
        lhs = jnp.concatenate([tables[DIST[q], half] for q, half in parts], axis=1)
        key = (iota((BLOCK, 256), 1) // BLOCK) * 1024 + iota((BLOCK, 256), 0) + t * BLOCK
        for both in PAIRS:
            chosen = []
            for k in both:
                code = codes_in[x_peers[k][0]]
                chosen.append(
                    jnp.concatenate(
                        [hot(twice(code[q : q + 1]) == key + 2048 * half) for q, half in parts],
                        axis=1,
                    )
                )
            rows = mm(lhs, jnp.concatenate(chosen, axis=0), NT).astype(BF)
            for i, k in enumerate(both):
                part = rows[:, i * BLOCK : (i + 1) * BLOCK]
                if group > 0:
                    part = part + fstage[t, k]
                if send and k == 0:
                    flanded[t, me] = part
                else:
                    fstage[t, k] = part
                    if send:
                        go(ftile(t, k))

    def gather(t):
        for k in range(1, XG):
            s = lax.rem(me + XG - k, XG)
            remote(
                fstage.at[t, k], flanded.at[t, s], ftile_send.at[t, k], ftile_recv.at[t, k],
                x_peers[k][1],
            ).wait_recv()
        key = iota((XG * BLOCK, 256), 0)
        key = (key // BLOCK) * CAP + key % BLOCK + t * BLOCK

        def chunk(i, carry):
            lanes = pl.ds(pl.multiple_of(i * 256, 256), 256)
            lhs = jnp.concatenate([flanded[t, s] for s in range(XG)], axis=1)
            if t < TILES - 1:
                rows = mm(lhs, hot(key == place_ref[:, lanes]))
            else:
                rows = mm(lhs, last_hot[:, lanes])
            if t == 0:
                total[:, lanes] = rows
            elif t < TILES - 1:
                total[:, lanes] += rows
            else:
                rows_ref[:, lanes] = (total[:, lanes] + rows).astype(BF)
            return carry

        lax.fori_loop(0, ALL // 256, chunk, 0)

    def prepare():
        key = iota((XG * BLOCK, 256), 0)
        key = (key // BLOCK) * CAP + key % BLOCK + (TILES - 1) * BLOCK

        def chunk(i, carry):
            lanes = pl.ds(pl.multiple_of(i * 256, 256), 256)
            last_hot[:, lanes] = hot(key == place_ref[:, lanes])
            return carry

        lax.fori_loop(0, ALL // 256, chunk, 0)

    def relation_rows():
        high[...] = jnp.zeros_like(high)
        low[...] = jnp.zeros_like(low)
        rel_load.wait()
        rel = rel_in[...]
        rel_high = rel.astype(BF)
        high[:, 0:REL] = rel_high
        low[:, 0:REL] = (rel - rel_high.astype(F32)).astype(BF)

        def chunk(i, carry):
            lanes = pl.ds(pl.multiple_of(i * 256, 256), 256)
            which = hot(iota((REL_PAD, 256), 0) == rel_ids_ref[:, lanes])
            hot_rel[:, lanes] = which
            relation[:, lanes] = mm(high[...], which) + mm(low[...], which)
            return carry

        lax.fori_loop(0, EDGES // 256, chunk, 0)

    def edges():
        neg_sum[...] = jnp.zeros_like(neg_sum)
        step = 256

        def chunk(i, carry):
            lanes = pl.ds(pl.multiple_of(i * step, step), step)
            tail_lanes = pl.ds(pl.multiple_of(EDGES + i * step, step), step)
            a, b = relation[0:mid, lanes], relation[mid:WIDTH, lanes]
            head = rows_ref[:, lanes].astype(F32)
            tail = rows_ref[:, tail_lanes].astype(F32)
            hr, hi = head[:mid], head[mid:]
            tr, ti = tail[:mid], tail[mid:]
            query = jnp.concatenate([hr * a - hi * b, hr * b + hi * a], axis=0)
            probe = jnp.concatenate([a * tr + b * ti, a * ti - b * tr], axis=0)
            positive = jnp.sum(query * tail, axis=0, keepdims=True)
            query_low, probe_low = query.astype(BF), probe.astype(BF)
            tail_neg = rows_ref[:, 2 * EDGES : 2 * EDGES + BLOCK]
            head_neg = rows_ref[:, 2 * EDGES + BLOCK : 2 * EDGES + 2 * BLOCK]
            valid = iota((BLOCK, step), 0) < NEG
            tail_coef, tail_weights = side(positive, mm(tail_neg, query_low, TN), valid)
            head_coef, head_weights = side(positive, mm(head_neg, probe_low, TN), valid)
            tail_low, head_low = tail_weights.astype(BF), head_weights.astype(BF)
            both = tail_coef + head_coef
            qg = both * tail + mm(tail_neg, tail_low)
            pg = mm(head_neg, head_low)
            neg_sum[0] += mm(query_low, tail_low, NT)
            neg_sum[1] += mm(probe_low, head_low, NT)
            qr, qi = qg[:mid], qg[mid:]
            pr, pi = pg[:mid], pg[mid:]
            grads_ref[:, lanes] = jnp.concatenate(
                [qr * a + qi * b, qi * a - qr * b], axis=0
            ).astype(BF)
            grads_ref[:, tail_lanes] = (
                both * query + jnp.concatenate([pr * a - pi * b, pr * b + pi * a], axis=0)
            ).astype(BF)
            edge_rel[:, lanes] = jnp.concatenate(
                [
                    qr * hr + qi * hi + pr * tr + pi * ti,
                    qi * hr - qr * hi + pr * ti - pi * tr,
                ],
                axis=0,
            ).astype(BF)
            return carry

        lax.fori_loop(0, EDGES // step, chunk, 0)
        grads_ref[:, 2 * EDGES : 2 * EDGES + BLOCK] = neg_sum[0].astype(BF)
        grads_ref[:, 2 * EDGES + BLOCK : 2 * EDGES + 2 * BLOCK] = neg_sum[1].astype(BF)

    def relation_scatter():
        def chunk(i, carry):
            lanes = pl.ds(pl.multiple_of(i * 256, 256), 256)
            total[:, lanes] = mm(edge_rel[...], hot_rel[lanes, :], NT)
            return carry

        lax.fori_loop(0, REL_PAD // 256, chunk, 0)
        total[:, REL_PAD - BLOCK : REL_PAD] = jnp.zeros((WIDTH, BLOCK), F32) + over_ref[0:1, :]

    def core_copy():
        return remote(core_out, core_in, core_send, core_recv, mate)

    def rel_core():
        core_out[...] = total[pl.ds(pl.multiple_of((1 - c) * HALF_START, 16), HALF), 0:REL_PAD].astype(BF)
        go(core_copy())

    def y_copy(k):
        return remote(y_out.at[k], y_in.at[k], y_send.at[k], y_recv.at[k], y_peers[k][1])

    def rel_y():
        core_copy().wait_recv()
        mine = pl.ds(pl.multiple_of(c * HALF_START, 16), HALF)
        sum_core[...] = total[mine, 0:REL_PAD] + core_in[...].astype(F32)
        for k in range(1, YS):
            other = y_peers[k][0]
            y_out[k] = sum_core[:, pl.ds(pl.multiple_of(other * 384, 128), 384)].astype(BF)
            go(y_copy(k))

    def x_copy(k):
        return remote(x_out.at[k], x_in.at[k], x_send.at[k], x_recv.at[k], same_core[k][1])

    def rel_x():
        for k in range(1, YS):
            y_copy(k).wait_recv()
        summed = sum_core[:, pl.ds(pl.multiple_of(y * 384, 128), 384)]
        for k in range(1, YS):
            summed = summed + y_in[k].astype(F32)
        sum_y[HALF:, :] = jnp.zeros((256 - HALF, 384), F32)
        sum_y[0:HALF, :] = summed
        for k in range(1, XS):
            other = same_core[k][0]
            x_out[k] = sum_y[pl.ds(pl.multiple_of(other * 64, 64), 64), :].astype(BF)
            go(x_copy(k))

    def z_copy(k):
        return remote(
            sum_x.at[pl.ds(pl.multiple_of(z_peers[k][0] * 8, 8), 8)], z_in.at[k],
            z_send.at[k], z_recv.at[k], z_peers[k][1],
        )

    def rel_z():
        for k in range(1, XS):
            x_copy(k).wait_recv()
        summed = sum_y[pl.ds(pl.multiple_of(x * 64, 64), 64), :]
        for k in range(1, XS):
            summed = summed + x_in[k].astype(F32)
        sum_x[...] = summed
        for k in range(1, ZS):
            go(z_copy(k))

    def zg_copy(k):
        return remote(zg_out, zg_in.at[z], zg_send.at[k], zg_recv.at[k], z_peers[k][1])

    def rel_zg():
        for k in range(1, ZS):
            z_copy(k).wait_recv()
        summed = sum_x[pl.ds(pl.multiple_of(z * 8, 8), 8), :]
        for k in range(1, ZS):
            summed = summed + z_in[k]
        zg_out[...] = summed
        zg_in[z] = summed
        for k in range(1, ZS):
            go(zg_copy(k))

    def xg_copy(k):
        return remote(xg_out, xg_in.at[x], xg_send.at[k], xg_recv.at[k], same_core[k][1])

    def rel_xg():
        for k in range(1, ZS):
            s = lax.rem(z + ZS - k, ZS)
            remote(zg_out, zg_in.at[s], zg_send.at[k], zg_recv.at[k], z_peers[k][1]).wait_recv()
        whole = jnp.concatenate([zg_in[i] for i in range(ZS)], axis=0).astype(BF)
        xg_out[...] = whole
        xg_in[x] = whole
        for k in range(1, XS):
            go(xg_copy(k))

    def yg_copy(k):
        return remote(yg_out, yg_in.at[y], yg_send.at[k], yg_recv.at[k], y_peers[k][1])

    def rel_yg():
        for k in range(1, XS):
            s = lax.rem(x + XS - k, XS)
            remote(xg_out, xg_in.at[s], xg_send.at[k], xg_recv.at[k], same_core[k][1]).wait_recv()
        whole = jnp.concatenate([xg_in[i] for i in range(XS)], axis=0)[0:HALF]
        yg_out[...] = whole
        yg_in[y] = whole
        for k in (2, 1, 3):
            go(yg_copy(k))
        go(cg_copy(0))

    def cg_copy(k):
        s = lax.rem(y + YS - k, YS)
        return remote(yg_in.at[s], cg_in.at[s], cg_send.at[k], cg_recv.at[k], mate)

    def rel_cg():
        for k in (1, 3, 2):
            s = lax.rem(y + YS - k, YS)
            remote(yg_out, yg_in.at[s], yg_send.at[k], yg_recv.at[k], y_peers[k][1]).wait_recv()
            go(cg_copy(k))

    def rel_end():
        for k in range(YS):
            cg_copy(k).wait_recv()
        for i in range(YS):
            mine, other = yg_in[i], cg_in[i]
            first = jnp.where(c == 0, mine, other)
            second = jnp.where(c == 0, other, mine)
            whole = jnp.concatenate([first, second[HALF - HALF_START :]], axis=0)
            if i < YS - 1:
                rel_ref[:, i * 384 : (i + 1) * 384] = whole
            else:
                rel_ref[:, i * 384 : REL] = whole[:, : REL - i * 384]
                flag_ref[0, 0] = jnp.max(whole[0:16, 256:384].astype(F32))

    def tile(t, k):
        return remote(
            stage.at[t, k], landed.at[t, me], tile_send.at[t, k], tile_recv.at[t, k], x_peers[k][1]
        )

    def scatter(t):
        for both in PAIRS:
            if t < TILES - 1:
                row = iota((BLOCK, ALL), 0) + t * BLOCK
                which = [hot(row + x_peers[k][0] * CAP == place_ref[...]) for k in both]
            else:
                which = [
                    last_hot[pl.ds(pl.multiple_of(x_peers[k][0] * BLOCK, BLOCK), BLOCK), :]
                    for k in both
                ]
            which = jnp.concatenate(which, axis=0)
            rows = mm(grads_ref[...], which, NT).astype(BF)
            for i, k in enumerate(both):
                part = rows[:, i * BLOCK : (i + 1) * BLOCK]
                if k == 0:
                    landed[t, me] = part
                else:
                    stage[t, k] = part
                    go(tile(t, k))

    def arrive(t):
        for k in range(1, XG):
            s = lax.rem(me + XG - k, XG)
            remote(
                stage.at[t, k], landed.at[t, s], tile_send.at[t, k], tile_recv.at[t, k],
                x_peers[k][1],
            ).wait_recv()

    def partial(dist, half):
        q = DIST.index(dist)
        least = [t for t in range(TILES) if (q, half) in PARTS[t]][0]
        parts = [(t, s) for t in range(least, TILES) for s in range(XG)]
        lhs = jnp.concatenate([landed[t, s] for t, s in parts], axis=1)
        key = (iota((BLOCK, 256), 1) // BLOCK + 2 * half) * 1024 + iota((BLOCK, 256), 0)
        which = jnp.concatenate(
            [hot(twice(codes_in[s, q : q + 1]) == key + t * BLOCK) for t, s in parts], axis=0
        )
        return mm(lhs, which)

    def ring(way, step, half):
        return remote(
            ring_out.at[way, step, half], ring_in.at[way, step, half],
            ring_send.at[way, step, half], ring_recv.at[way, step, half],
            right if way == 0 else left,
        )

    def has(way, step, half):
        return 0 < step or half == 1 - way

    def push(step, way, half):
        value = partial(4 - step if way == 0 else (4 + step) % ZS, half)
        if step > 0 and has(way, step - 1, half):
            ring(way, step - 1, half).wait_recv()
            value = value + ring_in[way, step - 1, half].astype(F32)
        ring_out[way, step, half] = value.astype(BF)
        go(ring(way, step, half))

    def begin():
        for way in range(2):
            go(gring(way, 0, 0))
        load(1).wait()
        tables[0, 1] = ent_in[:, 256:512].astype(BF)
        for way in range(2):
            go(gring(way, 0, 1))

    def plan():
        ids_ref[:, 0:EDGES] = head_ref[...]
        ids_ref[:, EDGES : 2 * EDGES] = tail_ref[...]
        ids_ref[:, 2 * EDGES :] = jnp.full((1, 2 * BLOCK), -1, I32)
        ids_ref[:, 2 * EDGES : 2 * EDGES + NEG] = ntail_ref[...]
        ids_ref[:, 2 * EDGES + BLOCK : 2 * EDGES + BLOCK + NEG] = nhead_ref[...]
        codes, places, overflow = plan_rows(ids_ref[...], owner_ref[...], block_ref[...], z)
        codes_mine[...] = codes.reshape(XG, 8, BLOCK)
        place_ref[...] = places
        over_ref[...] = jnp.zeros((8, BLOCK), F32) + overflow
        for k in range(1, XG):
            go(ask(k))
        codes_in[me] = codes_mine[me]

    def asked():
        for k in range(1, XG):
            s = lax.rem(me + XG - k, XG)
            remote(
                codes_mine.at[s], codes_in.at[s], ask_send.at[k], ask_recv.at[k], x_peers[k][1]
            ).wait_recv()

    def own():
        for half in range(2):
            ent_ref_a[:, half * 256 : (half + 1) * 256] = partial(0, half)

    def finish():
        for half in range(2):
            lanes = slice(half * 256, (half + 1) * 256)
            ring(0, 3, half).wait_recv()
            ent_ref_a[:, lanes] += ring_in[0, 3, half].astype(F32)
            ring(1, 3, half).wait_recv()
            ent_ref_b[:, lanes] = ring_in[1, 3, half]

    order = [
        (begin,), (plan,), (forward, 0, (0,)), (relation_rows,), (forward, 0, (1,)), (asked,),
        (select, 0, 0, True), (forward, 1, (0,)), (select, 1, 0, False),
        (forward, 1, (1,)), (select, 2, 0, False), (forward, 2, (0,)), (select, 1, 1, True),
        (forward, 2, (1,)), (gather, 0), (select, 2, 1, False), (forward, 3),
        (select, 2, 2, True), (prepare,), (gather, 1), (gather, 2), (edges,),
        (scatter, 2), (relation_scatter,), (rel_core,), (scatter, 1), (rel_y,), (scatter, 0),
        (arrive, 2), (push, 0, 0, 1), (push, 0, 1, 0), (push, 1, 1, 1), (rel_x,), (push, 1, 0, 1),
        (arrive, 1), (push, 1, 0, 0), (push, 1, 1, 0), (rel_z,), (push, 2, 1, 1), (push, 2, 0, 1),
        (rel_zg,), (push, 2, 0, 0), (push, 2, 1, 0), (arrive, 0), (push, 3, 1, 1), (rel_xg,),
        (push, 3, 0, 1), (rel_yg,), (push, 3, 0, 0), (push, 3, 1, 0), (own,), (rel_cg,),
        (finish,), (rel_end,),
    ]
    for function, *values in order:
        function(*values)
    for copy in pending:
        copy.wait_send()


def vmem():
    return pl.BlockSpec(memory_space=pltpu.VMEM)


def fast_step(ent, rel, owners, blocks, heads, rel_ids, tails, ntail, nhead):
    dma = pltpu.SemaphoreType.DMA
    v = pltpu.VMEM
    return pl.pallas_call(
        step_kernel,
        out_shape=(
            jax.ShapeDtypeStruct((WIDTH, 512), F32),
            jax.ShapeDtypeStruct((WIDTH, 512), BF),
            jax.ShapeDtypeStruct((WIDTH, REL), BF),
            jax.ShapeDtypeStruct((1, 1), F32),
        ),
        in_specs=[pl.BlockSpec(memory_space=pl.ANY)] * 2 + [vmem()] * 7,
        out_specs=[vmem()] * 3 + [pl.BlockSpec(memory_space=pltpu.SMEM)],
        scratch_shapes=[
            v((ZS, 2, WIDTH, 256), BF),
            v((XG, 8, BLOCK), I32), v((XG, 8, BLOCK), I32),
            v((TILES, XG, WIDTH, BLOCK), BF), v((TILES, XG, WIDTH, BLOCK), BF),
            v((WIDTH, ALL), F32), v((1, ALL), I32), v((1, ALL), I32), v((WIDTH, ALL), BF),
            v((REL_PAD, EDGES), BF), v((WIDTH, REL_PAD), BF), v((WIDTH, REL_PAD), BF),
            v((WIDTH, EDGES), F32), v((WIDTH, EDGES), BF), v((2, WIDTH, BLOCK), F32),
            v((WIDTH, ALL), BF),
            v((TILES, XG, WIDTH, BLOCK), BF), v((TILES, XG, WIDTH, BLOCK), BF),
            v((2, 4, 2, WIDTH, 256), BF), v((2, 4, 2, WIDTH, 256), BF),
            v((HALF, REL_PAD), BF), v((HALF, REL_PAD), BF),
            v((YS, HALF, 384), BF), v((YS, HALF, 384), BF),
            v((XS, 64, 384), BF), v((XS, 64, 384), BF),
            v((ZS, 8, 384), F32), v((8, 384), F32), v((ZS, 8, 384), F32),
            v((64, 384), BF), v((XS, 64, 384), BF),
            v((HALF, 384), BF), v((YS, HALF, 384), BF), v((YS, HALF, 384), BF),
            v((HALF, REL_PAD), F32), v((256, 384), F32), v((64, 384), F32), v((8, BLOCK), F32),
            v((WIDTH, 512), F32), v((WIDTH, REL), F32), v((XG * BLOCK, ALL), BF),
            dma((2, 4, 2)), dma((2, 4, 2)), dma((XG,)), dma((XG,)),
            dma((TILES, XG)), dma((TILES, XG)),
            dma((TILES, XG)), dma((TILES, XG)), dma((2, 4, 2)), dma((2, 4, 2)),
            dma, dma, dma((YS,)), dma((YS,)), dma((ZS,)), dma((ZS,)), dma((XS,)), dma((XS,)),
            dma((ZS,)), dma((ZS,)), dma((XS,)), dma((XS,)), dma((YS,)), dma((YS,)), dma((YS,)), dma((YS,)), dma((3,)),
        ],
        compiler_params=pltpu.CompilerParams(
            collective_id=0, has_side_effects=True, vmem_limit_bytes=60 * MIB
        ),
        name="step",
    )(ent, rel, owners, blocks, heads, rel_ids, tails, ntail, nhead)


def widen_kernel(ent_a_ref, ent_b_ref, rel_in_ref, ent_ref, rel_ref):
    ent_ref[...] = ent_a_ref[...] + ent_b_ref[...].astype(F32)
    rel_ref[...] = rel_in_ref[...].astype(F32)


def widen(ent_a, ent_b, rel):
    return pl.pallas_call(
        widen_kernel,
        out_shape=(
            jax.ShapeDtypeStruct((WIDTH, 512), F32), jax.ShapeDtypeStruct((WIDTH, REL), F32)
        ),
        in_specs=[vmem()] * 3,
        out_specs=[vmem()] * 2,
        compiler_params=pltpu.CompilerParams(vmem_limit_bytes=16 * MIB),
        name="widen",
    )(ent_a, ent_b, rel)


def sum_everywhere(part):
    rows = part.shape[0]
    for axis in ("row", "bucket"):
        count = lax.axis_size(axis)
        each = -(-rows // count)
        padded = jnp.pad(part, ((0, each * count - rows), (0, 0)))
        pieces = lax.all_to_all(padded, axis, split_axis=0, concat_axis=0, tiled=True)
        piece = jnp.sum(pieces.reshape(count, each, -1), axis=0)
        copies = jnp.tile(piece, (count, 1))
        part = lax.all_to_all(copies, axis, split_axis=0, concat_axis=0, tiled=True)[:rows]
    return part


def side_weights(positive, scores):
    largest = jnp.maximum(positive, jnp.max(scores, axis=1))
    own_term = jnp.exp(positive - largest)
    others = jnp.exp(scores - largest[:, None])
    total = own_term + jnp.sum(others, axis=1)
    return (own_term / total - 1.0, others / total[:, None])


def edge_block_grads(buffer, relations, head_ids, rel_ids, tail_ids, neg_tail, neg_head):
    middle = relations.shape[1] // 2
    head_rows = jnp.take(buffer, head_ids, axis=0).astype(jnp.float32)
    tail_rows = jnp.take(buffer, tail_ids, axis=0).astype(jnp.float32)
    rel_rows = jnp.take(relations, rel_ids, axis=0)
    rel_real, rel_imag = (rel_rows[:, :middle], rel_rows[:, middle:])
    head_real, head_imag = (head_rows[:, :middle], head_rows[:, middle:])
    tail_real, tail_imag = (tail_rows[:, :middle], tail_rows[:, middle:])
    query = jnp.concatenate(
        [head_real * rel_real - head_imag * rel_imag, head_real * rel_imag + head_imag * rel_real],
        axis=1,
    )
    probe = jnp.concatenate(
        [rel_real * tail_real + rel_imag * tail_imag, rel_real * tail_imag - rel_imag * tail_real],
        axis=1,
    )
    positive = jnp.sum(query * tail_rows, axis=1)
    tail_negs = jnp.take(buffer, neg_tail, axis=0)
    head_negs = jnp.take(buffer, neg_head, axis=0)
    query_low = query.astype(jnp.bfloat16)
    probe_low = probe.astype(jnp.bfloat16)
    contract_last = (((1,), (1,)), ((), ()))
    contract_first = (((0,), (0,)), ((), ()))
    tail_scores = lax.dot_general(
        query_low, tail_negs, contract_last, preferred_element_type=jnp.float32
    )
    head_scores = lax.dot_general(
        probe_low, head_negs, contract_last, preferred_element_type=jnp.float32
    )
    tail_coef, tail_weights = side_weights(positive, tail_scores)
    head_coef, head_weights = side_weights(positive, head_scores)
    tail_low = tail_weights.astype(jnp.bfloat16)
    head_low = head_weights.astype(jnp.bfloat16)
    both_coef = (tail_coef + head_coef)[:, None]
    query_grad = both_coef * tail_rows + jnp.dot(
        tail_low, tail_negs, preferred_element_type=jnp.float32
    )
    probe_grad = jnp.dot(head_low, head_negs, preferred_element_type=jnp.float32)
    tail_neg_grad = lax.dot_general(
        tail_low, query_low, contract_first, preferred_element_type=jnp.float32
    )
    head_neg_grad = lax.dot_general(
        head_low, probe_low, contract_first, preferred_element_type=jnp.float32
    )
    qgrad_real, qgrad_imag = (query_grad[:, :middle], query_grad[:, middle:])
    pgrad_real, pgrad_imag = (probe_grad[:, :middle], probe_grad[:, middle:])
    head_grad = jnp.concatenate(
        [
            qgrad_real * rel_real + qgrad_imag * rel_imag,
            qgrad_imag * rel_real - qgrad_real * rel_imag,
        ],
        axis=1,
    )
    tail_grad = both_coef * query + jnp.concatenate(
        [
            pgrad_real * rel_real - pgrad_imag * rel_imag,
            pgrad_real * rel_imag + pgrad_imag * rel_real,
        ],
        axis=1,
    )
    rel_edge_grad = jnp.concatenate(
        [
            qgrad_real * head_real
            + qgrad_imag * head_imag
            + pgrad_real * tail_real
            + pgrad_imag * tail_imag,
            qgrad_imag * head_real
            - qgrad_real * head_imag
            + pgrad_real * tail_imag
            - pgrad_imag * tail_real,
        ],
        axis=1,
    )
    row_ids = jnp.concatenate([head_ids, tail_ids, neg_tail, neg_head])
    row_vals = jnp.concatenate([head_grad, tail_grad, tail_neg_grad, head_neg_grad], axis=0)
    return (row_ids, row_vals, rel_edge_grad)


def device_grads(buffer, relations, head_ids, rel_ids, tail_ids, neg_tail, neg_head):
    blocks_count = neg_tail.shape[0]
    start_zero = (jnp.zeros(buffer.shape, jnp.float32), jnp.zeros(relations.shape, jnp.float32))

    def advance(totals, position):
        row_ids, row_vals, rel_edge_grad = edge_block_grads(
            buffer, relations, head_ids, rel_ids, tail_ids, neg_tail[position], neg_head[position]
        )
        return (
            (totals[0].at[row_ids].add(row_vals), totals[1].at[rel_ids].add(rel_edge_grad)),
            None,
        )

    totals, unused = lax.scan(advance, start_zero, jnp.arange(blocks_count, dtype=jnp.int32))
    return totals


def dense_step(
    entities, relations, touch_owner, touch_block, head_ids, rel_ids, tail_ids, neg_tail, neg_head
):
    bucket_count = lax.axis_size("bucket")
    block_rows = BLOCK
    width = entities.shape[1]
    owned = entities.shape[0] // block_rows
    owners = touch_owner[0]
    wanted = touch_block[0]
    touched = owners.shape[0]
    slot_ids = jnp.arange(bucket_count, dtype=jnp.int32)
    matches = owners[:, None] == slot_ids[None, :]
    request = jnp.sum(jnp.where(matches, wanted[:, None] + 1, 0), axis=0) - 1
    incoming = lax.all_to_all(request, "bucket", split_axis=0, concat_axis=0, tiled=True)
    selector = (incoming[:, None] == jnp.arange(owned, dtype=jnp.int32)[None, :]).astype(
        jnp.float32
    )
    owned_flat = entities.reshape(owned, block_rows * width)
    reply = jnp.dot(selector, owned_flat, precision=lax.Precision.HIGHEST).astype(jnp.bfloat16)
    reply = reply.reshape(bucket_count, block_rows, width)
    fetched = lax.all_to_all(reply, "bucket", split_axis=0, concat_axis=0, tiled=True)
    buffer = jnp.take(fetched, owners, axis=0).reshape(touched * block_rows, width)
    buffer_grad, rel_part = device_grads(
        buffer, relations, head_ids, rel_ids, tail_ids, neg_tail, neg_head
    )
    outgoing = jnp.zeros((bucket_count, block_rows, width), jnp.float32)
    outgoing = outgoing.at[owners].set(buffer_grad.reshape(touched, block_rows, width))
    returned = lax.all_to_all(outgoing, "bucket", split_axis=0, concat_axis=0, tiled=True)
    entity_grad = lax.dot_general(
        selector,
        returned.reshape(bucket_count, block_rows * width),
        (((0,), (0,)), ((), ())),
        precision=lax.Precision.HIGHEST,
    )
    entity_grad = entity_grad.reshape(owned * block_rows, width)
    relation_grad = sum_everywhere(rel_part)
    return (entity_grad, relation_grad)


def per_device(
    entities, relations, touch_owner, touch_block, head_ids, rel_ids, tail_ids, neg_tail, neg_head
):
    ent_a, ent_b, rel, over = fast_step(
        entities.T, relations.T, touch_owner, touch_block,
        head_ids[None, :], rel_ids[None, :], tail_ids[None, :], neg_tail, neg_head,
    )
    ent, rel = lax.cond(
        over[0, 0] > 0.5,
        lambda: tuple(
            part.T
            for part in dense_step(
                entities, relations, touch_owner, touch_block, head_ids, rel_ids, tail_ids,
                neg_tail, neg_head,
            )
        ),
        lambda: widen(ent_a, ent_b, rel),
    )
    return (ent.T, rel.T)


def solution(mesh):
    return jax.shard_map(
        per_device,
        mesh=mesh,
        in_specs=(
            P(("bucket", "row"), None),
            P(),
            P(("bucket", "row"), None),
            P(("bucket", "row"), None),
            P(("bucket", "row")),
            P(("bucket", "row")),
            P(("bucket", "row")),
            P(("bucket", "row"), None),
            P(("bucket", "row"), None),
        ),
        out_specs=(P(("bucket", "row"), None), P()),
        check_vma=False,
    )
```

```python
import functools

import jax
import jax.numpy as jnp
from jax import lax
from jax.experimental import pallas as pl
from jax.experimental.pallas import tpu as pltpu
from jax.sharding import PartitionSpec as P

BLOCK = 128
WIDTH = 400
EDGES = 1024
NEG = 100
REL = 1300
REL_PAD = 1536
ALL = 2 * EDGES + 2 * BLOCK
XS, ZS, CS, YS = 4, 8, 2, 4
XG = XS * CS
TILES = 3
CAP = TILES * BLOCK
DIST = (0, 1, 7, 2, 6, 3, 5, 4)
PARTS = (
    ((0, 0), (0, 1), (1, 0), (1, 1), (2, 0), (2, 1)),
    ((3, 0), (3, 1), (4, 0), (4, 1), (5, 0), (6, 0)),
    ((5, 1), (6, 1), (7, 0), (7, 1)),
)
PAIRS = ((4, 3), (5, 2), (6, 1), (7, 0))
HALF = 208
HALF_START = 192
BF = jnp.bfloat16
F32 = jnp.float32
I32 = jnp.int32
NT = (((1,), (1,)), ((), ()))
TN = (((0,), (0,)), ((), ()))
MIB = 1024 * 1024


def mm(a, b, dims=(((1,), (0,)), ((), ()))):
    return lax.dot_general(a, b, dims, preferred_element_type=F32)


def iota(shape, dim):
    return lax.broadcasted_iota(I32, shape, dim)


def hot(mask):
    return jnp.where(mask, 1.0, 0.0).astype(BF)


def place():
    b = lax.axis_index("bucket")
    return b // (ZS * CS), (b // CS) % ZS, b % CS, lax.axis_index("row")


def bucket_of(x, z, c):
    return (x * ZS + z) * CS + c


def x_peer(x, z, c, k):
    s = lax.rem(x * CS + c + k, XG)
    return s, {"bucket": bucket_of(s // CS, z, s % CS)}


def z_peer(x, z, c, k):
    other = lax.rem(z + k, ZS)
    return other, {"bucket": bucket_of(x, other, c)}


def greet(peers):
    for peer in peers:
        pl.semaphore_signal(
            pltpu.get_barrier_semaphore(), inc=1, device_id=peer,
            device_id_type=pl.DeviceIdType.MESH,
        )


def remote(src, dst, send, recv, peer):
    return pltpu.make_async_remote_copy(
        src_ref=src, dst_ref=dst, send_sem=send, recv_sem=recv,
        device_id=peer, device_id_type=pl.DeviceIdType.MESH,
    )


def plan_rows(ids, owners, blocks, z):
    slot = lax.shift_right_arithmetic(ids, 7)
    row = jnp.bitwise_and(ids, 127)
    slot_hot = hot(iota((64, ALL), 0) == slot)
    row_is = iota((BLOCK, ALL), 0) == row
    row_hot = hot(row_is)
    count = mm(slot_hot, row_hot, NT)
    wanted_slot = hot(count > 0.5)
    j = iota((64, 64), 0)
    s, q = j // 8, j % 8
    dist = jnp.where(q % 2 == 1, (q + 1) // 2, (8 - q // 2) % 8)
    target = bucket_of(s // CS, (z + dist) % ZS, s % CS)
    perm_is = owners == target
    perm = hot(perm_is)
    wanted = mm(perm, wanted_slot)
    block = jnp.sum(jnp.where(perm_is, blocks, 0), axis=1, keepdims=True)
    wanted_low = wanted.astype(BF)
    before = mm(wanted_low, hot(iota((BLOCK, BLOCK), 0) < iota((BLOCK, BLOCK), 1)))
    number = mm(wanted_low, jnp.ones((BLOCK, BLOCK), BF))
    jj = iota((64, 64), 1)
    same = hot(s == jj // 8)
    ahead = hot((s == jj // 8) & (jj % 8 < q))
    q_wide = iota((64, BLOCK), 0) % 8
    late = (q_wide == 7) | ((q_wide >= 5) & (jnp.zeros((64, BLOCK), I32) + block >= 2))
    tile_of = jnp.where(q_wide < 3, 0, jnp.where(late, 2, 1))
    lead = jnp.zeros((64, BLOCK), F32)
    sums = []
    for t in range(TILES):
        part = jnp.where(tile_of == t, number, 0.0).astype(BF)
        lead = jnp.where(tile_of == t, mm(ahead, part), lead)
        sums.append(mm(same, part))
    start1 = jnp.maximum(float(BLOCK), sums[0])
    start2 = jnp.maximum(float(2 * BLOCK), start1 + sums[1])
    end = start2 + sums[2]
    start = jnp.where(tile_of == 0, 0.0, jnp.where(tile_of == 1, start1, start2))
    rank = (start + lead + before).astype(I32)
    codes = jnp.where(wanted > 0.5, block * 1024 + rank, -1)
    overflow = jnp.max(jnp.where(end > float(CAP), 1.0, 0.0))
    position = (iota((64, BLOCK), 0) // 8) * CAP + rank
    high = lax.shift_right_arithmetic(position, 7).astype(F32).astype(BF)
    low = jnp.bitwise_and(position, 127).astype(F32).astype(BF)
    high_slot = mm(perm, high, TN).astype(BF)
    low_slot = mm(perm, low, TN).astype(BF)
    high_ids = mm(high_slot, slot_hot, TN)
    low_ids = mm(low_slot, slot_hot, TN)
    value = jnp.sum(jnp.where(row_is, high_ids * 128.0 + low_ids, 0.0), axis=0, keepdims=True)
    places = jnp.where(slot >= 0, value.astype(I32), -1)
    return codes, places, overflow


def twice(row):
    return jnp.concatenate([row, row], axis=1)


def side(positive, scores, valid):
    largest = jnp.maximum(
        positive, jnp.max(jnp.where(valid, scores, -3e38), axis=0, keepdims=True)
    )
    own = jnp.exp(positive - largest)
    others = jnp.where(valid, jnp.exp(scores - largest), 0.0)
    total = own + jnp.sum(others, axis=0, keepdims=True)
    return own / total - 1.0, others / total


def step_kernel(
    ent_ref, rel_in_ref, owner_ref, block_ref, head_ref, rel_ids_ref, tail_ref, ntail_ref, nhead_ref,
    ent_ref_a, ent_ref_b, rel_ref, flag_ref,
    tables, codes_mine, codes_in, fstage, flanded, total, ids_ref, place_ref, rows_ref,
    hot_rel, high, low, relation, edge_rel, neg_sum, grads_ref,
    stage, landed, ring_out, ring_in,
    core_out, core_in, y_out, y_in, x_out, x_in, z_in, zg_out, zg_in, xg_out, xg_in, yg_out, yg_in, cg_in,
    sum_core, sum_y, sum_x, over_ref, ent_in, rel_in, last_hot,
    gring_send, gring_recv, ask_send, ask_recv, ftile_send, ftile_recv,
    tile_send, tile_recv, ring_send, ring_recv,
    core_send, core_recv, y_send, y_recv, z_send, z_recv, x_send, x_recv,
    zg_send, zg_recv, xg_send, xg_recv, yg_send, yg_recv, cg_send, cg_recv, in_sem,
):
    x, z, c, y = place()
    me = x * CS + c
    z_peers = [z_peer(x, z, c, k) for k in range(ZS)]
    x_peers = [x_peer(x, z, c, k) for k in range(XG)]
    y_peers = [(lax.rem(y + k, YS), {"row": lax.rem(y + k, YS)}) for k in range(YS)]
    same_core = [
        (lax.rem(x + k, XS), {"bucket": bucket_of(lax.rem(x + k, XS), z, c)}) for k in range(XS)
    ]
    mate = {"bucket": bucket_of(x, z, 1 - c)}
    right, left = z_peers[1][1], z_peers[ZS - 1][1]
    mid = WIDTH // 2
    pending = []

    def go(copy):
        copy.start()
        pending.append(copy)

    everyone = [p for _, p in z_peers[1:]] + [p for _, p in x_peers[1:]] + [p for _, p in y_peers[1:]]
    greet(everyone)

    def load(half):
        lanes = pl.ds(half * 256, 256)
        return pltpu.make_async_copy(ent_ref.at[:, lanes], ent_in.at[:, lanes], in_sem.at[half])

    rel_load = pltpu.make_async_copy(rel_in_ref, rel_in, in_sem.at[2])
    load(0).start()
    load(1).start()
    rel_load.start()
    load(0).wait()
    tables[0, 0] = ent_in[:, 0:256].astype(BF)
    pl.semaphore_wait(pltpu.get_barrier_semaphore(), len(everyone))

    def gring(way, step, half):
        if way == 0:
            src, dst = (-step) % ZS, (-step - 1) % ZS
        else:
            src, dst = step, step + 1
        return remote(
            tables.at[src, half], tables.at[dst, half],
            gring_send.at[way, step, half], gring_recv.at[way, step, half],
            right if way == 0 else left,
        )

    def legs(step):
        if step < 3:
            return [(0, 0), (1, 0), (0, 1), (1, 1)]
        return [(0, 1), (1, 0)]

    def forward(step, halves=(0, 1)):
        for way, half in legs(step):
            if half not in halves:
                continue
            gring(way, step, half).wait_recv()
            if step < 3 and (way, half) in legs(step + 1):
                go(gring(way, step + 1, half))

    def ask(k):
        s, peer = x_peers[k]
        return remote(codes_mine.at[s], codes_in.at[me], ask_send.at[k], ask_recv.at[k], peer)

    def ftile(t, k):
        return remote(
            fstage.at[t, k], flanded.at[t, me], ftile_send.at[t, k], ftile_recv.at[t, k],
            x_peers[k][1],
        )

    def select(t, group, send):
        parts = PARTS[group]
        lhs = jnp.concatenate([tables[DIST[q], half] for q, half in parts], axis=1)
        key = (iota((BLOCK, 256), 1) // BLOCK) * 1024 + iota((BLOCK, 256), 0) + t * BLOCK
        for both in PAIRS:
            chosen = []
            for k in both:
                code = codes_in[x_peers[k][0]]
                chosen.append(
                    jnp.concatenate(
                        [hot(twice(code[q : q + 1]) == key + 2048 * half) for q, half in parts],
                        axis=1,
                    )
                )
            rows = mm(lhs, jnp.concatenate(chosen, axis=0), NT).astype(BF)
            for i, k in enumerate(both):
                part = rows[:, i * BLOCK : (i + 1) * BLOCK]
                if group > 0:
                    part = part + fstage[t, k]
                if send and k == 0:
                    flanded[t, me] = part
                else:
                    fstage[t, k] = part
                    if send:
                        go(ftile(t, k))

    def gather(t):
        for k in range(1, XG):
            s = lax.rem(me + XG - k, XG)
            remote(
                fstage.at[t, k], flanded.at[t, s], ftile_send.at[t, k], ftile_recv.at[t, k],
                x_peers[k][1],
            ).wait_recv()
        key = iota((XG * BLOCK, 256), 0)
        key = (key // BLOCK) * CAP + key % BLOCK + t * BLOCK

        def chunk(i, carry):
            lanes = pl.ds(pl.multiple_of(i * 256, 256), 256)
            lhs = jnp.concatenate([flanded[t, s] for s in range(XG)], axis=1)
            rows = mm(lhs, hot(key == place_ref[:, lanes]))
            if t == 0:
                total[:, lanes] = rows
            else:
                total[:, lanes] += rows
            return carry

        lax.fori_loop(0, ALL // 256, chunk, 0)

    def gather_last(ks, whole):
        t = TILES - 1
        sources = [lax.rem(me + XG - k, XG) for k in ks]
        for k, s in zip(ks, sources):
            if k > 0:
                remote(
                    fstage.at[t, k], flanded.at[t, s], ftile_send.at[t, k], ftile_recv.at[t, k],
                    x_peers[k][1],
                ).wait_recv()

        def chunk(i, carry):
            lanes = pl.ds(pl.multiple_of(i * 256, 256), 256)
            lhs = jnp.concatenate([flanded[t, s] for s in sources], axis=1)
            which = [
                last_hot[pl.ds(pl.multiple_of(s * BLOCK, BLOCK), BLOCK), lanes] for s in sources
            ]
            rows = total[:, lanes] + mm(lhs, jnp.concatenate(which, axis=0))
            if whole:
                rows_ref[:, lanes] = rows.astype(BF)
            else:
                total[:, lanes] = rows
            return carry

        lax.fori_loop(0, ALL // 256, chunk, 0)

    def prepare():
        key = iota((XG * BLOCK, 256), 0)
        key = (key // BLOCK) * CAP + key % BLOCK + (TILES - 1) * BLOCK

        def chunk(i, carry):
            lanes = pl.ds(pl.multiple_of(i * 256, 256), 256)
            last_hot[:, lanes] = hot(key == place_ref[:, lanes])
            return carry

        lax.fori_loop(0, ALL // 256, chunk, 0)

    def relation_rows():
        high[...] = jnp.zeros_like(high)
        low[...] = jnp.zeros_like(low)
        rel_load.wait()
        rel = rel_in[...]
        rel_high = rel.astype(BF)
        high[:, 0:REL] = rel_high
        low[:, 0:REL] = (rel - rel_high.astype(F32)).astype(BF)

        def chunk(i, carry):
            lanes = pl.ds(pl.multiple_of(i * 256, 256), 256)
            which = hot(iota((REL_PAD, 256), 0) == rel_ids_ref[:, lanes])
            hot_rel[:, lanes] = which
            relation[:, lanes] = mm(high[...], which) + mm(low[...], which)
            return carry

        lax.fori_loop(0, EDGES // 256, chunk, 0)

    def edges():
        neg_sum[...] = jnp.zeros_like(neg_sum)
        step = 256

        def chunk(i, carry):
            lanes = pl.ds(pl.multiple_of(i * step, step), step)
            tail_lanes = pl.ds(pl.multiple_of(EDGES + i * step, step), step)
            a, b = relation[0:mid, lanes], relation[mid:WIDTH, lanes]
            head = rows_ref[:, lanes].astype(F32)
            tail = rows_ref[:, tail_lanes].astype(F32)
            hr, hi = head[:mid], head[mid:]
            tr, ti = tail[:mid], tail[mid:]
            query = jnp.concatenate([hr * a - hi * b, hr * b + hi * a], axis=0)
            probe = jnp.concatenate([a * tr + b * ti, a * ti - b * tr], axis=0)
            positive = jnp.sum(query * tail, axis=0, keepdims=True)
            query_low, probe_low = query.astype(BF), probe.astype(BF)
            tail_neg = rows_ref[:, 2 * EDGES : 2 * EDGES + BLOCK]
            head_neg = rows_ref[:, 2 * EDGES + BLOCK : 2 * EDGES + 2 * BLOCK]
            valid = iota((BLOCK, step), 0) < NEG
            tail_coef, tail_weights = side(positive, mm(tail_neg, query_low, TN), valid)
            head_coef, head_weights = side(positive, mm(head_neg, probe_low, TN), valid)
            tail_low, head_low = tail_weights.astype(BF), head_weights.astype(BF)
            both = tail_coef + head_coef
            qg = both * tail + mm(tail_neg, tail_low)
            pg = mm(head_neg, head_low)
            neg_sum[0] += mm(query_low, tail_low, NT)
            neg_sum[1] += mm(probe_low, head_low, NT)
            qr, qi = qg[:mid], qg[mid:]
            pr, pi = pg[:mid], pg[mid:]
            grads_ref[:, lanes] = jnp.concatenate(
                [qr * a + qi * b, qi * a - qr * b], axis=0
            ).astype(BF)
            grads_ref[:, tail_lanes] = (
                both * query + jnp.concatenate([pr * a - pi * b, pr * b + pi * a], axis=0)
            ).astype(BF)
            edge_rel[:, lanes] = jnp.concatenate(
                [
                    qr * hr + qi * hi + pr * tr + pi * ti,
                    qi * hr - qr * hi + pr * ti - pi * tr,
                ],
                axis=0,
            ).astype(BF)
            return carry

        lax.fori_loop(0, EDGES // step, chunk, 0)
        grads_ref[:, 2 * EDGES : 2 * EDGES + BLOCK] = neg_sum[0].astype(BF)
        grads_ref[:, 2 * EDGES + BLOCK : 2 * EDGES + 2 * BLOCK] = neg_sum[1].astype(BF)

    def relation_scatter():
        def chunk(i, carry):
            lanes = pl.ds(pl.multiple_of(i * 256, 256), 256)
            total[:, lanes] = mm(edge_rel[...], hot_rel[lanes, :], NT)
            return carry

        lax.fori_loop(0, REL_PAD // 256, chunk, 0)
        total[:, REL_PAD - BLOCK : REL_PAD] = jnp.zeros((WIDTH, BLOCK), F32) + over_ref[0:1, :]

    def core_copy():
        return remote(core_out, core_in, core_send, core_recv, mate)

    def rel_core():
        core_out[...] = total[pl.ds(pl.multiple_of((1 - c) * HALF_START, 16), HALF), 0:REL_PAD].astype(BF)
        go(core_copy())

    def y_copy(k):
        return remote(y_out.at[k], y_in.at[k], y_send.at[k], y_recv.at[k], y_peers[k][1])

    def rel_y():
        core_copy().wait_recv()
        mine = pl.ds(pl.multiple_of(c * HALF_START, 16), HALF)
        sum_core[...] = total[mine, 0:REL_PAD] + core_in[...].astype(F32)
        for k in range(1, YS):
            other = y_peers[k][0]
            y_out[k] = sum_core[:, pl.ds(pl.multiple_of(other * 384, 128), 384)].astype(BF)
            go(y_copy(k))

    def x_copy(k):
        return remote(x_out.at[k], x_in.at[k], x_send.at[k], x_recv.at[k], same_core[k][1])

    def rel_x():
        for k in range(1, YS):
            y_copy(k).wait_recv()
        summed = sum_core[:, pl.ds(pl.multiple_of(y * 384, 128), 384)]
        for k in range(1, YS):
            summed = summed + y_in[k].astype(F32)
        sum_y[HALF:, :] = jnp.zeros((256 - HALF, 384), F32)
        sum_y[0:HALF, :] = summed
        for k in range(1, XS):
            other = same_core[k][0]
            x_out[k] = sum_y[pl.ds(pl.multiple_of(other * 64, 64), 64), :].astype(BF)
            go(x_copy(k))

    def z_copy(k):
        return remote(
            sum_x.at[pl.ds(pl.multiple_of(z_peers[k][0] * 8, 8), 8)], z_in.at[k],
            z_send.at[k], z_recv.at[k], z_peers[k][1],
        )

    def rel_z():
        for k in range(1, XS):
            x_copy(k).wait_recv()
        summed = sum_y[pl.ds(pl.multiple_of(x * 64, 64), 64), :]
        for k in range(1, XS):
            summed = summed + x_in[k].astype(F32)
        sum_x[...] = summed
        for k in range(1, ZS):
            go(z_copy(k))

    def zg_copy(k):
        return remote(zg_out, zg_in.at[z], zg_send.at[k], zg_recv.at[k], z_peers[k][1])

    def rel_zg():
        for k in range(1, ZS):
            z_copy(k).wait_recv()
        summed = sum_x[pl.ds(pl.multiple_of(z * 8, 8), 8), :]
        for k in range(1, ZS):
            summed = summed + z_in[k]
        zg_out[...] = summed
        zg_in[z] = summed
        for k in range(1, ZS):
            go(zg_copy(k))

    def xg_copy(k):
        return remote(xg_out, xg_in.at[x], xg_send.at[k], xg_recv.at[k], same_core[k][1])

    def rel_xg():
        for k in range(1, ZS):
            s = lax.rem(z + ZS - k, ZS)
            remote(zg_out, zg_in.at[s], zg_send.at[k], zg_recv.at[k], z_peers[k][1]).wait_recv()
        whole = jnp.concatenate([zg_in[i] for i in range(ZS)], axis=0).astype(BF)
        xg_out[...] = whole
        xg_in[x] = whole
        for k in range(1, XS):
            go(xg_copy(k))

    def yg_copy(k):
        return remote(yg_out, yg_in.at[y], yg_send.at[k], yg_recv.at[k], y_peers[k][1])

    def rel_yg():
        for k in range(1, XS):
            s = lax.rem(x + XS - k, XS)
            remote(xg_out, xg_in.at[s], xg_send.at[k], xg_recv.at[k], same_core[k][1]).wait_recv()
        whole = jnp.concatenate([xg_in[i] for i in range(XS)], axis=0)[0:HALF]
        yg_out[...] = whole
        yg_in[y] = whole
        for k in (2, 1, 3):
            go(yg_copy(k))
        go(cg_copy(0))

    def cg_copy(k):
        s = lax.rem(y + YS - k, YS)
        return remote(yg_in.at[s], cg_in.at[s], cg_send.at[k], cg_recv.at[k], mate)

    def rel_cg():
        for k in (1, 3, 2):
            s = lax.rem(y + YS - k, YS)
            remote(yg_out, yg_in.at[s], yg_send.at[k], yg_recv.at[k], y_peers[k][1]).wait_recv()
            go(cg_copy(k))

    def rel_end():
        for k in range(YS):
            cg_copy(k).wait_recv()
        for i in range(YS):
            mine, other = yg_in[i], cg_in[i]
            first = jnp.where(c == 0, mine, other)
            second = jnp.where(c == 0, other, mine)
            whole = jnp.concatenate([first, second[HALF - HALF_START :]], axis=0)
            if i < YS - 1:
                rel_ref[:, i * 384 : (i + 1) * 384] = whole
            else:
                rel_ref[:, i * 384 : REL] = whole[:, : REL - i * 384]
                flag_ref[0, 0] = jnp.max(whole[0:16, 256:384].astype(F32))

    def tile(t, k):
        return remote(
            stage.at[t, k], landed.at[t, me], tile_send.at[t, k], tile_recv.at[t, k], x_peers[k][1]
        )

    def scatter(t):
        for both in PAIRS:
            if t < TILES - 1:
                row = iota((BLOCK, ALL), 0) + t * BLOCK
                which = [hot(row + x_peers[k][0] * CAP == place_ref[...]) for k in both]
            else:
                which = [
                    last_hot[pl.ds(pl.multiple_of(x_peers[k][0] * BLOCK, BLOCK), BLOCK), :]
                    for k in both
                ]
            which = jnp.concatenate(which, axis=0)
            rows = mm(grads_ref[...], which, NT).astype(BF)
            for i, k in enumerate(both):
                part = rows[:, i * BLOCK : (i + 1) * BLOCK]
                if k == 0:
                    landed[t, me] = part
                else:
                    stage[t, k] = part
                    go(tile(t, k))

    def arrive(t):
        for k in range(1, XG):
            s = lax.rem(me + XG - k, XG)
            remote(
                stage.at[t, k], landed.at[t, s], tile_send.at[t, k], tile_recv.at[t, k],
                x_peers[k][1],
            ).wait_recv()

    def partial(dist, half):
        q = DIST.index(dist)
        least = [t for t in range(TILES) if (q, half) in PARTS[t]][0]
        parts = [(t, s) for t in range(least, TILES) for s in range(XG)]
        lhs = jnp.concatenate([landed[t, s] for t, s in parts], axis=1)
        key = (iota((BLOCK, 256), 1) // BLOCK + 2 * half) * 1024 + iota((BLOCK, 256), 0)
        which = jnp.concatenate(
            [hot(twice(codes_in[s, q : q + 1]) == key + t * BLOCK) for t, s in parts], axis=0
        )
        return mm(lhs, which)

    def ring(way, step, half):
        return remote(
            ring_out.at[way, step, half], ring_in.at[way, step, half],
            ring_send.at[way, step, half], ring_recv.at[way, step, half],
            right if way == 0 else left,
        )

    def has(way, step, half):
        return 0 < step or half == 1 - way

    def push(step, way, half):
        value = partial(4 - step if way == 0 else (4 + step) % ZS, half)
        if step > 0 and has(way, step - 1, half):
            ring(way, step - 1, half).wait_recv()
            value = value + ring_in[way, step - 1, half].astype(F32)
        ring_out[way, step, half] = value.astype(BF)
        go(ring(way, step, half))

    def begin():
        for way in range(2):
            go(gring(way, 0, 0))
        load(1).wait()
        tables[0, 1] = ent_in[:, 256:512].astype(BF)
        for way in range(2):
            go(gring(way, 0, 1))

    def plan():
        ids_ref[:, 0:EDGES] = head_ref[...]
        ids_ref[:, EDGES : 2 * EDGES] = tail_ref[...]
        ids_ref[:, 2 * EDGES :] = jnp.full((1, 2 * BLOCK), -1, I32)
        ids_ref[:, 2 * EDGES : 2 * EDGES + NEG] = ntail_ref[...]
        ids_ref[:, 2 * EDGES + BLOCK : 2 * EDGES + BLOCK + NEG] = nhead_ref[...]
        codes, places, overflow = plan_rows(ids_ref[...], owner_ref[...], block_ref[...], z)
        codes_mine[...] = codes.reshape(XG, 8, BLOCK)
        place_ref[...] = places
        over_ref[...] = jnp.zeros((8, BLOCK), F32) + overflow
        for k in range(1, XG):
            go(ask(k))
        codes_in[me] = codes_mine[me]

    def asked():
        for k in range(1, XG):
            s = lax.rem(me + XG - k, XG)
            remote(
                codes_mine.at[s], codes_in.at[s], ask_send.at[k], ask_recv.at[k], x_peers[k][1]
            ).wait_recv()

    def own():
        for half in range(2):
            ent_ref_a[:, half * 256 : (half + 1) * 256] = partial(0, half)

    def finish():
        for half in range(2):
            lanes = slice(half * 256, (half + 1) * 256)
            ring(0, 3, half).wait_recv()
            ent_ref_a[:, lanes] += ring_in[0, 3, half].astype(F32)
            ring(1, 3, half).wait_recv()
            ent_ref_b[:, lanes] = ring_in[1, 3, half]

    order = [
        (begin,), (plan,), (forward, 0, (0,)), (relation_rows,), (forward, 0, (1,)), (asked,),
        (select, 0, 0, True), (forward, 1, (0,)), (select, 1, 0, False),
        (forward, 1, (1,)), (select, 2, 0, False), (forward, 2, (0,)), (select, 1, 1, True),
        (select, 2, 1, False), (forward, 2, (1,)), (gather, 0), (forward, 3),
        (select, 2, 2, True), (prepare,), (gather, 1), (gather_last, (4, 3, 5, 2), False),
        (gather_last, (6, 1, 7, 0), True), (edges,),
        (scatter, 2), (relation_scatter,), (rel_core,), (scatter, 1), (rel_y,), (scatter, 0),
        (arrive, 2), (push, 0, 0, 1), (push, 0, 1, 0), (push, 1, 1, 1), (rel_x,), (push, 1, 0, 1),
        (arrive, 1), (push, 1, 0, 0), (push, 1, 1, 0), (rel_z,), (push, 2, 1, 1), (push, 2, 0, 1),
        (rel_zg,), (push, 2, 0, 0), (push, 2, 1, 0), (arrive, 0), (push, 3, 1, 1), (rel_xg,),
        (push, 3, 0, 1), (rel_yg,), (push, 3, 0, 0), (push, 3, 1, 0), (own,), (rel_cg,),
        (finish,), (rel_end,),
    ]
    for function, *values in order:
        function(*values)
    for copy in pending:
        copy.wait_send()


def vmem():
    return pl.BlockSpec(memory_space=pltpu.VMEM)


def fast_step(ent, rel, owners, blocks, heads, rel_ids, tails, ntail, nhead):
    dma = pltpu.SemaphoreType.DMA
    v = pltpu.VMEM
    return pl.pallas_call(
        step_kernel,
        out_shape=(
            jax.ShapeDtypeStruct((WIDTH, 512), F32),
            jax.ShapeDtypeStruct((WIDTH, 512), BF),
            jax.ShapeDtypeStruct((WIDTH, REL), BF),
            jax.ShapeDtypeStruct((1, 1), F32),
        ),
        in_specs=[pl.BlockSpec(memory_space=pl.ANY)] * 2 + [vmem()] * 7,
        out_specs=[vmem()] * 3 + [pl.BlockSpec(memory_space=pltpu.SMEM)],
        scratch_shapes=[
            v((ZS, 2, WIDTH, 256), BF),
            v((XG, 8, BLOCK), I32), v((XG, 8, BLOCK), I32),
            v((TILES, XG, WIDTH, BLOCK), BF), v((TILES, XG, WIDTH, BLOCK), BF),
            v((WIDTH, ALL), F32), v((1, ALL), I32), v((1, ALL), I32), v((WIDTH, ALL), BF),
            v((REL_PAD, EDGES), BF), v((WIDTH, REL_PAD), BF), v((WIDTH, REL_PAD), BF),
            v((WIDTH, EDGES), F32), v((WIDTH, EDGES), BF), v((2, WIDTH, BLOCK), F32),
            v((WIDTH, ALL), BF),
            v((TILES, XG, WIDTH, BLOCK), BF), v((TILES, XG, WIDTH, BLOCK), BF),
            v((2, 4, 2, WIDTH, 256), BF), v((2, 4, 2, WIDTH, 256), BF),
            v((HALF, REL_PAD), BF), v((HALF, REL_PAD), BF),
            v((YS, HALF, 384), BF), v((YS, HALF, 384), BF),
            v((XS, 64, 384), BF), v((XS, 64, 384), BF),
            v((ZS, 8, 384), F32), v((8, 384), F32), v((ZS, 8, 384), F32),
            v((64, 384), BF), v((XS, 64, 384), BF),
            v((HALF, 384), BF), v((YS, HALF, 384), BF), v((YS, HALF, 384), BF),
            v((HALF, REL_PAD), F32), v((256, 384), F32), v((64, 384), F32), v((8, BLOCK), F32),
            v((WIDTH, 512), F32), v((WIDTH, REL), F32), v((XG * BLOCK, ALL), BF),
            dma((2, 4, 2)), dma((2, 4, 2)), dma((XG,)), dma((XG,)),
            dma((TILES, XG)), dma((TILES, XG)),
            dma((TILES, XG)), dma((TILES, XG)), dma((2, 4, 2)), dma((2, 4, 2)),
            dma, dma, dma((YS,)), dma((YS,)), dma((ZS,)), dma((ZS,)), dma((XS,)), dma((XS,)),
            dma((ZS,)), dma((ZS,)), dma((XS,)), dma((XS,)), dma((YS,)), dma((YS,)), dma((YS,)), dma((YS,)), dma((3,)),
        ],
        compiler_params=pltpu.CompilerParams(
            collective_id=0, has_side_effects=True, vmem_limit_bytes=60 * MIB
        ),
        name="step",
    )(ent, rel, owners, blocks, heads, rel_ids, tails, ntail, nhead)


def widen_kernel(ent_a_ref, ent_b_ref, rel_in_ref, ent_ref, rel_ref):
    ent_ref[...] = ent_a_ref[...] + ent_b_ref[...].astype(F32)
    rel_ref[...] = rel_in_ref[...].astype(F32)


def widen(ent_a, ent_b, rel):
    return pl.pallas_call(
        widen_kernel,
        out_shape=(
            jax.ShapeDtypeStruct((WIDTH, 512), F32), jax.ShapeDtypeStruct((WIDTH, REL), F32)
        ),
        in_specs=[vmem()] * 3,
        out_specs=[vmem()] * 2,
        compiler_params=pltpu.CompilerParams(vmem_limit_bytes=16 * MIB),
        name="widen",
    )(ent_a, ent_b, rel)


def sum_everywhere(part):
    rows = part.shape[0]
    for axis in ("row", "bucket"):
        count = lax.axis_size(axis)
        each = -(-rows // count)
        padded = jnp.pad(part, ((0, each * count - rows), (0, 0)))
        pieces = lax.all_to_all(padded, axis, split_axis=0, concat_axis=0, tiled=True)
        piece = jnp.sum(pieces.reshape(count, each, -1), axis=0)
        copies = jnp.tile(piece, (count, 1))
        part = lax.all_to_all(copies, axis, split_axis=0, concat_axis=0, tiled=True)[:rows]
    return part


def side_weights(positive, scores):
    largest = jnp.maximum(positive, jnp.max(scores, axis=1))
    own_term = jnp.exp(positive - largest)
    others = jnp.exp(scores - largest[:, None])
    total = own_term + jnp.sum(others, axis=1)
    return (own_term / total - 1.0, others / total[:, None])


def edge_block_grads(buffer, relations, head_ids, rel_ids, tail_ids, neg_tail, neg_head):
    middle = relations.shape[1] // 2
    head_rows = jnp.take(buffer, head_ids, axis=0).astype(jnp.float32)
    tail_rows = jnp.take(buffer, tail_ids, axis=0).astype(jnp.float32)
    rel_rows = jnp.take(relations, rel_ids, axis=0)
    rel_real, rel_imag = (rel_rows[:, :middle], rel_rows[:, middle:])
    head_real, head_imag = (head_rows[:, :middle], head_rows[:, middle:])
    tail_real, tail_imag = (tail_rows[:, :middle], tail_rows[:, middle:])
    query = jnp.concatenate(
        [head_real * rel_real - head_imag * rel_imag, head_real * rel_imag + head_imag * rel_real],
        axis=1,
    )
    probe = jnp.concatenate(
        [rel_real * tail_real + rel_imag * tail_imag, rel_real * tail_imag - rel_imag * tail_real],
        axis=1,
    )
    positive = jnp.sum(query * tail_rows, axis=1)
    tail_negs = jnp.take(buffer, neg_tail, axis=0)
    head_negs = jnp.take(buffer, neg_head, axis=0)
    query_low = query.astype(jnp.bfloat16)
    probe_low = probe.astype(jnp.bfloat16)
    contract_last = (((1,), (1,)), ((), ()))
    contract_first = (((0,), (0,)), ((), ()))
    tail_scores = lax.dot_general(
        query_low, tail_negs, contract_last, preferred_element_type=jnp.float32
    )
    head_scores = lax.dot_general(
        probe_low, head_negs, contract_last, preferred_element_type=jnp.float32
    )
    tail_coef, tail_weights = side_weights(positive, tail_scores)
    head_coef, head_weights = side_weights(positive, head_scores)
    tail_low = tail_weights.astype(jnp.bfloat16)
    head_low = head_weights.astype(jnp.bfloat16)
    both_coef = (tail_coef + head_coef)[:, None]
    query_grad = both_coef * tail_rows + jnp.dot(
        tail_low, tail_negs, preferred_element_type=jnp.float32
    )
    probe_grad = jnp.dot(head_low, head_negs, preferred_element_type=jnp.float32)
    tail_neg_grad = lax.dot_general(
        tail_low, query_low, contract_first, preferred_element_type=jnp.float32
    )
    head_neg_grad = lax.dot_general(
        head_low, probe_low, contract_first, preferred_element_type=jnp.float32
    )
    qgrad_real, qgrad_imag = (query_grad[:, :middle], query_grad[:, middle:])
    pgrad_real, pgrad_imag = (probe_grad[:, :middle], probe_grad[:, middle:])
    head_grad = jnp.concatenate(
        [
            qgrad_real * rel_real + qgrad_imag * rel_imag,
            qgrad_imag * rel_real - qgrad_real * rel_imag,
        ],
        axis=1,
    )
    tail_grad = both_coef * query + jnp.concatenate(
        [
            pgrad_real * rel_real - pgrad_imag * rel_imag,
            pgrad_real * rel_imag + pgrad_imag * rel_real,
        ],
        axis=1,
    )
    rel_edge_grad = jnp.concatenate(
        [
            qgrad_real * head_real
            + qgrad_imag * head_imag
            + pgrad_real * tail_real
            + pgrad_imag * tail_imag,
            qgrad_imag * head_real
            - qgrad_real * head_imag
            + pgrad_real * tail_imag
            - pgrad_imag * tail_real,
        ],
        axis=1,
    )
    row_ids = jnp.concatenate([head_ids, tail_ids, neg_tail, neg_head])
    row_vals = jnp.concatenate([head_grad, tail_grad, tail_neg_grad, head_neg_grad], axis=0)
    return (row_ids, row_vals, rel_edge_grad)


def device_grads(buffer, relations, head_ids, rel_ids, tail_ids, neg_tail, neg_head):
    blocks_count = neg_tail.shape[0]
    start_zero = (jnp.zeros(buffer.shape, jnp.float32), jnp.zeros(relations.shape, jnp.float32))

    def advance(totals, position):
        row_ids, row_vals, rel_edge_grad = edge_block_grads(
            buffer, relations, head_ids, rel_ids, tail_ids, neg_tail[position], neg_head[position]
        )
        return (
            (totals[0].at[row_ids].add(row_vals), totals[1].at[rel_ids].add(rel_edge_grad)),
            None,
        )

    totals, unused = lax.scan(advance, start_zero, jnp.arange(blocks_count, dtype=jnp.int32))
    return totals


def dense_step(
    entities, relations, touch_owner, touch_block, head_ids, rel_ids, tail_ids, neg_tail, neg_head
):
    bucket_count = lax.axis_size("bucket")
    block_rows = BLOCK
    width = entities.shape[1]
    owned = entities.shape[0] // block_rows
    owners = touch_owner[0]
    wanted = touch_block[0]
    touched = owners.shape[0]
    slot_ids = jnp.arange(bucket_count, dtype=jnp.int32)
    matches = owners[:, None] == slot_ids[None, :]
    request = jnp.sum(jnp.where(matches, wanted[:, None] + 1, 0), axis=0) - 1
    incoming = lax.all_to_all(request, "bucket", split_axis=0, concat_axis=0, tiled=True)
    selector = (incoming[:, None] == jnp.arange(owned, dtype=jnp.int32)[None, :]).astype(
        jnp.float32
    )
    owned_flat = entities.reshape(owned, block_rows * width)
    reply = jnp.dot(selector, owned_flat, precision=lax.Precision.HIGHEST).astype(jnp.bfloat16)
    reply = reply.reshape(bucket_count, block_rows, width)
    fetched = lax.all_to_all(reply, "bucket", split_axis=0, concat_axis=0, tiled=True)
    buffer = jnp.take(fetched, owners, axis=0).reshape(touched * block_rows, width)
    buffer_grad, rel_part = device_grads(
        buffer, relations, head_ids, rel_ids, tail_ids, neg_tail, neg_head
    )
    outgoing = jnp.zeros((bucket_count, block_rows, width), jnp.float32)
    outgoing = outgoing.at[owners].set(buffer_grad.reshape(touched, block_rows, width))
    returned = lax.all_to_all(outgoing, "bucket", split_axis=0, concat_axis=0, tiled=True)
    entity_grad = lax.dot_general(
        selector,
        returned.reshape(bucket_count, block_rows * width),
        (((0,), (0,)), ((), ())),
        precision=lax.Precision.HIGHEST,
    )
    entity_grad = entity_grad.reshape(owned * block_rows, width)
    relation_grad = sum_everywhere(rel_part)
    return (entity_grad, relation_grad)


def per_device(
    entities, relations, touch_owner, touch_block, head_ids, rel_ids, tail_ids, neg_tail, neg_head
):
    ent_a, ent_b, rel, over = fast_step(
        entities.T, relations.T, touch_owner, touch_block,
        head_ids[None, :], rel_ids[None, :], tail_ids[None, :], neg_tail, neg_head,
    )
    ent, rel = lax.cond(
        over[0, 0] > 0.5,
        lambda: tuple(
            part.T
            for part in dense_step(
                entities, relations, touch_owner, touch_block, head_ids, rel_ids, tail_ids,
                neg_tail, neg_head,
            )
        ),
        lambda: widen(ent_a, ent_b, rel),
    )
    return (ent.T, rel.T)


def solution(mesh):
    return jax.shard_map(
        per_device,
        mesh=mesh,
        in_specs=(
            P(("bucket", "row"), None),
            P(),
            P(("bucket", "row"), None),
            P(("bucket", "row"), None),
            P(("bucket", "row")),
            P(("bucket", "row")),
            P(("bucket", "row")),
            P(("bucket", "row"), None),
            P(("bucket", "row"), None),
        ),
        out_specs=(P(("bucket", "row"), None), P()),
        check_vma=False,
    )
```

```python
import functools

import jax
import jax.numpy as jnp
from jax import lax
from jax.experimental import pallas as pl
from jax.experimental.pallas import tpu as pltpu
from jax.sharding import PartitionSpec as P

BLOCK = 128
WIDTH = 400
EDGES = 1024
NEG = 100
REL = 1300
REL_PAD = 1536
ALL = 2 * EDGES + 2 * BLOCK
XS, ZS, CS, YS = 4, 8, 2, 4
XG = XS * CS
TILES = 3
CAP = TILES * BLOCK
DIST = (0, 1, 7, 2, 6, 3, 5, 4)
PARTS = (
    ((0, 0), (0, 1), (1, 0), (1, 1), (2, 0), (2, 1)),
    ((3, 0), (3, 1), (4, 0), (4, 1), (5, 0), (6, 0)),
    ((5, 1), (6, 1), (7, 0), (7, 1)),
)
PAIRS = ((4, 3), (5, 2), (6, 1), (7, 0))
HALF = 208
HALF_START = 192
BF = jnp.bfloat16
F32 = jnp.float32
I32 = jnp.int32
NT = (((1,), (1,)), ((), ()))
TN = (((0,), (0,)), ((), ()))
MIB = 1024 * 1024


def mm(a, b, dims=(((1,), (0,)), ((), ()))):
    return lax.dot_general(a, b, dims, preferred_element_type=F32)


def iota(shape, dim):
    return lax.broadcasted_iota(I32, shape, dim)


def hot(mask):
    return jnp.where(mask, 1.0, 0.0).astype(BF)


def place():
    b = lax.axis_index("bucket")
    return b // (ZS * CS), (b // CS) % ZS, b % CS, lax.axis_index("row")


def bucket_of(x, z, c):
    return (x * ZS + z) * CS + c


def x_peer(x, z, c, k):
    s = lax.rem(x * CS + c + k, XG)
    return s, {"bucket": bucket_of(s // CS, z, s % CS)}


def z_peer(x, z, c, k):
    other = lax.rem(z + k, ZS)
    return other, {"bucket": bucket_of(x, other, c)}


def greet(peers):
    for peer in peers:
        pl.semaphore_signal(
            pltpu.get_barrier_semaphore(), inc=1, device_id=peer,
            device_id_type=pl.DeviceIdType.MESH,
        )


def remote(src, dst, send, recv, peer):
    return pltpu.make_async_remote_copy(
        src_ref=src, dst_ref=dst, send_sem=send, recv_sem=recv,
        device_id=peer, device_id_type=pl.DeviceIdType.MESH,
    )


def plan_rows(ids, owners, blocks, z):
    slot = lax.shift_right_arithmetic(ids, 7)
    row = jnp.bitwise_and(ids, 127)
    slot_hot = hot(iota((64, ALL), 0) == slot)
    row_is = iota((BLOCK, ALL), 0) == row
    row_hot = hot(row_is)
    count = mm(slot_hot, row_hot, NT)
    wanted_slot = hot(count > 0.5)
    j = iota((64, 64), 0)
    s, q = j // 8, j % 8
    dist = jnp.where(q % 2 == 1, (q + 1) // 2, (8 - q // 2) % 8)
    target = bucket_of(s // CS, (z + dist) % ZS, s % CS)
    perm_is = owners == target
    perm = hot(perm_is)
    wanted = mm(perm, wanted_slot)
    block = jnp.sum(jnp.where(perm_is, blocks, 0), axis=1, keepdims=True)
    wanted_low = wanted.astype(BF)
    before = mm(wanted_low, hot(iota((BLOCK, BLOCK), 0) < iota((BLOCK, BLOCK), 1)))
    number = mm(wanted_low, jnp.ones((BLOCK, BLOCK), BF))
    jj = iota((64, 64), 1)
    same = hot(s == jj // 8)
    ahead = hot((s == jj // 8) & (jj % 8 < q))
    q_wide = iota((64, BLOCK), 0) % 8
    late = (q_wide == 7) | ((q_wide >= 5) & (jnp.zeros((64, BLOCK), I32) + block >= 2))
    tile_of = jnp.where(q_wide < 3, 0, jnp.where(late, 2, 1))
    lead = jnp.zeros((64, BLOCK), F32)
    sums = []
    for t in range(TILES):
        part = jnp.where(tile_of == t, number, 0.0).astype(BF)
        lead = jnp.where(tile_of == t, mm(ahead, part), lead)
        sums.append(mm(same, part))
    start1 = jnp.maximum(float(BLOCK), sums[0])
    start2 = jnp.maximum(float(2 * BLOCK), start1 + sums[1])
    end = start2 + sums[2]
    start = jnp.where(tile_of == 0, 0.0, jnp.where(tile_of == 1, start1, start2))
    rank = (start + lead + before).astype(I32)
    codes = jnp.where(wanted > 0.5, block * 1024 + rank, -1)
    overflow = jnp.max(jnp.where(end > float(CAP), 1.0, 0.0))
    position = (iota((64, BLOCK), 0) // 8) * CAP + rank
    high = lax.shift_right_arithmetic(position, 7).astype(F32).astype(BF)
    low = jnp.bitwise_and(position, 127).astype(F32).astype(BF)
    high_slot = mm(perm, high, TN).astype(BF)
    low_slot = mm(perm, low, TN).astype(BF)
    high_ids = mm(high_slot, slot_hot, TN)
    low_ids = mm(low_slot, slot_hot, TN)
    value = jnp.sum(jnp.where(row_is, high_ids * 128.0 + low_ids, 0.0), axis=0, keepdims=True)
    places = jnp.where(slot >= 0, value.astype(I32), -1)
    return codes, places, overflow


def twice(row):
    return jnp.concatenate([row, row], axis=1)


def side(positive, scores, valid):
    largest = jnp.maximum(
        positive, jnp.max(jnp.where(valid, scores, -3e38), axis=0, keepdims=True)
    )
    own = jnp.exp(positive - largest)
    others = jnp.where(valid, jnp.exp(scores - largest), 0.0)
    total = own + jnp.sum(others, axis=0, keepdims=True)
    return own / total - 1.0, others / total


def step_kernel(
    ent_ref, rel_in_ref, owner_ref, block_ref, head_ref, rel_ids_ref, tail_ref, ntail_ref, nhead_ref,
    ent_ref_a, ent_ref_b, rel_ref, flag_ref,
    tables, codes_mine, codes_in, fstage, flanded, total, ids_ref, place_ref, rows_ref,
    hot_rel, high, low, relation, edge_rel, neg_sum, grads_ref,
    stage, landed, ring_out, ring_in,
    core_out, core_in, y_out, y_in, x_out, x_in, z_in, zg_out, zg_in, xg_out, xg_in, yg_out, yg_in, cg_in,
    sum_core, sum_y, sum_x, over_ref, ent_in, rel_in, last_hot,
    gring_send, gring_recv, ask_send, ask_recv, ftile_send, ftile_recv,
    tile_send, tile_recv, ring_send, ring_recv,
    core_send, core_recv, y_send, y_recv, z_send, z_recv, x_send, x_recv,
    zg_send, zg_recv, xg_send, xg_recv, yg_send, yg_recv, cg_send, cg_recv, in_sem,
):
    x, z, c, y = place()
    me = x * CS + c
    z_peers = [z_peer(x, z, c, k) for k in range(ZS)]
    x_peers = [x_peer(x, z, c, k) for k in range(XG)]
    y_peers = [(lax.rem(y + k, YS), {"row": lax.rem(y + k, YS)}) for k in range(YS)]
    same_core = [
        (lax.rem(x + k, XS), {"bucket": bucket_of(lax.rem(x + k, XS), z, c)}) for k in range(XS)
    ]
    mate = {"bucket": bucket_of(x, z, 1 - c)}
    right, left = z_peers[1][1], z_peers[ZS - 1][1]
    mid = WIDTH // 2
    pending = []

    def go(copy):
        copy.start()
        pending.append(copy)

    everyone = [p for _, p in z_peers[1:]] + [p for _, p in x_peers[1:]] + [p for _, p in y_peers[1:]]
    greet(everyone)

    def load(half):
        lanes = pl.ds(half * 256, 256)
        return pltpu.make_async_copy(ent_ref.at[:, lanes], ent_in.at[:, lanes], in_sem.at[half])

    rel_load = pltpu.make_async_copy(rel_in_ref, rel_in, in_sem.at[2])
    load(0).start()
    load(1).start()
    rel_load.start()
    load(0).wait()
    tables[0, 0] = ent_in[:, 0:256].astype(BF)
    pl.semaphore_wait(pltpu.get_barrier_semaphore(), len(everyone))

    def gring(way, step, half):
        if way == 0:
            src, dst = (-step) % ZS, (-step - 1) % ZS
        else:
            src, dst = step, step + 1
        return remote(
            tables.at[src, half], tables.at[dst, half],
            gring_send.at[way, step, half], gring_recv.at[way, step, half],
            right if way == 0 else left,
        )

    def legs(step):
        if step < 3:
            return [(0, 0), (1, 0), (0, 1), (1, 1)]
        return [(0, 1), (1, 0)]

    def forward(step, halves=(0, 1)):
        for way, half in legs(step):
            if half not in halves:
                continue
            gring(way, step, half).wait_recv()
            if step < 3 and (way, half) in legs(step + 1):
                go(gring(way, step + 1, half))

    def ask(k):
        s, peer = x_peers[k]
        return remote(codes_mine.at[s], codes_in.at[me], ask_send.at[k], ask_recv.at[k], peer)

    def ftile(t, k):
        return remote(
            fstage.at[t, k], flanded.at[t, me], ftile_send.at[t, k], ftile_recv.at[t, k],
            x_peers[k][1],
        )

    def select(t, group, send):
        parts = PARTS[group]
        lhs = jnp.concatenate([tables[DIST[q], half] for q, half in parts], axis=1)
        key = (iota((BLOCK, 256), 1) // BLOCK) * 1024 + iota((BLOCK, 256), 0) + t * BLOCK
        for both in PAIRS:
            chosen = []
            for k in both:
                code = codes_in[x_peers[k][0]]
                chosen.append(
                    jnp.concatenate(
                        [hot(twice(code[q : q + 1]) == key + 2048 * half) for q, half in parts],
                        axis=1,
                    )
                )
            rows = mm(lhs, jnp.concatenate(chosen, axis=0), NT).astype(BF)
            for i, k in enumerate(both):
                part = rows[:, i * BLOCK : (i + 1) * BLOCK]
                if group > 0:
                    part = part + fstage[t, k]
                if send and k == 0:
                    flanded[t, me] = part
                else:
                    fstage[t, k] = part
                    if send:
                        go(ftile(t, k))

    def gather(t):
        for k in range(1, XG):
            s = lax.rem(me + XG - k, XG)
            remote(
                fstage.at[t, k], flanded.at[t, s], ftile_send.at[t, k], ftile_recv.at[t, k],
                x_peers[k][1],
            ).wait_recv()
        key = iota((XG * BLOCK, 256), 0)
        key = (key // BLOCK) * CAP + key % BLOCK + t * BLOCK

        def chunk(i, carry):
            lanes = pl.ds(pl.multiple_of(i * 256, 256), 256)
            lhs = jnp.concatenate([flanded[t, s] for s in range(XG)], axis=1)
            if t < TILES - 1:
                rows = mm(lhs, hot(key == place_ref[:, lanes]))
            else:
                rows = mm(lhs, last_hot[:, lanes])
            if t == 0:
                total[:, lanes] = rows
            elif t < TILES - 1:
                total[:, lanes] += rows
            else:
                rows_ref[:, lanes] = (total[:, lanes] + rows).astype(BF)
            return carry

        lax.fori_loop(0, ALL // 256, chunk, 0)

    def prepare():
        key = iota((XG * BLOCK, 256), 0)
        key = (key // BLOCK) * CAP + key % BLOCK + (TILES - 1) * BLOCK

        def chunk(i, carry):
            lanes = pl.ds(pl.multiple_of(i * 256, 256), 256)
            last_hot[:, lanes] = hot(key == place_ref[:, lanes])
            return carry

        lax.fori_loop(0, ALL // 256, chunk, 0)

    def relation_rows():
        high[...] = jnp.zeros_like(high)
        low[...] = jnp.zeros_like(low)
        rel_load.wait()
        rel = rel_in[...]
        rel_high = rel.astype(BF)
        high[:, 0:REL] = rel_high
        low[:, 0:REL] = (rel - rel_high.astype(F32)).astype(BF)

        def chunk(i, carry):
            lanes = pl.ds(pl.multiple_of(i * 256, 256), 256)
            which = hot(iota((REL_PAD, 256), 0) == rel_ids_ref[:, lanes])
            hot_rel[:, lanes] = which
            relation[:, lanes] = mm(high[...], which) + mm(low[...], which)
            return carry

        lax.fori_loop(0, EDGES // 256, chunk, 0)

    def edges():
        neg_sum[...] = jnp.zeros_like(neg_sum)
        step = 256

        def chunk(i, carry):
            lanes = pl.ds(pl.multiple_of(i * step, step), step)
            tail_lanes = pl.ds(pl.multiple_of(EDGES + i * step, step), step)
            a, b = relation[0:mid, lanes], relation[mid:WIDTH, lanes]
            head = rows_ref[:, lanes].astype(F32)
            tail = rows_ref[:, tail_lanes].astype(F32)
            hr, hi = head[:mid], head[mid:]
            tr, ti = tail[:mid], tail[mid:]
            query = jnp.concatenate([hr * a - hi * b, hr * b + hi * a], axis=0)
            probe = jnp.concatenate([a * tr + b * ti, a * ti - b * tr], axis=0)
            positive = jnp.sum(query * tail, axis=0, keepdims=True)
            query_low, probe_low = query.astype(BF), probe.astype(BF)
            tail_neg = rows_ref[:, 2 * EDGES : 2 * EDGES + BLOCK]
            head_neg = rows_ref[:, 2 * EDGES + BLOCK : 2 * EDGES + 2 * BLOCK]
            valid = iota((BLOCK, step), 0) < NEG
            tail_coef, tail_weights = side(positive, mm(tail_neg, query_low, TN), valid)
            head_coef, head_weights = side(positive, mm(head_neg, probe_low, TN), valid)
            tail_low, head_low = tail_weights.astype(BF), head_weights.astype(BF)
            both = tail_coef + head_coef
            qg = both * tail + mm(tail_neg, tail_low)
            pg = mm(head_neg, head_low)
            neg_sum[0] += mm(query_low, tail_low, NT)
            neg_sum[1] += mm(probe_low, head_low, NT)
            qr, qi = qg[:mid], qg[mid:]
            pr, pi = pg[:mid], pg[mid:]
            grads_ref[:, lanes] = jnp.concatenate(
                [qr * a + qi * b, qi * a - qr * b], axis=0
            ).astype(BF)
            grads_ref[:, tail_lanes] = (
                both * query + jnp.concatenate([pr * a - pi * b, pr * b + pi * a], axis=0)
            ).astype(BF)
            edge_rel[:, lanes] = jnp.concatenate(
                [
                    qr * hr + qi * hi + pr * tr + pi * ti,
                    qi * hr - qr * hi + pr * ti - pi * tr,
                ],
                axis=0,
            ).astype(BF)
            return carry

        lax.fori_loop(0, EDGES // step, chunk, 0)
        grads_ref[:, 2 * EDGES : 2 * EDGES + BLOCK] = neg_sum[0].astype(BF)
        grads_ref[:, 2 * EDGES + BLOCK : 2 * EDGES + 2 * BLOCK] = neg_sum[1].astype(BF)

    def relation_scatter():
        def chunk(i, carry):
            lanes = pl.ds(pl.multiple_of(i * 256, 256), 256)
            total[:, lanes] = mm(edge_rel[...], hot_rel[lanes, :], NT)
            return carry

        lax.fori_loop(0, REL_PAD // 256, chunk, 0)
        total[:, REL_PAD - BLOCK : REL_PAD] = jnp.zeros((WIDTH, BLOCK), F32) + over_ref[0:1, :]

    def core_copy():
        return remote(core_out, core_in, core_send, core_recv, mate)

    def rel_core():
        core_out[...] = total[pl.ds(pl.multiple_of((1 - c) * HALF_START, 16), HALF), 0:REL_PAD].astype(BF)
        go(core_copy())

    def y_copy(k):
        return remote(y_out.at[k], y_in.at[k], y_send.at[k], y_recv.at[k], y_peers[k][1])

    def rel_y():
        core_copy().wait_recv()
        mine = pl.ds(pl.multiple_of(c * HALF_START, 16), HALF)
        sum_core[...] = total[mine, 0:REL_PAD] + core_in[...].astype(F32)
        for k in range(1, YS):
            other = y_peers[k][0]
            y_out[k] = sum_core[:, pl.ds(pl.multiple_of(other * 384, 128), 384)].astype(BF)
            go(y_copy(k))

    def x_copy(k):
        return remote(x_out.at[k], x_in.at[k], x_send.at[k], x_recv.at[k], same_core[k][1])

    def rel_x():
        for k in range(1, YS):
            y_copy(k).wait_recv()
        summed = sum_core[:, pl.ds(pl.multiple_of(y * 384, 128), 384)]
        for k in range(1, YS):
            summed = summed + y_in[k].astype(F32)
        sum_y[HALF:, :] = jnp.zeros((256 - HALF, 384), F32)
        sum_y[0:HALF, :] = summed
        for k in range(1, XS):
            other = same_core[k][0]
            x_out[k] = sum_y[pl.ds(pl.multiple_of(other * 64, 64), 64), :].astype(BF)
            go(x_copy(k))

    def z_copy(k):
        return remote(
            sum_x.at[pl.ds(pl.multiple_of(z_peers[k][0] * 8, 8), 8)], z_in.at[k],
            z_send.at[k], z_recv.at[k], z_peers[k][1],
        )

    def rel_z():
        for k in range(1, XS):
            x_copy(k).wait_recv()
        summed = sum_y[pl.ds(pl.multiple_of(x * 64, 64), 64), :]
        for k in range(1, XS):
            summed = summed + x_in[k].astype(F32)
        sum_x[...] = summed
        for k in range(1, ZS):
            go(z_copy(k))

    def zg_copy(k):
        return remote(zg_out, zg_in.at[z], zg_send.at[k], zg_recv.at[k], z_peers[k][1])

    def rel_zg():
        for k in range(1, ZS):
            z_copy(k).wait_recv()
        summed = sum_x[pl.ds(pl.multiple_of(z * 8, 8), 8), :]
        for k in range(1, ZS):
            summed = summed + z_in[k]
        zg_out[...] = summed
        zg_in[z] = summed
        for k in range(1, ZS):
            go(zg_copy(k))

    def xg_copy(k):
        return remote(xg_out, xg_in.at[x], xg_send.at[k], xg_recv.at[k], same_core[k][1])

    def rel_xg():
        for k in range(1, ZS):
            s = lax.rem(z + ZS - k, ZS)
            remote(zg_out, zg_in.at[s], zg_send.at[k], zg_recv.at[k], z_peers[k][1]).wait_recv()
        whole = jnp.concatenate([zg_in[i] for i in range(ZS)], axis=0).astype(BF)
        xg_out[...] = whole
        xg_in[x] = whole
        for k in range(1, XS):
            go(xg_copy(k))

    def yg_copy(k):
        return remote(yg_out, yg_in.at[y], yg_send.at[k], yg_recv.at[k], y_peers[k][1])

    def rel_yg():
        for k in range(1, XS):
            s = lax.rem(x + XS - k, XS)
            remote(xg_out, xg_in.at[s], xg_send.at[k], xg_recv.at[k], same_core[k][1]).wait_recv()
        whole = jnp.concatenate([xg_in[i] for i in range(XS)], axis=0)[0:HALF]
        yg_out[...] = whole
        yg_in[y] = whole
        for k in (2, 1, 3):
            go(yg_copy(k))
        go(cg_copy(0))

    def cg_copy(k):
        s = lax.rem(y + YS - k, YS)
        return remote(yg_in.at[s], cg_in.at[s], cg_send.at[k], cg_recv.at[k], mate)

    def rel_cg():
        for k in (1, 3, 2):
            s = lax.rem(y + YS - k, YS)
            remote(yg_out, yg_in.at[s], yg_send.at[k], yg_recv.at[k], y_peers[k][1]).wait_recv()
            go(cg_copy(k))

    def rel_end():
        for k in range(YS):
            cg_copy(k).wait_recv()
        for i in range(YS):
            mine, other = yg_in[i], cg_in[i]
            first = jnp.where(c == 0, mine, other)
            second = jnp.where(c == 0, other, mine)
            whole = jnp.concatenate([first, second[HALF - HALF_START :]], axis=0)
            if i < YS - 1:
                rel_ref[:, i * 384 : (i + 1) * 384] = whole
            else:
                rel_ref[:, i * 384 : REL] = whole[:, : REL - i * 384]
                flag_ref[0, 0] = jnp.max(whole[0:16, 256:384].astype(F32))

    def tile(t, k):
        return remote(
            stage.at[t, k], landed.at[t, me], tile_send.at[t, k], tile_recv.at[t, k], x_peers[k][1]
        )

    def scatter(t):
        for both in PAIRS:
            if t < TILES - 1:
                row = iota((BLOCK, ALL), 0) + t * BLOCK
                which = [hot(row + x_peers[k][0] * CAP == place_ref[...]) for k in both]
            else:
                which = [
                    last_hot[pl.ds(pl.multiple_of(x_peers[k][0] * BLOCK, BLOCK), BLOCK), :]
                    for k in both
                ]
            which = jnp.concatenate(which, axis=0)
            rows = mm(grads_ref[...], which, NT).astype(BF)
            for i, k in enumerate(both):
                part = rows[:, i * BLOCK : (i + 1) * BLOCK]
                if k == 0:
                    landed[t, me] = part
                else:
                    stage[t, k] = part
                    go(tile(t, k))

    def arrive(t):
        for k in range(1, XG):
            s = lax.rem(me + XG - k, XG)
            remote(
                stage.at[t, k], landed.at[t, s], tile_send.at[t, k], tile_recv.at[t, k],
                x_peers[k][1],
            ).wait_recv()

    def partial(dist, half):
        q = DIST.index(dist)
        least = [t for t in range(TILES) if (q, half) in PARTS[t]][0]
        parts = [(t, s) for t in range(least, TILES) for s in range(XG)]
        lhs = jnp.concatenate([landed[t, s] for t, s in parts], axis=1)
        key = (iota((BLOCK, 256), 1) // BLOCK + 2 * half) * 1024 + iota((BLOCK, 256), 0)
        which = jnp.concatenate(
            [hot(twice(codes_in[s, q : q + 1]) == key + t * BLOCK) for t, s in parts], axis=0
        )
        return mm(lhs, which)

    def ring(way, step, half):
        return remote(
            ring_out.at[way, step, half], ring_in.at[way, step, half],
            ring_send.at[way, step, half], ring_recv.at[way, step, half],
            right if way == 0 else left,
        )

    def has(way, step, half):
        return 0 < step or half == 1 - way

    def push(step, way, half):
        value = partial(4 - step if way == 0 else (4 + step) % ZS, half)
        if step > 0 and has(way, step - 1, half):
            ring(way, step - 1, half).wait_recv()
            value = value + ring_in[way, step - 1, half].astype(F32)
        ring_out[way, step, half] = value.astype(BF)
        go(ring(way, step, half))

    def begin():
        for way in range(2):
            go(gring(way, 0, 0))
        load(1).wait()
        tables[0, 1] = ent_in[:, 256:512].astype(BF)
        for way in range(2):
            go(gring(way, 0, 1))

    def plan():
        ids_ref[:, 0:EDGES] = head_ref[...]
        ids_ref[:, EDGES : 2 * EDGES] = tail_ref[...]
        ids_ref[:, 2 * EDGES :] = jnp.full((1, 2 * BLOCK), -1, I32)
        ids_ref[:, 2 * EDGES : 2 * EDGES + NEG] = ntail_ref[...]
        ids_ref[:, 2 * EDGES + BLOCK : 2 * EDGES + BLOCK + NEG] = nhead_ref[...]
        codes, places, overflow = plan_rows(ids_ref[...], owner_ref[...], block_ref[...], z)
        codes_mine[...] = codes.reshape(XG, 8, BLOCK)
        place_ref[...] = places
        over_ref[...] = jnp.zeros((8, BLOCK), F32) + overflow
        for k in range(1, XG):
            go(ask(k))
        codes_in[me] = codes_mine[me]

    def asked():
        for k in range(1, XG):
            s = lax.rem(me + XG - k, XG)
            remote(
                codes_mine.at[s], codes_in.at[s], ask_send.at[k], ask_recv.at[k], x_peers[k][1]
            ).wait_recv()

    def own():
        for half in range(2):
            ent_ref_a[:, half * 256 : (half + 1) * 256] = partial(0, half)

    def finish():
        for half in range(2):
            lanes = slice(half * 256, (half + 1) * 256)
            ring(0, 3, half).wait_recv()
            ent_ref_a[:, lanes] += ring_in[0, 3, half].astype(F32)
            ring(1, 3, half).wait_recv()
            ent_ref_b[:, lanes] = ring_in[1, 3, half]

    order = [
        (begin,), (plan,), (forward, 0, (0,)), (relation_rows,), (forward, 0, (1,)), (asked,),
        (select, 0, 0, True), (forward, 1, (0,)), (select, 1, 0, False),
        (forward, 1, (1,)), (select, 2, 0, False), (forward, 2, (0,)), (select, 1, 1, True),
        (select, 2, 1, False), (forward, 2, (1,)), (gather, 0), (forward, 3),
        (select, 2, 2, True), (prepare,), (gather, 1), (gather, 2), (edges,),
        (scatter, 2), (relation_scatter,), (rel_core,), (scatter, 1), (rel_y,), (scatter, 0),
        (arrive, 2), (push, 0, 0, 1), (push, 0, 1, 0), (push, 1, 1, 1), (rel_x,), (push, 1, 0, 1),
        (arrive, 1), (push, 1, 0, 0), (push, 1, 1, 0), (rel_z,), (push, 2, 1, 1), (push, 2, 0, 1),
        (rel_zg,), (push, 2, 0, 0), (push, 2, 1, 0), (arrive, 0), (push, 3, 1, 1), (rel_xg,),
        (push, 3, 0, 1), (rel_yg,), (push, 3, 0, 0), (push, 3, 1, 0), (own,), (rel_cg,),
        (finish,), (rel_end,),
    ]
    for function, *values in order:
        function(*values)
    for copy in pending:
        copy.wait_send()


def vmem():
    return pl.BlockSpec(memory_space=pltpu.VMEM)


def fast_step(ent, rel, owners, blocks, heads, rel_ids, tails, ntail, nhead):
    dma = pltpu.SemaphoreType.DMA
    v = pltpu.VMEM
    return pl.pallas_call(
        step_kernel,
        out_shape=(
            jax.ShapeDtypeStruct((WIDTH, 512), F32),
            jax.ShapeDtypeStruct((WIDTH, 512), BF),
            jax.ShapeDtypeStruct((WIDTH, REL), BF),
            jax.ShapeDtypeStruct((1, 1), F32),
        ),
        in_specs=[pl.BlockSpec(memory_space=pl.ANY)] * 2 + [vmem()] * 7,
        out_specs=[vmem()] * 3 + [pl.BlockSpec(memory_space=pltpu.SMEM)],
        scratch_shapes=[
            v((ZS, 2, WIDTH, 256), BF),
            v((XG, 8, BLOCK), I32), v((XG, 8, BLOCK), I32),
            v((TILES, XG, WIDTH, BLOCK), BF), v((TILES, XG, WIDTH, BLOCK), BF),
            v((WIDTH, ALL), F32), v((1, ALL), I32), v((1, ALL), I32), v((WIDTH, ALL), BF),
            v((REL_PAD, EDGES), BF), v((WIDTH, REL_PAD), BF), v((WIDTH, REL_PAD), BF),
            v((WIDTH, EDGES), F32), v((WIDTH, EDGES), BF), v((2, WIDTH, BLOCK), F32),
            v((WIDTH, ALL), BF),
            v((TILES, XG, WIDTH, BLOCK), BF), v((TILES, XG, WIDTH, BLOCK), BF),
            v((2, 4, 2, WIDTH, 256), BF), v((2, 4, 2, WIDTH, 256), BF),
            v((HALF, REL_PAD), BF), v((HALF, REL_PAD), BF),
            v((YS, HALF, 384), BF), v((YS, HALF, 384), BF),
            v((XS, 64, 384), BF), v((XS, 64, 384), BF),
            v((ZS, 8, 384), F32), v((8, 384), F32), v((ZS, 8, 384), F32),
            v((64, 384), BF), v((XS, 64, 384), BF),
            v((HALF, 384), BF), v((YS, HALF, 384), BF), v((YS, HALF, 384), BF),
            v((HALF, REL_PAD), F32), v((256, 384), F32), v((64, 384), F32), v((8, BLOCK), F32),
            v((WIDTH, 512), F32), v((WIDTH, REL), F32), v((XG * BLOCK, ALL), BF),
            dma((2, 4, 2)), dma((2, 4, 2)), dma((XG,)), dma((XG,)),
            dma((TILES, XG)), dma((TILES, XG)),
            dma((TILES, XG)), dma((TILES, XG)), dma((2, 4, 2)), dma((2, 4, 2)),
            dma, dma, dma((YS,)), dma((YS,)), dma((ZS,)), dma((ZS,)), dma((XS,)), dma((XS,)),
            dma((ZS,)), dma((ZS,)), dma((XS,)), dma((XS,)), dma((YS,)), dma((YS,)), dma((YS,)), dma((YS,)), dma((3,)),
        ],
        compiler_params=pltpu.CompilerParams(
            collective_id=0, has_side_effects=True, vmem_limit_bytes=60 * MIB
        ),
        name="step",
    )(ent, rel, owners, blocks, heads, rel_ids, tails, ntail, nhead)


def widen_kernel(ent_a_ref, ent_b_ref, rel_in_ref, ent_ref, rel_ref):
    ent_ref[...] = ent_a_ref[...] + ent_b_ref[...].astype(F32)
    rel_ref[...] = rel_in_ref[...].astype(F32)


def widen(ent_a, ent_b, rel):
    return pl.pallas_call(
        widen_kernel,
        out_shape=(
            jax.ShapeDtypeStruct((WIDTH, 512), F32), jax.ShapeDtypeStruct((WIDTH, REL), F32)
        ),
        grid=(5,),
        in_specs=[pl.BlockSpec((80, width), lambda i: (i, 0)) for width in (512, 512, REL)],
        out_specs=[pl.BlockSpec((80, width), lambda i: (i, 0)) for width in (512, REL)],
        compiler_params=pltpu.CompilerParams(vmem_limit_bytes=16 * MIB),
        name="widen",
    )(ent_a, ent_b, rel)


def sum_everywhere(part):
    rows = part.shape[0]
    for axis in ("row", "bucket"):
        count = lax.axis_size(axis)
        each = -(-rows // count)
        padded = jnp.pad(part, ((0, each * count - rows), (0, 0)))
        pieces = lax.all_to_all(padded, axis, split_axis=0, concat_axis=0, tiled=True)
        piece = jnp.sum(pieces.reshape(count, each, -1), axis=0)
        copies = jnp.tile(piece, (count, 1))
        part = lax.all_to_all(copies, axis, split_axis=0, concat_axis=0, tiled=True)[:rows]
    return part


def side_weights(positive, scores):
    largest = jnp.maximum(positive, jnp.max(scores, axis=1))
    own_term = jnp.exp(positive - largest)
    others = jnp.exp(scores - largest[:, None])
    total = own_term + jnp.sum(others, axis=1)
    return (own_term / total - 1.0, others / total[:, None])


def edge_block_grads(buffer, relations, head_ids, rel_ids, tail_ids, neg_tail, neg_head):
    middle = relations.shape[1] // 2
    head_rows = jnp.take(buffer, head_ids, axis=0).astype(jnp.float32)
    tail_rows = jnp.take(buffer, tail_ids, axis=0).astype(jnp.float32)
    rel_rows = jnp.take(relations, rel_ids, axis=0)
    rel_real, rel_imag = (rel_rows[:, :middle], rel_rows[:, middle:])
    head_real, head_imag = (head_rows[:, :middle], head_rows[:, middle:])
    tail_real, tail_imag = (tail_rows[:, :middle], tail_rows[:, middle:])
    query = jnp.concatenate(
        [head_real * rel_real - head_imag * rel_imag, head_real * rel_imag + head_imag * rel_real],
        axis=1,
    )
    probe = jnp.concatenate(
        [rel_real * tail_real + rel_imag * tail_imag, rel_real * tail_imag - rel_imag * tail_real],
        axis=1,
    )
    positive = jnp.sum(query * tail_rows, axis=1)
    tail_negs = jnp.take(buffer, neg_tail, axis=0)
    head_negs = jnp.take(buffer, neg_head, axis=0)
    query_low = query.astype(jnp.bfloat16)
    probe_low = probe.astype(jnp.bfloat16)
    contract_last = (((1,), (1,)), ((), ()))
    contract_first = (((0,), (0,)), ((), ()))
    tail_scores = lax.dot_general(
        query_low, tail_negs, contract_last, preferred_element_type=jnp.float32
    )
    head_scores = lax.dot_general(
        probe_low, head_negs, contract_last, preferred_element_type=jnp.float32
    )
    tail_coef, tail_weights = side_weights(positive, tail_scores)
    head_coef, head_weights = side_weights(positive, head_scores)
    tail_low = tail_weights.astype(jnp.bfloat16)
    head_low = head_weights.astype(jnp.bfloat16)
    both_coef = (tail_coef + head_coef)[:, None]
    query_grad = both_coef * tail_rows + jnp.dot(
        tail_low, tail_negs, preferred_element_type=jnp.float32
    )
    probe_grad = jnp.dot(head_low, head_negs, preferred_element_type=jnp.float32)
    tail_neg_grad = lax.dot_general(
        tail_low, query_low, contract_first, preferred_element_type=jnp.float32
    )
    head_neg_grad = lax.dot_general(
        head_low, probe_low, contract_first, preferred_element_type=jnp.float32
    )
    qgrad_real, qgrad_imag = (query_grad[:, :middle], query_grad[:, middle:])
    pgrad_real, pgrad_imag = (probe_grad[:, :middle], probe_grad[:, middle:])
    head_grad = jnp.concatenate(
        [
            qgrad_real * rel_real + qgrad_imag * rel_imag,
            qgrad_imag * rel_real - qgrad_real * rel_imag,
        ],
        axis=1,
    )
    tail_grad = both_coef * query + jnp.concatenate(
        [
            pgrad_real * rel_real - pgrad_imag * rel_imag,
            pgrad_real * rel_imag + pgrad_imag * rel_real,
        ],
        axis=1,
    )
    rel_edge_grad = jnp.concatenate(
        [
            qgrad_real * head_real
            + qgrad_imag * head_imag
            + pgrad_real * tail_real
            + pgrad_imag * tail_imag,
            qgrad_imag * head_real
            - qgrad_real * head_imag
            + pgrad_real * tail_imag
            - pgrad_imag * tail_real,
        ],
        axis=1,
    )
    row_ids = jnp.concatenate([head_ids, tail_ids, neg_tail, neg_head])
    row_vals = jnp.concatenate([head_grad, tail_grad, tail_neg_grad, head_neg_grad], axis=0)
    return (row_ids, row_vals, rel_edge_grad)


def device_grads(buffer, relations, head_ids, rel_ids, tail_ids, neg_tail, neg_head):
    blocks_count = neg_tail.shape[0]
    start_zero = (jnp.zeros(buffer.shape, jnp.float32), jnp.zeros(relations.shape, jnp.float32))

    def advance(totals, position):
        row_ids, row_vals, rel_edge_grad = edge_block_grads(
            buffer, relations, head_ids, rel_ids, tail_ids, neg_tail[position], neg_head[position]
        )
        return (
            (totals[0].at[row_ids].add(row_vals), totals[1].at[rel_ids].add(rel_edge_grad)),
            None,
        )

    totals, unused = lax.scan(advance, start_zero, jnp.arange(blocks_count, dtype=jnp.int32))
    return totals


def dense_step(
    entities, relations, touch_owner, touch_block, head_ids, rel_ids, tail_ids, neg_tail, neg_head
):
    bucket_count = lax.axis_size("bucket")
    block_rows = BLOCK
    width = entities.shape[1]
    owned = entities.shape[0] // block_rows
    owners = touch_owner[0]
    wanted = touch_block[0]
    touched = owners.shape[0]
    slot_ids = jnp.arange(bucket_count, dtype=jnp.int32)
    matches = owners[:, None] == slot_ids[None, :]
    request = jnp.sum(jnp.where(matches, wanted[:, None] + 1, 0), axis=0) - 1
    incoming = lax.all_to_all(request, "bucket", split_axis=0, concat_axis=0, tiled=True)
    selector = (incoming[:, None] == jnp.arange(owned, dtype=jnp.int32)[None, :]).astype(
        jnp.float32
    )
    owned_flat = entities.reshape(owned, block_rows * width)
    reply = jnp.dot(selector, owned_flat, precision=lax.Precision.HIGHEST).astype(jnp.bfloat16)
    reply = reply.reshape(bucket_count, block_rows, width)
    fetched = lax.all_to_all(reply, "bucket", split_axis=0, concat_axis=0, tiled=True)
    buffer = jnp.take(fetched, owners, axis=0).reshape(touched * block_rows, width)
    buffer_grad, rel_part = device_grads(
        buffer, relations, head_ids, rel_ids, tail_ids, neg_tail, neg_head
    )
    outgoing = jnp.zeros((bucket_count, block_rows, width), jnp.float32)
    outgoing = outgoing.at[owners].set(buffer_grad.reshape(touched, block_rows, width))
    returned = lax.all_to_all(outgoing, "bucket", split_axis=0, concat_axis=0, tiled=True)
    entity_grad = lax.dot_general(
        selector,
        returned.reshape(bucket_count, block_rows * width),
        (((0,), (0,)), ((), ())),
        precision=lax.Precision.HIGHEST,
    )
    entity_grad = entity_grad.reshape(owned * block_rows, width)
    relation_grad = sum_everywhere(rel_part)
    return (entity_grad, relation_grad)


def per_device(
    entities, relations, touch_owner, touch_block, head_ids, rel_ids, tail_ids, neg_tail, neg_head
):
    ent_a, ent_b, rel, over = fast_step(
        entities.T, relations.T, touch_owner, touch_block,
        head_ids[None, :], rel_ids[None, :], tail_ids[None, :], neg_tail, neg_head,
    )
    ent, rel = lax.cond(
        over[0, 0] > 0.5,
        lambda: tuple(
            part.T
            for part in dense_step(
                entities, relations, touch_owner, touch_block, head_ids, rel_ids, tail_ids,
                neg_tail, neg_head,
            )
        ),
        lambda: widen(ent_a, ent_b, rel),
    )
    return (ent.T, rel.T)


def solution(mesh):
    return jax.shard_map(
        per_device,
        mesh=mesh,
        in_specs=(
            P(("bucket", "row"), None),
            P(),
            P(("bucket", "row"), None),
            P(("bucket", "row"), None),
            P(("bucket", "row")),
            P(("bucket", "row")),
            P(("bucket", "row")),
            P(("bucket", "row"), None),
            P(("bucket", "row"), None),
        ),
        out_specs=(P(("bucket", "row"), None), P()),
        check_vma=False,
    )
```
